128 devices in a mesh: gx: 32 (over y, z_hi, x), gy: 4 (over z_lo, core).
Axes of the slice: x: 4, y: 4, z: 4 (z_hi: 2, z_lo: 2; z = z_hi * 2 + z_lo), core: 2. Of those that a mesh axis runs over, the one named last changes fastest.
Arguments:
- occupied: bfloat16 [256, 8, 32768], P(('gx', 'gy')), may hold values from -6 to 6
- virtual: bfloat16 [256, 8, 32768], P(('gx', 'gy')), may hold values from -6 to 6
- trials: bfloat16 [256, 4, 8, 8], P(('gx', 'gy')), may hold values from -1 to 1
- anchor_x: int32 [256], P(('gx', 'gy')), may hold values from 0 to 7
- anchor_y: int32 [256], P(('gx', 'gy')), may hold values from 0 to 127
- anchor_z: int32 [256], P(('gx', 'gy')), may hold values from 0 to 96
Outputs:
- potential: float32 [4, 256, 512, 128], P(None, 'gx', 'gy')
- coupling: float32 [256, 4, 8, 8], P(('gx', 'gy'))
The draws below stay inside these ranges and needn't reach their ends.
All inputs are finite; a program needn't handle non-finite values.
Results may differ from the reference program's by a relative error of at most 0.00051.
Values sent between devices are 32-bit elements; how exact they have to be, the bound alone decides.
A program may use at most 192 MiB of HBM per device.

```python
import jax
import jax.numpy as jnp
from jax import lax

BOX = 32
OCC = 8
VIR = 8
TRIALS = 4
LEVELS = 3
BOX_DEV = 2
CX = 8
CY = 128
NZ = 128
BOXES = 256
NX = 256
NY = 512
N_GY = 4


def place_ends(array, rng, low, high):
    extent = array.shape
    spot = [jax.random.randint(jax.random.fold_in(rng, axis), (), 0, extent[axis]) for axis in range(len(extent))]
    array = array.at[tuple(spot)].set(low)
    longest = extent.index(max(extent))
    spot[longest] = (spot[longest] + 1) % extent[longest]
    return array.at[tuple(spot)].set(high)


def level_of(own_key, dims, split, smallest, largest):
    level, own = 1.0, jax.random.fold_in(own_key, 6)
    for dim, parts in split:
        draws = jnp.exp(jax.random.uniform(jax.random.fold_in(own, dim), (parts,), jnp.float32, smallest / len(split), largest / len(split)))
        level = level * jnp.repeat(draws, dims[dim] // parts).reshape([-1 if axis == dim else 1 for axis in range(len(dims))])
    return level


def bell_draw(own_key, extent, scale, most, split=(), held_as=jnp.bfloat16):
    drawn = scale * jax.random.normal(own_key, extent, jnp.float32)
    if split:
        drawn = drawn * level_of(own_key, extent, split, -0.22, 0.18)
    return jnp.clip(drawn, -most, most).astype(held_as)


def setup_inputs(seed: int = 0) -> dict:
    splits = jax.random.split(jax.random.key(seed), 7)
    occupied = bell_draw(splits[0], (BOXES, OCC, BOX ** 3), 1.0, 6.0, ((0, 128),))
    virtual = bell_draw(splits[1], (BOXES, VIR, BOX ** 3), 1.0, 6.0, ((0, 128),))
    trials = bell_draw(splits[2], (BOXES, TRIALS, OCC, VIR), 0.125, 1.0, ((0, 128),))
    anchor_x = place_ends(jax.random.randint(splits[3], (BOXES,), 0, CX), jax.random.fold_in(splits[3], 1), 0, CX - 1).astype(jnp.int32)
    anchor_y = place_ends(jax.random.randint(splits[4], (BOXES,), 0, CY), jax.random.fold_in(splits[4], 1), 0, CY - 1).astype(jnp.int32)
    anchor_z = place_ends(jax.random.randint(splits[5], (BOXES,), 0, NZ - BOX + 1), jax.random.fold_in(splits[5], 1), 0, NZ - BOX).astype(jnp.int32)
    return dict(occupied=occupied, virtual=virtual, trials=trials, anchor_x=anchor_x, anchor_y=anchor_y, anchor_z=anchor_z)


SCREEN = 0.05
DAMPING = 2.0 / 3.0

def hartley(count):
    index = jnp.arange(count, dtype=jnp.int32)
    product = index[:, None] * index[None, :] % count
    angle = 2.0 * jnp.pi / count * product.astype(jnp.float32)
    return (jnp.cos(angle) + jnp.sin(angle)) / jnp.sqrt(jnp.float32(count))

def eigen_line(count, spacing):
    index = jnp.arange(count, dtype=jnp.int32).astype(jnp.float32)
    return (2.0 - 2.0 * jnp.cos(2.0 * jnp.pi / count * index)) / (spacing * spacing)

def transform_all(field, table_x, table_y, table_z):
    high = lax.Precision.HIGHEST
    field = jnp.einsum('txyz,xa->tayz', field, table_x, precision=high)
    field = jnp.einsum('tayz,yb->tabz', field, table_y, precision=high)
    return jnp.einsum('tabz,zc->tabc', field, table_z, precision=high)

def spectral_solve(source, spacing):
    size_x, size_y, size_z = (source.shape[1], source.shape[2], source.shape[3])
    table_x, table_y, table_z = (hartley(size_x), hartley(size_y), hartley(size_z))
    eigen_values = SCREEN * SCREEN + eigen_line(size_x, spacing)[:, None, None] + eigen_line(size_y, spacing)[None, :, None] + eigen_line(size_z, spacing)[None, None, :]
    spectrum = transform_all(source, table_x, table_y, table_z)
    return transform_all(spectrum / eigen_values, table_x, table_y, table_z)

def operate(field, spacing):
    beside = jnp.roll(field, -1, 1) + jnp.roll(field, 1, 1)
    beside = beside + jnp.roll(field, -1, 2) + jnp.roll(field, 1, 2)
    beside = beside + jnp.roll(field, -1, 3) + jnp.roll(field, 1, 3)
    return (6.0 / spacing ** 2 + SCREEN ** 2) * field - beside / spacing ** 2

def restrict(field):
    trial_count, size_x, size_y, size_z = field.shape
    blocks = field.reshape(trial_count, size_x // 2, 2, size_y // 2, 2, size_z // 2, 2)
    return blocks.mean(axis=(2, 4, 6))

def prolong(field):
    return jnp.repeat(jnp.repeat(jnp.repeat(field, 2, 1), 2, 2), 2, 3)

def vcycle(source, depth_level):
    spacing = 2.0 ** depth_level
    if depth_level == LEVELS:
        return spectral_solve(source, spacing)
    center = 6.0 / spacing ** 2 + SCREEN ** 2
    first = DAMPING * source / center
    residue = source - operate(first, spacing)
    second = first + prolong(vcycle(restrict(residue), depth_level + 1))
    return second + DAMPING * (source - operate(second, spacing)) / center

def box_anchor(box_index, anchor_x, anchor_y, anchor_z):
    owner = box_index // BOX_DEV
    start_x = owner // N_GY * CX + anchor_x[box_index]
    start_y = owner % N_GY * CY + anchor_y[box_index]
    return (start_x.astype(jnp.int32), start_y.astype(jnp.int32), anchor_z[box_index].astype(jnp.int32))

def reference(occupied, virtual, trials, anchor_x, anchor_y, anchor_z):
    zero = jnp.int32(0)
    grid = jnp.zeros((TRIALS, NX + BOX, NY + BOX, NZ), jnp.float32)

    def deposit(grid, box_index):
        mixture = jnp.einsum('tia,ar->tir', trials[box_index].astype(jnp.float32), virtual[box_index].astype(jnp.float32))
        box_density = lax.optimization_barrier(jnp.sum(occupied[box_index].astype(jnp.float32)[None] * mixture, axis=1))
        start_x, start_y, start_z = box_anchor(box_index, anchor_x, anchor_y, anchor_z)
        spot = (zero, start_x, start_y, start_z)
        block = lax.dynamic_slice(grid, spot, (TRIALS, BOX, BOX, BOX))
        block = block + box_density.reshape(TRIALS, BOX, BOX, BOX)
        return (lax.dynamic_update_slice(grid, block, spot), None)
    grid, _ = lax.scan(deposit, grid, jnp.arange(BOXES, dtype=jnp.int32))
    folded = grid[:, :NX].at[:, :BOX].add(grid[:, NX:])
    density = folded[:, :, :NY].at[:, :, :BOX].add(folded[:, :, NY:])
    potential = vcycle(density, 0)
    padded = jnp.concatenate([potential, potential[:, :BOX]], axis=1)
    padded = jnp.concatenate([padded, padded[:, :, :BOX]], axis=2)
    scale = float(BOX) ** (-1.5)

    def project(box_index):
        start_x, start_y, start_z = box_anchor(box_index, anchor_x, anchor_y, anchor_z)
        window = lax.dynamic_slice(padded, (zero, start_x, start_y, start_z), (TRIALS, BOX, BOX, BOX))
        window = window.reshape(TRIALS, BOX * BOX * BOX)
        weighted = (occupied[box_index].astype(jnp.float32)[None] * window[:, None]).astype(jnp.bfloat16)
        return scale * jnp.einsum('tir,ar->tia', weighted.astype(jnp.float32), virtual[box_index].astype(jnp.float32))
    coupling = lax.map(project, jnp.arange(BOXES, dtype=jnp.int32))
    return (potential, coupling)
```

```python
import functools

import jax
import jax.numpy as jnp
import numpy as np
from jax import lax
from jax.experimental import pallas as pl
from jax.experimental.pallas import tpu as pltpu
from jax.sharding import PartitionSpec as P

BOX = 32
TRIALS = 4
CX = 8
CY = 128
NZ = 128
SCREEN = 0.05
DAMPING = 2.0 / 3.0
MESH = pl.DeviceIdType.MESH
F32 = jnp.float32
BF16 = jnp.bfloat16
HIGH = lax.Precision.HIGHEST
VMEM = pl.BlockSpec(memory_space=pltpu.VMEM)
SMEM = pl.BlockSpec(memory_space=pltpu.SMEM)
ANY = pl.BlockSpec(memory_space=pl.ANY)


def center_of(level):
    spacing = 2.0**level
    return 6.0 / spacing**2 + SCREEN**2


def split2(x):
    hi = x.astype(BF16)
    lo = (x - hi.astype(F32)).astype(BF16)
    return hi, lo


def dot(a, b):
    return jnp.dot(a, b, preferred_element_type=F32)


def dot_right(x, w):
    hi, lo = split2(x)
    return dot(hi, w) + dot(lo, w)


def dot_left(w, x):
    hi, lo = split2(x)
    return dot(w, hi) + dot(w, lo)


def dot_high(a, b):
    return jnp.dot(a, b, preferred_element_type=F32, precision=HIGH)


def z_beside(x, n):
    if n == 128:
        return pltpu.roll(x, 1, 1) + pltpu.roll(x, 127, 1)
    lane = lax.broadcasted_iota(jnp.int32, x.shape, 1) % n
    below = jnp.where(lane == 0, pltpu.roll(x, 129 - n, 1), pltpu.roll(x, 1, 1))
    above = jnp.where(lane == n - 1, pltpu.roll(x, n - 1, 1), pltpu.roll(x, 127, 1))
    return below + above


def hartley_np(count):
    index = np.arange(count)
    angle = 2.0 * np.pi / count * ((index[:, None] * index[None, :]) % count)
    return (np.cos(angle) + np.sin(angle)) / np.sqrt(count)


def eigen_np(count, spacing):
    return (2.0 - 2.0 * np.cos(2.0 * np.pi / count * np.arange(count))) / (spacing * spacing)


@functools.lru_cache(None)
def tables(slabs, tiles):
    out = {}
    r0 = np.zeros((2, 128, 2, 64))
    r1 = np.zeros((2, 2, 64, 4, 32))
    p1 = np.zeros((2, 4, 32, 2, 64))
    p0 = np.zeros((2, 64, 2, 128))
    for t in range(2):
        for z in range(128):
            r0[t, z, t, z // 2] = 0.125
            p0[t, z // 2, t, z] = 1.0
        for z in range(64):
            for p in range(2):
                r1[p, t, z, 2 * p + t, z // 2] = 0.125
                p1[p, 2 * p + t, z // 2, t, z] = 1.0
    out["r0"] = r0.reshape(256, 128)
    out["r1"] = r1.reshape(2, 128, 128)
    out["p1"] = p1.reshape(2, 128, 128)
    out["p0"] = p0.reshape(128, 256)
    hz = hartley_np(16)
    mean_z = np.zeros((32, 16))
    mean_z[np.arange(32), np.arange(32) // 2] = 1.0
    fz = np.zeros((4, 32, 128))
    bz = np.zeros((128, 4, 32))
    for t in range(4):
        fz[t, :, t * 16 : t * 16 + 16] = 0.125 * mean_z @ hz
        bz[t * 16 : t * 16 + 16, t, :] = hz @ mean_z.T
    out["fz"] = fz.reshape(128, 128)
    out["bz"] = bz.reshape(128, 128)
    size_y = 16 * tiles
    hy = hartley_np(size_y)
    mean_y = np.zeros((16, 32))
    mean_y[np.arange(32) // 2, np.arange(32)] = 1.0
    fy = np.zeros((tiles, size_y, 128))
    by = np.zeros((tiles, 48, 128))
    for q in range(tiles):
        fy[q, :, :32] = hy[:, q * 16 : q * 16 + 16] @ mean_y
        for y in range(-2, 34):
            by[q, 8 + y, :size_y] = hy[(q * 16 + y // 2) % size_y]
    out["fy"] = fy
    out["by"] = by
    out["kx"] = np.kron(hartley_np(slabs), np.eye(8))
    lam_x, lam_y, lam_z = eigen_np(slabs, 8.0), eigen_np(size_y, 8.0), eigen_np(16, 8.0)
    inv = np.zeros((tiles, slabs, 8, 2, 4, 16))
    for q in range(tiles):
        ky = lam_y[q * 16 : q * 16 + 16].reshape(2, 8)
        total = (
            SCREEN * SCREEN
            + lam_x[:, None, None, None, None]
            + ky.T[None, :, :, None, None]
            + lam_z[None, None, None, None, :]
        )
        inv[q] = np.broadcast_to(1.0 / total, (slabs, 8, 2, 4, 16))
    out["inv"] = inv.reshape(tiles, slabs * 8, 128)
    return out


def density_kernel(ax_ref, occ_ref, vir_ref, mix_ref, out_ref):
    out_ref[...] = jnp.zeros_like(out_ref)
    for b in range(2):
        weights = mix_ref[b]

        def step(s, carry, b=b, weights=weights):
            rows = pl.ds(pl.multiple_of(s * 16, 16), 16)
            vir = vir_ref[b, :, rows, :].astype(F32)
            occ = occ_ref[b, :, rows, :].astype(F32)
            parts = [vir[:, 8 * h : 8 * h + 8].reshape(64, 128) for h in range(2)]
            mixed = dot(weights, jnp.concatenate(parts, axis=1).astype(BF16))
            mixed = mixed.reshape(8, 4, 8, 256)
            for h in range(2):
                dens = jnp.sum(occ[:, None, 8 * h : 8 * h + 8] * mixed[..., 128 * h : 128 * h + 128], axis=0)
                out_ref[ax_ref[b] + 2 * s + h, b] = dens
            return carry

        lax.fori_loop(0, 16, step, 0)


def deposit_kernel(src_ref, anc_ref, got_ref, ganc_ref, send, recv):
    gx, gy = lax.axis_index("gx"), lax.axis_index("gy")
    n = lax.axis_size("gx")
    targets = [1, 2, 3, 4, -1]
    barrier = pltpu.get_barrier_semaphore()
    for k in targets:
        pl.semaphore_signal(barrier, inc=1, device_id=(lax.rem(gx - k + n, n), gy), device_id_type=MESH)
    pl.semaphore_wait(barrier, 5)
    pieces = [(7, 10, 0), (15, 10, 0), (23, 10, 0), (31, 8, 0), (0, 1, 9)]
    copies = []
    for s, k in enumerate(targets):
        first, count, to = pieces[s]
        where = (lax.rem(gx + k + n, n), gy)
        copies.append(
            pltpu.make_async_remote_copy(
                src_ref=anc_ref,
                dst_ref=ganc_ref.at[s],
                send_sem=send.at[5 + s],
                recv_sem=recv.at[5 + s],
                device_id=where,
                device_id_type=MESH,
            )
        )
        copies.append(
            pltpu.make_async_remote_copy(
                src_ref=src_ref.at[pl.ds(first, count)],
                dst_ref=got_ref.at[s, pl.ds(to, count)],
                send_sem=send.at[s],
                recv_sem=recv.at[s],
                device_id=where,
                device_id_type=MESH,
            )
        )
    for c in copies:
        c.start()
    for c in copies:
        c.wait()


def box_anchors(anc_ref, ganc_ref, sources):
    pairs = []
    for s in sources:
        for b in range(2):
            if s < 0:
                pairs.append((anc_ref[0, b], anc_ref[0, 2 + b]))
            else:
                pairs.append((ganc_ref[s, 0, b], ganc_ref[s, 0, 2 + b]))
    return pairs


def select_rows(pairs):
    row = lax.broadcasted_iota(jnp.int32, (160, 320), 0)
    col = lax.broadcasted_iota(jnp.int32, (160, 320), 1)
    want = 4 * (col % 8) + (col // 8) % 4
    box = col // 32
    for k, (ay, _) in enumerate(pairs):
        want = want + jnp.where(box == k, ay, 0)
    return jnp.where(row == want, 1.0, 0.0).astype(BF16)


def accumulate_kernel(anc_ref, ganc_ref, own_ref, got_ref, out_ref, sel_ref):
    usual = box_anchors(anc_ref, ganc_ref, [-1, 0, 1, 2, 3])
    last = box_anchors(anc_ref, ganc_ref, [-1, 0, 1, 2, 4])
    sel_ref[0] = select_rows(usual)
    sel_ref[1] = select_rows(last)
    lane = lax.broadcasted_iota(jnp.int32, (8, 128), 1)
    blank = jnp.zeros((8, 128), F32)

    def plane(e, which, own, got, edge):
        pairs = last if edge else usual
        loads = []
        for s in range(5):
            for b in range(2):
                if s == 0:
                    loads.append((lambda t, b=b: own_ref[e - 1, b, t]) if own else None)
                elif s == 4 and edge:
                    loads.append(lambda t, b=b: got_ref[4, 9, b, t])
                elif s in got:
                    loads.append(lambda t, s=s, b=b: got_ref[s - 1, e, b, t])
                else:
                    loads.append(None)
        masks = [(lane >= az) & (lane < az + 32) for _, az in pairs]
        for half in range(2):
            columns = []
            for t in (2 * half, 2 * half + 1):
                rows = []
                for k, load in enumerate(loads):
                    if load is None:
                        rows += [blank] * 4
                        continue
                    value = load(t)
                    for j in range(4):
                        moved = pltpu.roll(value, lax.rem(pairs[k][1] + 128 - 32 * j, 128), 1)
                        rows.append(jnp.where(masks[k], moved, 0.0))
                columns.append(jnp.concatenate(rows, axis=0))
            placed = dot_left(sel_ref[which], jnp.concatenate(columns, axis=1))
            out_ref[e, 2 * half] = placed[:, :128]
            out_ref[e, 2 * half + 1] = placed[:, 128:]

    plane(0, 0, False, (1, 2, 3, 4), False)

    def step(e, carry):
        plane(e, 0, True, (1, 2, 3, 4), False)
        return carry

    lax.fori_loop(1, 8, step, 0)
    plane(8, 0, True, (1, 2, 3), False)
    plane(9, 1, True, (1, 2, 3), True)


def cycle_kernel(
    f_ref, r0_ref, r1_ref, p1_ref, p0_ref, fz_ref, bz_ref, fy_ref, by_ref, kx_ref, inv_ref,
    pot_ref, margin_ref,
    rim, low, fp, f1p, f2p, v0, v1p, w1, v2p, w2, tmp, tmp1, qs, qr, gs, gall, us, ur,
    send, recv, gsend, grecv,
):
    gx, gy = lax.axis_index("gx"), lax.axis_index("gy")
    n, m = lax.axis_size("gx"), lax.axis_size("gy")
    east, west = lax.rem(gx + 1, n), lax.rem(gx + n - 1, n)
    north, south = lax.rem(gy + 1, m), lax.rem(gy + m - 1, m)

    barrier = pltpu.get_barrier_semaphore()
    for d in range(1, m):
        pl.semaphore_signal(barrier, inc=1, device_id=(gx, lax.rem(gy + d, m)), device_id_type=MESH)
    for x in (east, west):
        for y in (north, south):
            pl.semaphore_signal(barrier, inc=1, device_id=(x, y), device_id_type=MESH)

    def greet(d, carry):
        pl.semaphore_signal(barrier, inc=1, device_id=(lax.rem(gx + d, n), gy), device_id_type=MESH)
        return carry

    lax.fori_loop(1, n, greet, 0)
    pl.semaphore_wait(barrier, m - 1 + 4 + n - 1)

    def copy(src, dst, slot, x, y):
        return pltpu.make_async_remote_copy(
            src_ref=src, dst_ref=dst, send_sem=send.at[slot], recv_sem=recv.at[slot],
            device_id=(x, y), device_id_type=MESH,
        )

    copies = [
        copy(f_ref.at[:, :, pl.ds(120, 40), :], rim, 0, gx, north),
        copy(f_ref.at[:, :, pl.ds(0, 8), :], low, 1, gx, south),
    ]
    for c in copies:
        c.start()
    for c in copies:
        c.wait()

    def join(e, carry):
        for t in range(4):
            fp[e, t, 0:8] = rim[e, t, 0:8]
            fp[e, t, 8:40] = f_ref[e, t, 0:32] + rim[e, t, 8:40]
            fp[e, t, 40:136] = f_ref[e, t, 32:128]
            fp[e, t, 136:144] = f_ref[e, t, 128:136] + low[e, t]
        return carry

    lax.fori_loop(0, 10, join, 0)

    scale = DAMPING / center_of(0)

    def down0(xc, carry):
        for p in range(2):
            halves = []
            for t in (2 * p, 2 * p + 1):
                total = None
                for x in range(2):
                    e = 2 * xc + 1 + x
                    mid = fp[e, t, 8:136]
                    beside = fp[e, t, 7:135] + fp[e, t, 9:137] + fp[e - 1, t, 8:136] + fp[e + 1, t, 8:136]
                    beside = beside + z_beside(mid, 128)
                    res = (1.0 - DAMPING) * mid + scale * beside
                    total = res if total is None else total + res
                tmp[0:128, :] = total
                halves.append(tmp[pl.ds(0, 64, stride=2), :] + tmp[pl.ds(1, 64, stride=2), :])
            f1p[2 + xc, p, 8:72] = dot_right(jnp.concatenate(halves, axis=1), r0_ref[...])
        return carry

    lax.fori_loop(0, 4, down0, 0)

    def swap(buf, a, c, slot):
        lead = (slice(None),) * (len(buf.shape) - 3)

        def part(x0, nx, y0, ny):
            return buf.at[(pl.ds(x0, nx),) + lead + (pl.ds(y0, ny),)]

        hi_x, lo_x, hi_y, lo_y = a, 2, c, 8
        return [
            copy(part(hi_x, 2, 8, c), part(0, 2, 8, c), slot, east, gy),
            copy(part(lo_x, 2, 8, c), part(a + 2, 2, 8, c), slot + 1, west, gy),
            copy(part(2, a, hi_y, 8), part(2, a, 0, 8), slot + 2, gx, north),
            copy(part(2, a, lo_y, 8), part(2, a, c + 8, 8), slot + 3, gx, south),
            copy(part(hi_x, 2, hi_y, 8), part(0, 2, 0, 8), slot + 4, east, north),
            copy(part(hi_x, 2, lo_y, 8), part(0, 2, c + 8, 8), slot + 5, east, south),
            copy(part(lo_x, 2, hi_y, 8), part(a + 2, 2, 0, 8), slot + 6, west, north),
            copy(part(lo_x, 2, lo_y, 8), part(a + 2, 2, c + 8, 8), slot + 7, west, south),
        ]

    copies = swap(f1p, 4, 64, 2)
    for c in copies:
        c.start()
    for c in copies:
        c.wait()

    scale = DAMPING / center_of(1) / 4.0
    for xc in range(2):
        total = None
        for p in range(2):
            both = None
            for x in range(2):
                e = 2 + 2 * xc + x
                mid = f1p[e, p, 8:72]
                beside = f1p[e, p, 7:71] + f1p[e, p, 9:73] + f1p[e - 1, p, 8:72] + f1p[e + 1, p, 8:72]
                beside = beside + z_beside(mid, 64)
                res = (1.0 - DAMPING) * mid + scale * beside
                both = res if both is None else both + res
            tmp[0:64, :] = both
            pair = tmp[pl.ds(0, 32, stride=2), :] + tmp[pl.ds(1, 32, stride=2), :]
            part = dot_right(pair, r1_ref[p])
            total = part if total is None else total + part
        f2p[2 + xc, 8:40] = total

    copies = swap(f2p, 2, 32, 10)
    for c in copies:
        c.start()
    for c in copies:
        c.wait()

    scale = DAMPING / center_of(2) / 16.0
    total = None
    for x in range(2):
        e = 2 + x
        mid = f2p[e, 8:40]
        beside = f2p[e, 7:39] + f2p[e, 9:41] + f2p[e - 1, 8:40] + f2p[e + 1, 8:40]
        beside = beside + z_beside(mid, 32)
        res = (1.0 - DAMPING) * mid + scale * beside
        total = res if total is None else total + res
    modes = dot_high(total, fz_ref[...])
    modes = jnp.concatenate([modes, jnp.zeros((96, 128), F32)], axis=0)
    modes = dot_high(fy_ref[gy], modes)
    for q in range(m):
        qs[q] = modes[16 * q : 16 * q + 8] + pltpu.roll(modes[16 * q + 8 : 16 * q + 16], 64, 1)
    copies = []
    for d in range(1, m):
        to = lax.rem(gy + d, m)
        copies.append(copy(qs.at[to], qr.at[d - 1], 17 + d, gx, to))
    for c in copies:
        c.start()
    mine = qs[gy]
    for c in copies:
        c.wait()
    for d in range(1, m):
        mine = mine + qr[d - 1]
    gs[...] = mine

    def shout(d):
        return pltpu.make_async_remote_copy(
            src_ref=gs, dst_ref=gall.at[gx], send_sem=gsend.at[d], recv_sem=grecv.at[d],
            device_id=(lax.rem(gx + d, n), gy), device_id_type=MESH,
        )

    def begin(d, carry):
        shout(d).start()
        return carry

    def end(d, carry):
        shout(d).wait()
        return carry

    lax.fori_loop(1, n, begin, 0)
    gall[gx] = mine
    lax.fori_loop(1, n, end, 0)
    spectrum = dot_high(kx_ref[...], gall[...].reshape(8 * n, 128)) * inv_ref[gy]
    for s, x in enumerate((west, gx, east)):
        us[s] = dot_high(kx_ref[pl.ds(pl.multiple_of(8 * x, 8), 8), :], spectrum)

    copies = []
    for d in range(1, m):
        to = lax.rem(gy + d, m)
        copies.append(copy(us, ur.at[gy], 21 + d, gx, to))
    for c in copies:
        c.start()
    ur[gy] = us[...]
    for c in copies:
        c.wait()

    scale = DAMPING / center_of(2)
    for s in range(3):
        rows = []
        for q in range(m):
            half = ur[q, s]
            rows += [half, pltpu.roll(half, 64, 1)]
        if m < 8:
            rows.append(jnp.zeros((128 - 16 * m, 128), F32))
        ahead = dot_high(by_ref[gy], jnp.concatenate(rows, axis=0))
        ahead = dot_high(ahead, bz_ref[...])
        for x in range(2):
            v2p[2 * s + x] = scale * f2p[2 * s + x] + ahead
    for e in range(1, 5):
        mid = v2p[e]
        beside = v2p[e - 1] + v2p[e + 1] + pltpu.roll(mid, 1, 0) + pltpu.roll(mid, 47, 0)
        beside = beside + z_beside(mid, 32)
        w2[e - 1] = (1.0 - DAMPING) * mid + scale * f2p[e] + (scale / 16.0) * beside

    scale = DAMPING / center_of(1)
    for e in range(4):
        for p in range(2):
            wide = dot_right(w2[e, 4:44], p1_ref[p])
            tmp[pl.ds(0, 40, stride=2), :] = wide
            tmp[pl.ds(1, 40, stride=2), :] = wide
            for x in range(2):
                v1p[2 * e + x, p] = scale * f1p[2 * e + x, p] + tmp[0:80, :]

    def up1(e, carry):
        for p in range(2):
            mid = v1p[e, p]
            beside = v1p[e - 1, p] + v1p[e + 1, p] + pltpu.roll(mid, 1, 0) + pltpu.roll(mid, 79, 0)
            beside = beside + z_beside(mid, 64)
            w1[e - 1, p] = (1.0 - DAMPING) * mid + scale * f1p[e, p] + (scale / 4.0) * beside
        return carry

    lax.fori_loop(1, 7, up1, 0)

    scale = DAMPING / center_of(0)

    def widen(i, p):
        wide = dot_right(w1[i, p, 4:76], p0_ref[...])
        tmp1[0, pl.ds(0, 72, stride=2), :] = wide[:, :128]
        tmp1[0, pl.ds(1, 72, stride=2), :] = wide[:, :128]
        tmp1[1, pl.ds(0, 72, stride=2), :] = wide[:, 128:]
        tmp1[1, pl.ds(1, 72, stride=2), :] = wide[:, 128:]

    for i, e in ((0, 0), (5, 9)):
        for p in range(2):
            widen(i, p)
            for t in range(2):
                v0[e, 2 * p + t] = scale * fp[e, 2 * p + t] + tmp1[t]

    def raise0(i, carry):
        for p in range(2):
            widen(i, p)
            for x in range(2):
                for t in range(2):
                    v0[2 * i - 1 + x, 2 * p + t] = scale * fp[2 * i - 1 + x, 2 * p + t] + tmp1[t]
        return carry

    lax.fori_loop(1, 5, raise0, 0)

    def up0(e, carry):
        for t in range(4):
            mid = v0[e, t, 8:136]
            beside = v0[e, t, 7:135] + v0[e, t, 9:137] + v0[e - 1, t, 8:136] + v0[e + 1, t, 8:136]
            beside = beside + z_beside(mid, 128)
            pot_ref[t, e - 1] = (1.0 - DAMPING) * mid + scale * (fp[e, t, 8:136] + beside)
        return carry

    lax.fori_loop(1, 9, up0, 0)
    last = copy(pot_ref.at[:, :, pl.ds(0, 32), :], margin_ref, 26, gx, south)
    last.start()
    last.wait()


def window_kernel(anc_ref, ganc_ref, pot_ref, margin_ref, out_ref, win_ref, sel_ref):
    pairs = box_anchors(anc_ref, ganc_ref, [-1, 0, 1, 2, 3])
    row = lax.broadcasted_iota(jnp.int32, (320, 160), 0)
    col = lax.broadcasted_iota(jnp.int32, (320, 160), 1)
    want = 4 * (row % 8) + (row // 8) % 4
    box = row // 32
    for k, (ay, _) in enumerate(pairs):
        want = want + jnp.where(box == k, ay, 0)
    sel_ref[...] = jnp.where(col == want, 1.0, 0.0).astype(BF16)
    group = lax.broadcasted_iota(jnp.int32, (8, 128), 1) // 32

    def plane(x, carry):
        for half in range(2):
            columns = []
            for t in (2 * half, 2 * half + 1):
                here = pot_ref[t, x]
                out_ref[t, x] = here
                columns.append(jnp.concatenate([here, margin_ref[t, x]], axis=0))
            taken = dot_left(sel_ref[...], jnp.concatenate(columns, axis=1))
            for u in range(2):
                for k in range(10):
                    total = None
                    for j in range(4):
                        piece = taken[32 * k + 8 * j : 32 * k + 8 * j + 8, 128 * u : 128 * u + 128]
                        piece = pltpu.roll(piece, lax.rem(128 + 32 * j - pairs[k][1], 128), 1)
                        total = piece if total is None else jnp.where(group == j, piece, total)
                    win_ref[k // 2, x, k % 2, 2 * half + u] = total
        return carry

    lax.fori_loop(0, 8, plane, 0)


def return_kernel(src_ref, got_ref, send, recv):
    gx, gy = lax.axis_index("gx"), lax.axis_index("gy")
    n = lax.axis_size("gx")
    barrier = pltpu.get_barrier_semaphore()
    for k in range(1, 5):
        pl.semaphore_signal(barrier, inc=1, device_id=(lax.rem(gx + k, n), gy), device_id_type=MESH)
    pl.semaphore_wait(barrier, 4)
    copies = []
    for k in range(1, 5):
        copies.append(
            pltpu.make_async_remote_copy(
                src_ref=src_ref.at[k],
                dst_ref=got_ref.at[k - 1],
                send_sem=send.at[k - 1],
                recv_sem=recv.at[k - 1],
                device_id=(lax.rem(gx - k + n, n), gy),
                device_id_type=MESH,
            )
        )
    for c in copies:
        c.start()
    for c in copies:
        c.wait()


def project_kernel(ax_ref, occ_ref, vir_ref, own_ref, got_ref, out_ref, win):
    win[0:8] = own_ref[0]
    for k in range(4):
        win[8 * k + 8 : 8 * k + 16] = got_ref[k]
    for b in range(2):

        def step(s, total, b=b):
            left, right = [], []
            for h in range(4):
                rows = pl.ds(pl.multiple_of(s * 64 + 16 * h, 16), 16)
                occ = occ_ref[b, :, rows, :].astype(F32)
                vir = vir_ref[b, :, rows, :].astype(F32)
                for g in range(2):
                    cells = win[ax_ref[b] + s * 8 + 2 * h + g, b]
                    weighted = occ[None, :, 8 * g : 8 * g + 8] * cells[:, None]
                    left.append(weighted.reshape(256, 128).astype(BF16))
                    right.append(vir[:, 8 * g : 8 * g + 8].reshape(64, 128).astype(BF16))
            left, right = jnp.concatenate(left, axis=1), jnp.concatenate(right, axis=1)
            return total + lax.dot_general(
                left, right, (((1,), (1,)), ((), ())), preferred_element_type=F32
            )

        total = lax.fori_loop(0, 4, step, jnp.zeros((256, 64), F32))
        row = lax.broadcasted_iota(jnp.int32, (256, 64), 0) % 8
        col = lax.broadcasted_iota(jnp.int32, (256, 64), 1) % 8
        total = jnp.where(row == col, total, 0.0)
        total = jnp.sum(total.reshape(32, 8, 64), axis=1)
        col = lax.broadcasted_iota(jnp.int32, (64, 128), 1)
        row = lax.broadcasted_iota(jnp.int32, (64, 128), 0) // 8
        pick = jnp.where(row == col, float(BOX) ** (-1.5), 0.0)
        out_ref[b] = dot_high(total, pick)


def params(**more):
    return pltpu.CompilerParams(vmem_limit_bytes=40 * 1024 * 1024, **more)


def shaped(shape, dtype=F32):
    return jax.ShapeDtypeStruct(shape, dtype)


def per_device(slabs, tiles, occupied, virtual, trials, anchor_x, anchor_y, anchor_z):
    occ = occupied.reshape(2, 8, 256, 128)
    vir = virtual.reshape(2, 8, 256, 128)
    mix = jnp.einsum("btia,mn->bitman", trials, jnp.eye(8, dtype=BF16)).reshape(2, 256, 64)
    anchors = jnp.concatenate([anchor_y, anchor_z, jnp.zeros((124,), jnp.int32)])
    anchors = jnp.broadcast_to(anchors[None], (8, 128))
    tab = tables(slabs, tiles)
    exact = {k: jnp.asarray(tab[k], BF16) for k in ("r0", "r1", "p1", "p0")}
    wide = {k: jnp.asarray(tab[k], F32) for k in ("fz", "bz", "fy", "by", "kx", "inv")}

    dens = pl.pallas_call(
        density_kernel,
        out_shape=shaped((40, 2, 4, 8, 128)),
        in_specs=[SMEM, VMEM, VMEM, VMEM],
        out_specs=VMEM,
        compiler_params=params(),
        name="density",
    )(anchor_x, occ, vir, mix)

    got, ganc = pl.pallas_call(
        deposit_kernel,
        out_shape=(shaped((5, 10, 2, 4, 8, 128)), shaped((5, 8, 128), jnp.int32)),
        in_specs=[ANY, ANY],
        out_specs=(ANY, ANY),
        scratch_shapes=[pltpu.SemaphoreType.DMA((10,)), pltpu.SemaphoreType.DMA((10,))],
        compiler_params=params(collective_id=0, has_side_effects=True),
        name="deposit",
    )(dens, anchors)

    grid = pl.pallas_call(
        accumulate_kernel,
        out_shape=shaped((10, 4, 160, 128)),
        in_specs=[SMEM, SMEM, VMEM, VMEM],
        out_specs=VMEM,
        scratch_shapes=[pltpu.VMEM((2, 160, 320), BF16)],
        compiler_params=params(),
        name="accumulate",
    )(anchors, ganc, dens, got)

    names = ("r0", "r1", "p1", "p0")
    others = ("fz", "bz", "fy", "by", "kx", "inv")
    pot, margin = pl.pallas_call(
        cycle_kernel,
        out_shape=(shaped((4, 8, 128, 128)), shaped((4, 8, 32, 128))),
        in_specs=[VMEM] * 11,
        out_specs=(VMEM, VMEM),
        scratch_shapes=[
            pltpu.VMEM((10, 4, 40, 128), F32),
            pltpu.VMEM((10, 4, 8, 128), F32),
            pltpu.VMEM((10, 4, 144, 128), F32),
            pltpu.VMEM((8, 2, 80, 128), F32),
            pltpu.VMEM((6, 48, 128), F32),
            pltpu.VMEM((10, 4, 144, 128), F32),
            pltpu.VMEM((8, 2, 80, 128), F32),
            pltpu.VMEM((6, 2, 80, 128), F32),
            pltpu.VMEM((6, 48, 128), F32),
            pltpu.VMEM((4, 48, 128), F32),
            pltpu.VMEM((144, 128), F32),
            pltpu.VMEM((2, 144, 128), F32),
            pltpu.VMEM((tiles, 8, 128), F32),
            pltpu.VMEM((tiles, 8, 128), F32),
            pltpu.VMEM((8, 128), F32),
            pltpu.VMEM((slabs, 8, 128), F32),
            pltpu.VMEM((3, 8, 128), F32),
            pltpu.VMEM((tiles, 3, 8, 128), F32),
            pltpu.SemaphoreType.DMA((28,)),
            pltpu.SemaphoreType.DMA((28,)),
            pltpu.SemaphoreType.DMA((slabs,)),
            pltpu.SemaphoreType.DMA((slabs,)),
        ],
        compiler_params=params(collective_id=1, has_side_effects=True),
        name="cycle",
    )(grid, *[exact[k] for k in names], *[wide[k] for k in others])

    potential, windows = pl.pallas_call(
        window_kernel,
        out_shape=(shaped((4, 8, 128, 128)), shaped((5, 8, 2, 4, 8, 128))),
        in_specs=[SMEM, SMEM, VMEM, VMEM],
        out_specs=(VMEM, VMEM),
        scratch_shapes=[pltpu.VMEM((320, 160), BF16)],
        compiler_params=params(),
        name="window",
    )(anchors, ganc, pot, margin)

    back = pl.pallas_call(
        return_kernel,
        out_shape=shaped((4, 8, 2, 4, 8, 128)),
        in_specs=[ANY],
        out_specs=ANY,
        scratch_shapes=[pltpu.SemaphoreType.DMA((4,)), pltpu.SemaphoreType.DMA((4,))],
        compiler_params=params(collective_id=2, has_side_effects=True),
        name="send_back",
    )(windows)

    coupling = pl.pallas_call(
        project_kernel,
        out_shape=shaped((2, 32, 128)),
        in_specs=[SMEM, VMEM, VMEM, VMEM, VMEM],
        out_specs=VMEM,
        scratch_shapes=[pltpu.VMEM((40, 2, 4, 8, 128), F32)],
        compiler_params=params(),
        name="project",
    )(anchor_x, occ, vir, windows, back)
    return potential, coupling[:, :, :8].reshape(2, 4, 8, 8)


def solution(mesh):
    placed = (
        P(("gx", "gy"), None, None),
        P(("gx", "gy"), None, None),
        P(("gx", "gy"), None, None, None),
        P(("gx", "gy")),
        P(("gx", "gy")),
        P(("gx", "gy")),
    )
    return jax.shard_map(
        functools.partial(per_device, mesh.shape["gx"], mesh.shape["gy"]),
        mesh=mesh,
        in_specs=placed,
        out_specs=(P(None, "gx", "gy", None), P(("gx", "gy"), None, None, None)),
        check_vma=False,
    )
```

```python
import functools

import jax
import jax.numpy as jnp
import numpy as np
from jax import lax
from jax.experimental import pallas as pl
from jax.experimental.pallas import tpu as pltpu
from jax.sharding import PartitionSpec as P

BOX = 32
TRIALS = 4
CX = 8
CY = 128
NZ = 128
SCREEN = 0.05
DAMPING = 2.0 / 3.0
MESH = pl.DeviceIdType.MESH
F32 = jnp.float32
BF16 = jnp.bfloat16
HIGH = lax.Precision.HIGHEST
VMEM = pl.BlockSpec(memory_space=pltpu.VMEM)
SMEM = pl.BlockSpec(memory_space=pltpu.SMEM)
ANY = pl.BlockSpec(memory_space=pl.ANY)


def center_of(level):
    spacing = 2.0**level
    return 6.0 / spacing**2 + SCREEN**2


def split2(x):
    hi = x.astype(BF16)
    lo = (x - hi.astype(F32)).astype(BF16)
    return hi, lo


def dot(a, b):
    return jnp.dot(a, b, preferred_element_type=F32)


def dot_right(x, w):
    hi, lo = split2(x)
    return dot(hi, w) + dot(lo, w)


def dot_left(w, x):
    hi, lo = split2(x)
    return dot(w, hi) + dot(w, lo)


def dot_high(a, b):
    return jnp.dot(a, b, preferred_element_type=F32, precision=HIGH)


def z_beside(x, n):
    if n == 128:
        return pltpu.roll(x, 1, 1) + pltpu.roll(x, 127, 1)
    lane = lax.broadcasted_iota(jnp.int32, x.shape, 1) % n
    below = jnp.where(lane == 0, pltpu.roll(x, 129 - n, 1), pltpu.roll(x, 1, 1))
    above = jnp.where(lane == n - 1, pltpu.roll(x, n - 1, 1), pltpu.roll(x, 127, 1))
    return below + above


def hartley_np(count):
    index = np.arange(count)
    angle = 2.0 * np.pi / count * ((index[:, None] * index[None, :]) % count)
    return (np.cos(angle) + np.sin(angle)) / np.sqrt(count)


def eigen_np(count, spacing):
    return (2.0 - 2.0 * np.cos(2.0 * np.pi / count * np.arange(count))) / (spacing * spacing)


@functools.lru_cache(None)
def tables(slabs, tiles):
    out = {}
    r0 = np.zeros((2, 128, 2, 64))
    r1 = np.zeros((2, 2, 64, 4, 32))
    p1 = np.zeros((2, 4, 32, 2, 64))
    p0 = np.zeros((2, 64, 2, 128))
    for t in range(2):
        for z in range(128):
            r0[t, z, t, z // 2] = 0.125
            p0[t, z // 2, t, z] = 1.0
        for z in range(64):
            for p in range(2):
                r1[p, t, z, 2 * p + t, z // 2] = 0.125
                p1[p, 2 * p + t, z // 2, t, z] = 1.0
    out["r0"] = r0.reshape(256, 128)
    out["r1"] = r1.reshape(2, 128, 128)
    out["p1"] = p1.reshape(2, 128, 128)
    out["p0"] = p0.reshape(128, 256)
    hz = hartley_np(16)
    mean_z = np.zeros((32, 16))
    mean_z[np.arange(32), np.arange(32) // 2] = 1.0
    fz = np.zeros((4, 32, 128))
    bz = np.zeros((128, 4, 32))
    for t in range(4):
        fz[t, :, t * 16 : t * 16 + 16] = 0.125 * mean_z @ hz
        bz[t * 16 : t * 16 + 16, t, :] = hz @ mean_z.T
    out["fz"] = fz.reshape(128, 128)
    out["bz"] = bz.reshape(128, 128)
    size_y = 16 * tiles
    hy = hartley_np(size_y)
    mean_y = np.zeros((16, 32))
    mean_y[np.arange(32) // 2, np.arange(32)] = 1.0
    fy = np.zeros((tiles, size_y, 128))
    by = np.zeros((tiles, 48, 128))
    for q in range(tiles):
        fy[q, :, :32] = hy[:, q * 16 : q * 16 + 16] @ mean_y
        for y in range(-2, 34):
            by[q, 8 + y, :size_y] = hy[(q * 16 + y // 2) % size_y]
    out["fy"] = fy
    out["by"] = by
    out["kx"] = np.kron(hartley_np(slabs), np.eye(8))
    lam_x, lam_y, lam_z = eigen_np(slabs, 8.0), eigen_np(size_y, 8.0), eigen_np(16, 8.0)
    inv = np.zeros((tiles, slabs, 8, 2, 4, 16))
    for q in range(tiles):
        ky = lam_y[q * 16 : q * 16 + 16].reshape(2, 8)
        total = (
            SCREEN * SCREEN
            + lam_x[:, None, None, None, None]
            + ky.T[None, :, :, None, None]
            + lam_z[None, None, None, None, :]
        )
        inv[q] = np.broadcast_to(1.0 / total, (slabs, 8, 2, 4, 16))
    out["inv"] = inv.reshape(tiles, slabs * 8, 128)
    return out


def density_kernel(ax_ref, occ_ref, vir_ref, mix_ref, out_ref):
    out_ref[...] = jnp.zeros_like(out_ref)
    for b in range(2):
        weights = mix_ref[b]

        def step(s, carry, b=b, weights=weights):
            rows = pl.ds(pl.multiple_of(s * 16, 16), 16)
            vir = vir_ref[b, :, rows, :].astype(F32)
            occ = occ_ref[b, :, rows, :].astype(F32)
            parts = [vir[:, 8 * h : 8 * h + 8].reshape(64, 128) for h in range(2)]
            mixed = dot(weights, jnp.concatenate(parts, axis=1).astype(BF16))
            mixed = mixed.reshape(8, 4, 8, 256)
            for h in range(2):
                dens = jnp.sum(occ[:, None, 8 * h : 8 * h + 8] * mixed[..., 128 * h : 128 * h + 128], axis=0)
                out_ref[ax_ref[b] + 2 * s + h, b] = dens
            return carry

        lax.fori_loop(0, 16, step, 0)


def greet_slabs(gx, gy, n):
    barrier = pltpu.get_barrier_semaphore()
    for k in (-4, -3, -2, -1, 1, 2, 3, 4):
        pl.semaphore_signal(barrier, inc=1, device_id=(lax.rem(gx + k + n, n), gy), device_id_type=MESH)
    pl.semaphore_wait(barrier, 8)


def shift_slabs(sign, pieces, relays, send, recv):
    gx, gy = lax.axis_index("gx"), lax.axis_index("gy")
    n = lax.axis_size("gx")
    place = lax.rem(gx, 4) if sign > 0 else 3 - lax.rem(gx, 4)

    def copy(src, dst, slot, k):
        return pltpu.make_async_remote_copy(
            src_ref=src, dst_ref=dst, send_sem=send.at[slot], recv_sem=recv.at[slot],
            device_id=(lax.rem(gx + sign * k + n, n), gy), device_id_type=MESH,
        )

    count = len(pieces) + len(relays)
    outs = []
    for r, (k, src, dst, hold, least) in enumerate(relays):
        straight = copy(src, dst, len(pieces) + r, k)
        first = copy(src, hold, count + r, 4)
        second = copy(hold, dst, len(pieces) + r, k - 4)
        outs.append((straight, first, second, place >= least))
    for straight, first, second, bent in outs:
        pl.when(bent)(first.start)
    whole = [copy(src, dst, p, k) for p, (k, src, dst) in enumerate(pieces)]
    for c in whole:
        c.start()
    for straight, first, second, bent in outs:
        pl.when(jnp.logical_not(bent))(straight.start)
    for straight, first, second, bent in outs:

        def onward(first=first, second=second):
            first.wait_recv()
            second.start()

        pl.when(bent)(onward)
    for straight, first, second, bent in outs:

        def settle(first=first, second=second):
            first.wait_send()
            second.wait_send()

        pl.when(bent)(settle)
        pl.when(jnp.logical_not(bent))(straight.wait_send)
        straight.wait_recv()
    for c in whole:
        c.wait()


def deposit_kernel(src_ref, anc_ref, got_ref, ganc_ref, hold1, hold2, send, recv):
    gx, gy = lax.axis_index("gx"), lax.axis_index("gy")
    greet_slabs(gx, gy, lax.axis_size("gx"))
    pieces = [(k, anc_ref, ganc_ref.at[s]) for s, k in enumerate((1, 2, 3, 4, -1))]
    pieces += [
        (4, src_ref.at[pl.ds(31, 8)], got_ref.at[3, pl.ds(0, 8)]),
        (3, src_ref.at[pl.ds(23, 10)], got_ref.at[2]),
        (2, src_ref.at[pl.ds(15, 10), 0], got_ref.at[1, :, 0]),
        (-1, src_ref.at[pl.ds(0, 1)], got_ref.at[4, pl.ds(9, 1)]),
    ]
    relays = [
        (1, src_ref.at[pl.ds(7, 10)], got_ref.at[0], hold1, 3),
        (2, src_ref.at[pl.ds(15, 10), 1], got_ref.at[1, :, 1], hold2, 2),
    ]
    shift_slabs(1, pieces, relays, send, recv)


def box_anchors(anc_ref, ganc_ref, sources):
    pairs = []
    for s in sources:
        for b in range(2):
            if s < 0:
                pairs.append((anc_ref[0, b], anc_ref[0, 2 + b]))
            else:
                pairs.append((ganc_ref[s, 0, b], ganc_ref[s, 0, 2 + b]))
    return pairs


def select_rows(pairs):
    row = lax.broadcasted_iota(jnp.int32, (160, 320), 0)
    col = lax.broadcasted_iota(jnp.int32, (160, 320), 1)
    want = 4 * (col % 8) + (col // 8) % 4
    box = col // 32
    for k, (ay, _) in enumerate(pairs):
        want = want + jnp.where(box == k, ay, 0)
    return jnp.where(row == want, 1.0, 0.0).astype(BF16)


def accumulate_kernel(anc_ref, ganc_ref, own_ref, got_ref, out_ref, sel_ref):
    usual = box_anchors(anc_ref, ganc_ref, [-1, 0, 1, 2, 3])
    last = box_anchors(anc_ref, ganc_ref, [-1, 0, 1, 2, 4])
    sel_ref[0] = select_rows(usual)
    sel_ref[1] = select_rows(last)
    lane = lax.broadcasted_iota(jnp.int32, (8, 128), 1)
    blank = jnp.zeros((8, 128), F32)

    def plane(e, which, own, got, edge):
        pairs = last if edge else usual
        loads = []
        for s in range(5):
            for b in range(2):
                if s == 0:
                    loads.append((lambda t, b=b: own_ref[e - 1, b, t]) if own else None)
                elif s == 4 and edge:
                    loads.append(lambda t, b=b: got_ref[4, 9, b, t])
                elif s in got:
                    loads.append(lambda t, s=s, b=b: got_ref[s - 1, e, b, t])
                else:
                    loads.append(None)
        masks = [(lane >= az) & (lane < az + 32) for _, az in pairs]
        for half in range(2):
            columns = []
            for t in (2 * half, 2 * half + 1):
                rows = []
                for k, load in enumerate(loads):
                    if load is None:
                        rows += [blank] * 4
                        continue
                    value = load(t)
                    for j in range(4):
                        moved = pltpu.roll(value, lax.rem(pairs[k][1] + 128 - 32 * j, 128), 1)
                        rows.append(jnp.where(masks[k], moved, 0.0))
                columns.append(jnp.concatenate(rows, axis=0))
            placed = dot_left(sel_ref[which], jnp.concatenate(columns, axis=1))
            out_ref[e, 2 * half] = placed[:, :128]
            out_ref[e, 2 * half + 1] = placed[:, 128:]

    plane(0, 0, False, (1, 2, 3, 4), False)

    def step(e, carry):
        plane(e, 0, True, (1, 2, 3, 4), False)
        return carry

    lax.fori_loop(1, 8, step, 0)
    plane(8, 0, True, (1, 2, 3), False)
    plane(9, 1, True, (1, 2, 3), True)


def cycle_kernel(
    f_ref, r0_ref, r1_ref, p1_ref, p0_ref, fz_ref, bz_ref, fy_ref, by_ref, kx_ref, inv_ref,
    pot_ref, margin_ref,
    rim, sides, beyond, fp, f1p, f2p, v0, v1p, w1, v2p, w2, tmp, tmp1, qs, qr, gs, gall, us, ur,
    send, recv, gsend, grecv,
):
    gx, gy = lax.axis_index("gx"), lax.axis_index("gy")
    n, m = lax.axis_size("gx"), lax.axis_size("gy")
    east, west = lax.rem(gx + 1, n), lax.rem(gx + n - 1, n)
    north, south = lax.rem(gy + 1, m), lax.rem(gy + m - 1, m)

    barrier = pltpu.get_barrier_semaphore()
    for d in range(1, m):
        pl.semaphore_signal(barrier, inc=1, device_id=(gx, lax.rem(gy + d, m)), device_id_type=MESH)
    for x in (east, west):
        for y in (north, south):
            pl.semaphore_signal(barrier, inc=1, device_id=(x, y), device_id_type=MESH)

    def greet(d, carry):
        pl.semaphore_signal(barrier, inc=1, device_id=(lax.rem(gx + d, n), gy), device_id_type=MESH)
        return carry

    lax.fori_loop(1, n, greet, 0)
    pl.semaphore_wait(barrier, m - 1 + 4 + n - 1)

    def copy(src, dst, slot, x, y):
        return pltpu.make_async_remote_copy(
            src_ref=src, dst_ref=dst, send_sem=send.at[slot], recv_sem=recv.at[slot],
            device_id=(x, y), device_id_type=MESH,
        )

    def edge(e, carry):
        for t in range(4):
            sides[0, e, t : t + 1] = f_ref[e + 1, t, 127:128]
            sides[1, e, t : t + 1] = f_ref[e + 1, t, 0:1]
        return carry

    copies = [copy(f_ref.at[:, :, pl.ds(128, 32), :], rim, 0, gx, north)]
    copies[0].start()
    lax.fori_loop(0, 8, edge, 0)
    copies += [copy(sides.at[0], beyond.at[0], 1, gx, north), copy(sides.at[1], beyond.at[1], 38, gx, south)]
    for c in copies[1:]:
        c.start()

    def early(e, carry):
        for t in range(4):
            fp[e, t, 40:136] = f_ref[e, t, 32:128]
        return carry

    lax.fori_loop(0, 10, early, 0)
    for c in copies:
        c.wait()

    def join(e, carry):
        for t in range(4):
            fp[e, t, 8:40] = f_ref[e, t, 0:32] + rim[e, t]
        return carry

    def rims(e, carry):
        for t in range(4):
            fp[e, t, 7:8] = beyond[0, e - 1, t : t + 1]
            fp[e, t, 136:137] = f_ref[e, t, 128:129] + beyond[1, e - 1, t : t + 1]
        return carry

    lax.fori_loop(1, 9, rims, 0)
    lax.fori_loop(0, 10, join, 0)

    scale = DAMPING / center_of(0)

    def down0(xc, carry):
        for p in range(2):
            halves = []
            for t in (2 * p, 2 * p + 1):
                total = None
                for x in range(2):
                    e = 2 * xc + 1 + x
                    mid = fp[e, t, 8:136]
                    beside = fp[e, t, 7:135] + fp[e, t, 9:137] + fp[e - 1, t, 8:136] + fp[e + 1, t, 8:136]
                    beside = beside + z_beside(mid, 128)
                    res = (1.0 - DAMPING) * mid + scale * beside
                    total = res if total is None else total + res
                tmp[0:128, :] = total
                halves.append(tmp[pl.ds(0, 64, stride=2), :] + tmp[pl.ds(1, 64, stride=2), :])
            f1p[2 + xc, p, 8:72] = dot_right(jnp.concatenate(halves, axis=1), r0_ref[...])
        return carry

    lax.fori_loop(0, 4, down0, 0)

    def swap(buf, a, c, slot):
        lead = (slice(None),) * (len(buf.shape) - 3)

        def part(x0, nx, y0, ny):
            return buf.at[(pl.ds(x0, nx),) + lead + (pl.ds(y0, ny),)]

        near = [
            copy(part(a + 1, 1, 8, c), part(1, 1, 8, c), slot, east, gy),
            copy(part(2, 1, 8, c), part(a + 2, 1, 8, c), slot + 1, west, gy),
            copy(part(2, a, c, 8), part(2, a, 0, 8), slot + 2, gx, north),
            copy(part(2, a, 8, 8), part(2, a, c + 8, 8), slot + 3, gx, south),
        ]
        far = [
            copy(part(a, 1, 8, c), part(0, 1, 8, c), slot + 4, east, gy),
            copy(part(3, 1, 8, c), part(a + 3, 1, 8, c), slot + 5, west, gy),
            copy(part(a, 2, c, 8), part(0, 2, 0, 8), slot + 6, east, north),
            copy(part(a, 2, 8, 8), part(0, 2, c + 8, 8), slot + 7, east, south),
            copy(part(2, 2, c, 8), part(a + 2, 2, 0, 8), slot + 8, west, north),
            copy(part(2, 2, 8, 8), part(a + 2, 2, c + 8, 8), slot + 9, west, south),
        ]
        for one in near + far:
            one.start()
        for one in near:
            one.wait()
        return far

    far1 = swap(f1p, 4, 64, 2)

    scale = DAMPING / center_of(1) / 4.0
    for xc in range(2):
        total = None
        for p in range(2):
            both = None
            for x in range(2):
                e = 2 + 2 * xc + x
                mid = f1p[e, p, 8:72]
                beside = f1p[e, p, 7:71] + f1p[e, p, 9:73] + f1p[e - 1, p, 8:72] + f1p[e + 1, p, 8:72]
                beside = beside + z_beside(mid, 64)
                res = (1.0 - DAMPING) * mid + scale * beside
                both = res if both is None else both + res
            tmp[0:64, :] = both
            pair = tmp[pl.ds(0, 32, stride=2), :] + tmp[pl.ds(1, 32, stride=2), :]
            part = dot_right(pair, r1_ref[p])
            total = part if total is None else total + part
        f2p[2 + xc, 8:40] = total

    far2 = swap(f2p, 2, 32, 12)

    scale = DAMPING / center_of(2) / 16.0
    total = None
    for x in range(2):
        e = 2 + x
        mid = f2p[e, 8:40]
        beside = f2p[e, 7:39] + f2p[e, 9:41] + f2p[e - 1, 8:40] + f2p[e + 1, 8:40]
        beside = beside + z_beside(mid, 32)
        res = (1.0 - DAMPING) * mid + scale * beside
        total = res if total is None else total + res
    modes = dot_high(total, fz_ref[...])
    modes = jnp.concatenate([modes, jnp.zeros((96, 128), F32)], axis=0)
    modes = dot_high(fy_ref[gy], modes)
    for q in range(m):
        qs[q] = modes[16 * q : 16 * q + 8] + pltpu.roll(modes[16 * q + 8 : 16 * q + 16], 64, 1)
    copies = []
    for d in range(1, m):
        to = lax.rem(gy + d, m)
        copies.append(copy(qs.at[to], qr.at[d - 1], 22 + d, gx, to))
    for c in copies:
        c.start()
    mine = qs[gy]
    for c in copies:
        c.wait()
    for d in range(1, m):
        mine = mine + qr[d - 1]
    gs[...] = mine

    def shout(d):
        return pltpu.make_async_remote_copy(
            src_ref=gs, dst_ref=gall.at[gx], send_sem=gsend.at[d], recv_sem=grecv.at[d],
            device_id=(lax.rem(gx + d, n), gy), device_id_type=MESH,
        )

    def begin(d, carry):
        shout(d).start()
        return carry

    def end(d, carry):
        shout(d).wait()
        return carry

    lax.fori_loop(1, n, begin, 0)
    gall[gx] = mine
    lax.fori_loop(1, n, end, 0)
    spectrum = dot_high(kx_ref[...], gall[...].reshape(8 * n, 128)) * inv_ref[gy]
    for s, x in enumerate((west, gx, east)):
        us[s] = dot_high(kx_ref[pl.ds(pl.multiple_of(8 * x, 8), 8), :], spectrum)

    copies = []
    for d in range(1, m):
        to = lax.rem(gy + d, m)
        copies.append(copy(us, ur.at[gy], 28 + d, gx, to))
    for c in copies:
        c.start()
    ur[gy] = us[...]
    for c in copies:
        c.wait()

    for c in far2:
        c.wait()
    scale = DAMPING / center_of(2)
    for s in range(3):
        rows = []
        for q in range(m):
            half = ur[q, s]
            rows += [half, pltpu.roll(half, 64, 1)]
        if m < 8:
            rows.append(jnp.zeros((128 - 16 * m, 128), F32))
        ahead = dot_high(by_ref[gy], jnp.concatenate(rows, axis=0))
        ahead = dot_high(ahead, bz_ref[...])
        for x in range(2):
            v2p[2 * s + x] = scale * f2p[2 * s + x] + ahead
    for e in range(1, 5):
        mid = v2p[e]
        beside = v2p[e - 1] + v2p[e + 1] + pltpu.roll(mid, 1, 0) + pltpu.roll(mid, 47, 0)
        beside = beside + z_beside(mid, 32)
        w2[e - 1] = (1.0 - DAMPING) * mid + scale * f2p[e] + (scale / 16.0) * beside

    for c in far1:
        c.wait()
    scale = DAMPING / center_of(1)
    for e in range(4):
        for p in range(2):
            wide = dot_right(w2[e, 4:44], p1_ref[p])
            tmp[pl.ds(0, 40, stride=2), :] = wide
            tmp[pl.ds(1, 40, stride=2), :] = wide
            for x in range(2):
                v1p[2 * e + x, p] = scale * f1p[2 * e + x, p] + tmp[0:80, :]

    def up1(e, carry):
        for p in range(2):
            mid = v1p[e, p]
            beside = v1p[e - 1, p] + v1p[e + 1, p] + pltpu.roll(mid, 1, 0) + pltpu.roll(mid, 79, 0)
            beside = beside + z_beside(mid, 64)
            w1[e - 1, p] = (1.0 - DAMPING) * mid + scale * f1p[e, p] + (scale / 4.0) * beside
        return carry

    lax.fori_loop(1, 7, up1, 0)

    scale = DAMPING / center_of(0)

    def widen(i, p):
        wide = dot_right(w1[i, p, 4:76], p0_ref[...])
        tmp1[0, pl.ds(0, 72, stride=2), :] = wide[:, :128]
        tmp1[0, pl.ds(1, 72, stride=2), :] = wide[:, :128]
        tmp1[1, pl.ds(0, 72, stride=2), :] = wide[:, 128:]
        tmp1[1, pl.ds(1, 72, stride=2), :] = wide[:, 128:]

    for i, e in ((0, 0), (5, 9)):
        for p in range(2):
            widen(i, p)
            for t in range(2):
                v0[e, 2 * p + t] = scale * fp[e, 2 * p + t] + tmp1[t]

    def raise0(i, carry):
        for p in range(2):
            widen(i, p)
            for x in range(2):
                for t in range(2):
                    v0[2 * i - 1 + x, 2 * p + t] = scale * fp[2 * i - 1 + x, 2 * p + t] + tmp1[t]
        return carry

    lax.fori_loop(1, 5, raise0, 0)

    def up0(e, carry):
        for t in range(4):
            mid = v0[e, t, 8:136]
            beside = v0[e, t, 7:135] + v0[e, t, 9:137] + v0[e - 1, t, 8:136] + v0[e + 1, t, 8:136]
            beside = beside + z_beside(mid, 128)
            pot_ref[t, e - 1] = (1.0 - DAMPING) * mid + scale * (fp[e, t, 8:136] + beside)
        return carry

    lax.fori_loop(1, 9, up0, 0)
    last = copy(pot_ref.at[:, :, pl.ds(0, 32), :], margin_ref, 37, gx, south)
    last.start()
    last.wait()


def window_kernel(anc_ref, ganc_ref, pot_ref, margin_ref, out_ref, win_ref, sel_ref):
    pairs = box_anchors(anc_ref, ganc_ref, [-1, 0, 1, 2, 3])
    row = lax.broadcasted_iota(jnp.int32, (320, 160), 0)
    col = lax.broadcasted_iota(jnp.int32, (320, 160), 1)
    want = 4 * (row % 8) + (row // 8) % 4
    box = row // 32
    for k, (ay, _) in enumerate(pairs):
        want = want + jnp.where(box == k, ay, 0)
    sel_ref[...] = jnp.where(col == want, 1.0, 0.0).astype(BF16)
    group = lax.broadcasted_iota(jnp.int32, (8, 128), 1) // 32

    def plane(x, carry):
        for half in range(2):
            columns = []
            for t in (2 * half, 2 * half + 1):
                here = pot_ref[t, x]
                out_ref[t, x] = here
                columns.append(jnp.concatenate([here, margin_ref[t, x]], axis=0))
            taken = dot_left(sel_ref[...], jnp.concatenate(columns, axis=1))
            for u in range(2):
                for k in range(10):
                    total = None
                    for j in range(4):
                        piece = taken[32 * k + 8 * j : 32 * k + 8 * j + 8, 128 * u : 128 * u + 128]
                        piece = pltpu.roll(piece, lax.rem(128 + 32 * j - pairs[k][1], 128), 1)
                        total = piece if total is None else jnp.where(group == j, piece, total)
                    win_ref[k // 2, x, k % 2, 2 * half + u] = total
        return carry

    lax.fori_loop(0, 8, plane, 0)


def return_kernel(src_ref, got_ref, hold1, hold2, send, recv):
    gx, gy = lax.axis_index("gx"), lax.axis_index("gy")
    greet_slabs(gx, gy, lax.axis_size("gx"))
    pieces = [
        (4, src_ref.at[4], got_ref.at[3]),
        (3, src_ref.at[3], got_ref.at[2]),
        (2, src_ref.at[2, :, 0], got_ref.at[1, :, 0]),
    ]
    relays = [
        (1, src_ref.at[1], got_ref.at[0], hold1, 3),
        (2, src_ref.at[2, :, 1], got_ref.at[1, :, 1], hold2, 2),
    ]
    shift_slabs(-1, pieces, relays, send, recv)


def project_kernel(ax_ref, occ_ref, vir_ref, own_ref, got_ref, out_ref, win):
    win[0:8] = own_ref[0]
    for k in range(4):
        win[8 * k + 8 : 8 * k + 16] = got_ref[k]
    for b in range(2):

        def step(s, total, b=b):
            left, right = [], []
            for h in range(4):
                rows = pl.ds(pl.multiple_of(s * 64 + 16 * h, 16), 16)
                occ = occ_ref[b, :, rows, :].astype(F32)
                vir = vir_ref[b, :, rows, :].astype(F32)
                for g in range(2):
                    cells = win[ax_ref[b] + s * 8 + 2 * h + g, b]
                    weighted = occ[None, :, 8 * g : 8 * g + 8] * cells[:, None]
                    left.append(weighted.reshape(256, 128).astype(BF16))
                    right.append(vir[:, 8 * g : 8 * g + 8].reshape(64, 128).astype(BF16))
            left, right = jnp.concatenate(left, axis=1), jnp.concatenate(right, axis=1)
            return total + lax.dot_general(
                left, right, (((1,), (1,)), ((), ())), preferred_element_type=F32
            )

        total = lax.fori_loop(0, 4, step, jnp.zeros((256, 64), F32))
        row = lax.broadcasted_iota(jnp.int32, (256, 64), 0) % 8
        col = lax.broadcasted_iota(jnp.int32, (256, 64), 1) % 8
        total = jnp.where(row == col, total, 0.0)
        total = jnp.sum(total.reshape(32, 8, 64), axis=1)
        col = lax.broadcasted_iota(jnp.int32, (64, 128), 1)
        row = lax.broadcasted_iota(jnp.int32, (64, 128), 0) // 8
        pick = jnp.where(row == col, float(BOX) ** (-1.5), 0.0)
        out_ref[b] = dot_high(total, pick)


def params(**more):
    return pltpu.CompilerParams(vmem_limit_bytes=40 * 1024 * 1024, **more)


def shaped(shape, dtype=F32):
    return jax.ShapeDtypeStruct(shape, dtype)


def per_device(slabs, tiles, occupied, virtual, trials, anchor_x, anchor_y, anchor_z):
    occ = occupied.reshape(2, 8, 256, 128)
    vir = virtual.reshape(2, 8, 256, 128)
    mix = jnp.einsum("btia,mn->bitman", trials, jnp.eye(8, dtype=BF16)).reshape(2, 256, 64)
    anchors = jnp.concatenate([anchor_y, anchor_z, jnp.zeros((124,), jnp.int32)])
    anchors = jnp.broadcast_to(anchors[None], (8, 128))
    tab = tables(slabs, tiles)
    exact = {k: jnp.asarray(tab[k], BF16) for k in ("r0", "r1", "p1", "p0")}
    wide = {k: jnp.asarray(tab[k], F32) for k in ("fz", "bz", "fy", "by", "kx", "inv")}

    dens = pl.pallas_call(
        density_kernel,
        out_shape=shaped((40, 2, 4, 8, 128)),
        in_specs=[SMEM, VMEM, VMEM, VMEM],
        out_specs=VMEM,
        compiler_params=params(),
        name="density",
    )(anchor_x, occ, vir, mix)

    got, ganc = pl.pallas_call(
        deposit_kernel,
        out_shape=(shaped((5, 10, 2, 4, 8, 128)), shaped((5, 8, 128), jnp.int32)),
        in_specs=[ANY, ANY],
        out_specs=(ANY, ANY),
        scratch_shapes=[
            pltpu.VMEM((10, 2, 4, 8, 128), F32),
            pltpu.VMEM((10, 4, 8, 128), F32),
            pltpu.SemaphoreType.DMA((13,)),
            pltpu.SemaphoreType.DMA((13,)),
        ],
        compiler_params=params(collective_id=0, has_side_effects=True),
        name="deposit",
    )(dens, anchors)

    grid = pl.pallas_call(
        accumulate_kernel,
        out_shape=shaped((10, 4, 160, 128)),
        in_specs=[SMEM, SMEM, VMEM, VMEM],
        out_specs=VMEM,
        scratch_shapes=[pltpu.VMEM((2, 160, 320), BF16)],
        compiler_params=params(),
        name="accumulate",
    )(anchors, ganc, dens, got)

    names = ("r0", "r1", "p1", "p0")
    others = ("fz", "bz", "fy", "by", "kx", "inv")
    pot, margin = pl.pallas_call(
        cycle_kernel,
        out_shape=(shaped((4, 8, 128, 128)), shaped((4, 8, 32, 128))),
        in_specs=[VMEM] * 11,
        out_specs=(VMEM, VMEM),
        scratch_shapes=[
            pltpu.VMEM((10, 4, 32, 128), F32),
            pltpu.VMEM((2, 8, 8, 128), F32),
            pltpu.VMEM((2, 8, 8, 128), F32),
            pltpu.VMEM((10, 4, 144, 128), F32),
            pltpu.VMEM((8, 2, 80, 128), F32),
            pltpu.VMEM((6, 48, 128), F32),
            pltpu.VMEM((10, 4, 144, 128), F32),
            pltpu.VMEM((8, 2, 80, 128), F32),
            pltpu.VMEM((6, 2, 80, 128), F32),
            pltpu.VMEM((6, 48, 128), F32),
            pltpu.VMEM((4, 48, 128), F32),
            pltpu.VMEM((144, 128), F32),
            pltpu.VMEM((2, 144, 128), F32),
            pltpu.VMEM((tiles, 8, 128), F32),
            pltpu.VMEM((tiles, 8, 128), F32),
            pltpu.VMEM((8, 128), F32),
            pltpu.VMEM((slabs, 8, 128), F32),
            pltpu.VMEM((3, 8, 128), F32),
            pltpu.VMEM((tiles, 3, 8, 128), F32),
            pltpu.SemaphoreType.DMA((39,)),
            pltpu.SemaphoreType.DMA((39,)),
            pltpu.SemaphoreType.DMA((slabs,)),
            pltpu.SemaphoreType.DMA((slabs,)),
        ],
        compiler_params=params(collective_id=1, has_side_effects=True),
        name="cycle",
    )(grid, *[exact[k] for k in names], *[wide[k] for k in others])

    potential, windows = pl.pallas_call(
        window_kernel,
        out_shape=(shaped((4, 8, 128, 128)), shaped((5, 8, 2, 4, 8, 128))),
        in_specs=[SMEM, SMEM, VMEM, VMEM],
        out_specs=(VMEM, VMEM),
        scratch_shapes=[pltpu.VMEM((320, 160), BF16)],
        compiler_params=params(),
        name="window",
    )(anchors, ganc, pot, margin)

    back = pl.pallas_call(
        return_kernel,
        out_shape=shaped((4, 8, 2, 4, 8, 128)),
        in_specs=[ANY],
        out_specs=ANY,
        scratch_shapes=[
            pltpu.VMEM((8, 2, 4, 8, 128), F32),
            pltpu.VMEM((8, 4, 8, 128), F32),
            pltpu.SemaphoreType.DMA((7,)),
            pltpu.SemaphoreType.DMA((7,)),
        ],
        compiler_params=params(collective_id=2, has_side_effects=True),
        name="send_back",
    )(windows)

    coupling = pl.pallas_call(
        project_kernel,
        out_shape=shaped((2, 32, 128)),
        in_specs=[SMEM, VMEM, VMEM, VMEM, VMEM],
        out_specs=VMEM,
        scratch_shapes=[pltpu.VMEM((40, 2, 4, 8, 128), F32)],
        compiler_params=params(),
        name="project",
    )(anchor_x, occ, vir, windows, back)
    return potential, coupling[:, :, :8].reshape(2, 4, 8, 8)


def solution(mesh):
    placed = (
        P(("gx", "gy"), None, None),
        P(("gx", "gy"), None, None),
        P(("gx", "gy"), None, None, None),
        P(("gx", "gy")),
        P(("gx", "gy")),
        P(("gx", "gy")),
    )
    return jax.shard_map(
        functools.partial(per_device, mesh.shape["gx"], mesh.shape["gy"]),
        mesh=mesh,
        in_specs=placed,
        out_specs=(P(None, "gx", "gy", None), P(("gx", "gy"), None, None, None)),
        check_vma=False,
    )
```

```python
import functools

import jax
import jax.numpy as jnp
import numpy as np
from jax import lax
from jax.experimental import pallas as pl
from jax.experimental.pallas import tpu as pltpu
from jax.sharding import PartitionSpec as P

BOX = 32
TRIALS = 4
CX = 8
CY = 128
NZ = 128
SCREEN = 0.05
DAMPING = 2.0 / 3.0
MESH = pl.DeviceIdType.MESH
F32 = jnp.float32
BF16 = jnp.bfloat16
HIGH = lax.Precision.HIGHEST
VMEM = pl.BlockSpec(memory_space=pltpu.VMEM)
SMEM = pl.BlockSpec(memory_space=pltpu.SMEM)
ANY = pl.BlockSpec(memory_space=pl.ANY)


def center_of(level):
    spacing = 2.0**level
    return 6.0 / spacing**2 + SCREEN**2


def split2(x):
    hi = x.astype(BF16)
    lo = (x - hi.astype(F32)).astype(BF16)
    return hi, lo


def dot(a, b):
    return jnp.dot(a, b, preferred_element_type=F32)


def dot_right(x, w):
    hi, lo = split2(x)
    return dot(hi, w) + dot(lo, w)


def dot_left(w, x):
    hi, lo = split2(x)
    return dot(w, hi) + dot(w, lo)


def dot_high(a, b):
    return jnp.dot(a, b, preferred_element_type=F32, precision=HIGH)


def z_beside(x, n):
    if n == 128:
        return pltpu.roll(x, 1, 1) + pltpu.roll(x, 127, 1)
    lane = lax.broadcasted_iota(jnp.int32, x.shape, 1) % n
    below = jnp.where(lane == 0, pltpu.roll(x, 129 - n, 1), pltpu.roll(x, 1, 1))
    above = jnp.where(lane == n - 1, pltpu.roll(x, n - 1, 1), pltpu.roll(x, 127, 1))
    return below + above


def hartley_np(count):
    index = np.arange(count)
    angle = 2.0 * np.pi / count * ((index[:, None] * index[None, :]) % count)
    return (np.cos(angle) + np.sin(angle)) / np.sqrt(count)


def eigen_np(count, spacing):
    return (2.0 - 2.0 * np.cos(2.0 * np.pi / count * np.arange(count))) / (spacing * spacing)


@functools.lru_cache(None)
def tables(slabs, tiles):
    out = {}
    r0 = np.zeros((2, 128, 2, 64))
    r1 = np.zeros((2, 2, 64, 4, 32))
    p1 = np.zeros((2, 4, 32, 2, 64))
    p0 = np.zeros((2, 64, 2, 128))
    for t in range(2):
        for z in range(128):
            r0[t, z, t, z // 2] = 0.125
            p0[t, z // 2, t, z] = 1.0
        for z in range(64):
            for p in range(2):
                r1[p, t, z, 2 * p + t, z // 2] = 0.125
                p1[p, 2 * p + t, z // 2, t, z] = 1.0
    out["r0"] = r0.reshape(256, 128)
    out["r1"] = r1.reshape(2, 128, 128)
    out["p1"] = p1.reshape(2, 128, 128)
    out["p0"] = p0.reshape(128, 256)
    hz = hartley_np(16)
    mean_z = np.zeros((32, 16))
    mean_z[np.arange(32), np.arange(32) // 2] = 1.0
    fz = np.zeros((4, 32, 128))
    bz = np.zeros((128, 4, 32))
    for t in range(4):
        fz[t, :, t * 16 : t * 16 + 16] = 0.125 * mean_z @ hz
        bz[t * 16 : t * 16 + 16, t, :] = hz @ mean_z.T
    out["fz"] = fz.reshape(128, 128)
    out["bz"] = bz.reshape(128, 128)
    size_y = 16 * tiles
    hy = hartley_np(size_y)
    mean_y = np.zeros((16, 32))
    mean_y[np.arange(32) // 2, np.arange(32)] = 1.0
    fy = np.zeros((tiles, size_y, 128))
    by = np.zeros((tiles, 48, 128))
    for q in range(tiles):
        fy[q, :, :32] = hy[:, q * 16 : q * 16 + 16] @ mean_y
        for y in range(-2, 34):
            by[q, 8 + y, :size_y] = hy[(q * 16 + y // 2) % size_y]
    out["fy"] = fy
    out["by"] = by
    out["kx"] = np.kron(hartley_np(slabs), np.eye(8))
    lam_x, lam_y, lam_z = eigen_np(slabs, 8.0), eigen_np(size_y, 8.0), eigen_np(16, 8.0)
    inv = np.zeros((tiles, slabs, 8, 2, 4, 16))
    for q in range(tiles):
        ky = lam_y[q * 16 : q * 16 + 16].reshape(2, 8)
        total = (
            SCREEN * SCREEN
            + lam_x[:, None, None, None, None]
            + ky.T[None, :, :, None, None]
            + lam_z[None, None, None, None, :]
        )
        inv[q] = np.broadcast_to(1.0 / total, (slabs, 8, 2, 4, 16))
    out["inv"] = inv.reshape(tiles, slabs * 8, 128)
    return out


class Shift:
    def __init__(self, sign, pieces, relays, send, recv, slot):
        gx, gy = lax.axis_index("gx"), lax.axis_index("gy")
        n = lax.axis_size("gx")
        place = lax.rem(gx, 4) if sign > 0 else 3 - lax.rem(gx, 4)

        def copy(src, dst, at, k):
            return pltpu.make_async_remote_copy(
                src_ref=src, dst_ref=dst, send_sem=send.at[slot + at], recv_sem=recv.at[slot + at],
                device_id=(lax.rem(gx + sign * k + n, n), gy), device_id_type=MESH,
            )

        held = len(pieces)
        count = held + len(relays)
        self.relays = []
        for r, (k, src, dst, hold, least) in enumerate(relays):
            straight = copy(src, dst, held + r, k)
            first = copy(src, hold, count + r, 4)
            second = copy(hold, dst, held + r, k - 4)
            self.relays.append((straight, first, second, place >= least))
        self.whole = [copy(src, dst, p, k) for p, (k, src, dst) in enumerate(pieces)]

    def start(self):
        for straight, first, second, bent in self.relays:
            pl.when(bent)(first.start)
        for c in self.whole:
            c.start()
        for straight, first, second, bent in self.relays:
            pl.when(jnp.logical_not(bent))(straight.start)

    def pass_on(self):
        for straight, first, second, bent in self.relays:

            def onward(first=first, second=second):
                first.wait_recv()
                second.start()

            pl.when(bent)(onward)

    def arrive(self):
        for straight, first, second, bent in self.relays:
            straight.wait_recv()
        for c in self.whole:
            c.wait_recv()

    def settle(self):
        for straight, first, second, bent in self.relays:

            def sent(first=first, second=second):
                first.wait_send()
                second.wait_send()

            pl.when(bent)(sent)
            pl.when(jnp.logical_not(bent))(straight.wait_send)
        for c in self.whole:
            c.wait_send()


def box_anchors(anc_ref, ganc_ref, sources):
    pairs = []
    for s in sources:
        for b in range(2):
            if s < 0:
                pairs.append((anc_ref[0, b], anc_ref[0, 2 + b]))
            else:
                pairs.append((ganc_ref[s, 0, b], ganc_ref[s, 0, 2 + b]))
    return pairs


def select_rows(pairs, axis):
    shape = (160, 320) if axis == 0 else (320, 160)
    row = lax.broadcasted_iota(jnp.int32, shape, axis)
    col = lax.broadcasted_iota(jnp.int32, shape, 1 - axis)
    want = 4 * (col % 8) + (col // 8) % 4
    box = col // 32
    for k, (ay, _) in enumerate(pairs):
        want = want + jnp.where(box == k, ay, 0)
    return jnp.where(row == want, 1.0, 0.0).astype(BF16)


def whole_kernel(
    ax_ref, anc_ref, ancs_ref, occ_ref, vir_ref, mix_ref,
    r0_ref, r1_ref, p1_ref, p0_ref, fz_ref, bz_ref, fy_ref, by_ref, kx_ref, inv_ref,
    out_ref, coup_ref,
    dens, src, got, ganc, sanc, sel, selt, hold1, hold2, f_ref,
    rim, sides, beyond, fp, f1p, f2p, v0, v1p, w1, v2p, w2, tmp, tmp1, qs, qr, gs, gall, us, ur,
    pot, margin, cut, win0, win1, hold3, hold4,
    send, recv, gsend, grecv, local,
):
    gx, gy = lax.axis_index("gx"), lax.axis_index("gy")
    n, m = lax.axis_size("gx"), lax.axis_size("gy")
    east, west = lax.rem(gx + 1, n), lax.rem(gx + n - 1, n)
    north, south = lax.rem(gy + 1, m), lax.rem(gy + m - 1, m)
    wins = (win0, win1)
    used = [0]

    def slots(count):
        used[0] += count
        return used[0] - count

    barrier = pltpu.get_barrier_semaphore()
    for d in range(1, m):
        pl.semaphore_signal(barrier, inc=1, device_id=(gx, lax.rem(gy + d, m)), device_id_type=MESH)
    for x in (east, west):
        for y in (north, south):
            pl.semaphore_signal(barrier, inc=1, device_id=(x, y), device_id_type=MESH)

    def greet(d, carry):
        pl.semaphore_signal(barrier, inc=1, device_id=(lax.rem(gx + d, n), gy), device_id_type=MESH)
        return carry

    lax.fori_loop(1, n, greet, 0)

    def copy(src_ref, dst_ref, x, y):
        slot = slots(1)
        return pltpu.make_async_remote_copy(
            src_ref=src_ref, dst_ref=dst_ref, send_sem=send.at[slot], recv_sem=recv.at[slot],
            device_id=(x, y), device_id_type=MESH,
        )

    unsent = []

    for b in range(2):
        for x in range(8):
            dens[b, x] = jnp.zeros((2, 8, 128), F32)
            dens[b, 40 + x] = jnp.zeros((2, 8, 128), F32)

    def density(p):
        for b in range(2):
            weights = mix_ref[b, p]

            def step(s, carry, b=b, weights=weights):
                rows = pl.ds(pl.multiple_of(s * 16, 16), 16)
                vir = vir_ref[b, :, rows, :].astype(F32)
                occ = occ_ref[b, :, rows, :].astype(F32)
                parts = [vir[:, 8 * h : 8 * h + 8].reshape(64, 128) for h in range(2)]
                mixed = dot(weights, jnp.concatenate(parts, axis=1).astype(BF16))
                mixed = mixed.reshape(8, 2, 8, 256)
                for h in range(2):
                    part = mixed[..., 128 * h : 128 * h + 128]
                    dens[b, 8 + 2 * s + h] = jnp.sum(occ[:, None, 8 * h : 8 * h + 8] * part, axis=0)
                return carry

            lax.fori_loop(0, 16, step, 0)

        def place(x, carry):
            for b in range(2):
                src[p, x, b] = dens[b, x + 8 - ax_ref[b]]
            return carry

        lax.fori_loop(0, 40, place, 0)

    def deposit(p):
        s, g = src.at[p], got.at[p]
        pieces = [
            (4, s.at[pl.ds(31, 8)], g.at[3, pl.ds(0, 8)]),
            (3, s.at[pl.ds(23, 10)], g.at[2]),
            (2, s.at[pl.ds(15, 10), 0], g.at[1, :, 0]),
            (-1, s.at[pl.ds(0, 1)], g.at[4, pl.ds(9, 1)]),
        ]
        relays = [
            (1, s.at[pl.ds(7, 10)], g.at[0], hold1.at[p], 3),
            (2, s.at[pl.ds(15, 10), 1], g.at[1, :, 1], hold2.at[p], 2),
        ]
        return Shift(1, pieces, relays, send, recv, slots(8))

    density(0)
    pl.semaphore_wait(barrier, m - 1 + 4 + n - 1)
    words = [copy(ancs_ref, ganc.at[s], lax.rem(gx + k + n, n), gy) for s, k in enumerate((1, 2, 3, 4, -1))]
    moves = [deposit(0), deposit(1)]
    moves[0].start()
    for c in words:
        c.start()
    density(1)
    moves[1].start()
    moves[0].pass_on()
    for c in words:
        c.wait()
    read = pltpu.make_async_copy(ganc, sanc, local.at[0])
    read.start()
    read.wait()
    usual = box_anchors(anc_ref, sanc, [-1, 0, 1, 2, 3])
    last = box_anchors(anc_ref, sanc, [-1, 0, 1, 2, 4])
    sel[0] = select_rows(usual, 0)
    sel[1] = select_rows(last, 0)
    selt[...] = select_rows(usual, 1)
    lane = lax.broadcasted_iota(jnp.int32, (8, 128), 1)
    blank = jnp.zeros((8, 128), F32)

    def plane(p, e, own, takes, edge):
        pairs = last if edge else usual
        loads = []
        for s in range(5):
            for b in range(2):
                if s == 0:
                    loads.append((lambda t, b=b: src[p, e - 1, b, t]) if own else None)
                elif s == 4 and edge:
                    loads.append(lambda t, b=b: got[p, 4, 9, b, t])
                elif s in takes:
                    loads.append(lambda t, s=s, b=b: got[p, s - 1, e, b, t])
                else:
                    loads.append(None)
        masks = [(lane >= az) & (lane < az + 32) for _, az in pairs]
        columns = []
        for t in range(2):
            rows = []
            for k, load in enumerate(loads):
                if load is None:
                    rows += [blank] * 4
                    continue
                value = load(t)
                for j in range(4):
                    moved = pltpu.roll(value, lax.rem(pairs[k][1] + 128 - 32 * j, 128), 1)
                    rows.append(jnp.where(masks[k], moved, 0.0))
            columns.append(jnp.concatenate(rows, axis=0))
        placed = dot_left(sel[1 if edge else 0], jnp.concatenate(columns, axis=1))
        f_ref[p, e, 0] = placed[:, :128]
        f_ref[p, e, 1] = placed[:, 128:]

    def accumulate(p):
        plane(p, 0, False, (1, 2, 3, 4), False)

        def step(e, carry):
            plane(p, e, True, (1, 2, 3, 4), False)
            return carry

        lax.fori_loop(1, 8, step, 0)
        plane(p, 8, True, (1, 2, 3), False)
        plane(p, 9, True, (1, 2, 3), True)

    def send_rim(p):
        copies = [copy(f_ref.at[p, :, :, pl.ds(128, 32), :], rim.at[p], gx, north)]
        copies[0].start()

        def edge(e, carry):
            for t in range(2):
                sides[p, 0, e, t : t + 1] = f_ref[p, e + 1, t, 127:128]
                sides[p, 1, e, t : t + 1] = f_ref[p, e + 1, t, 0:1]
            return carry

        lax.fori_loop(0, 8, edge, 0)
        copies += [
            copy(sides.at[p, 0], beyond.at[p, 0], gx, north),
            copy(sides.at[p, 1], beyond.at[p, 1], gx, south),
        ]
        for c in copies[1:]:
            c.start()

        def early(e, carry):
            for t in range(2):
                fp[e, 2 * p + t, 40:136] = f_ref[p, e, t, 32:128]
            return carry

        lax.fori_loop(0, 10, early, 0)
        return copies

    def join_rim(p, copies):
        for c in copies:
            c.wait_recv()
        unsent.extend(copies)

        def join(e, carry):
            for t in range(2):
                fp[e, 2 * p + t, 8:40] = f_ref[p, e, t, 0:32] + rim[p, e, t]
            return carry

        def rims(e, carry):
            for t in range(2):
                fp[e, 2 * p + t, 7:8] = beyond[p, 0, e - 1, t : t + 1]
                fp[e, 2 * p + t, 136:137] = f_ref[p, e, t, 128:129] + beyond[p, 1, e - 1, t : t + 1]
            return carry

        lax.fori_loop(1, 9, rims, 0)
        lax.fori_loop(0, 10, join, 0)

    def down0(p):
        scale = DAMPING / center_of(0)

        def step(xc, carry):
            halves = []
            for t in (2 * p, 2 * p + 1):
                total = None
                for x in range(2):
                    e = 2 * xc + 1 + x
                    mid = fp[e, t, 8:136]
                    beside = fp[e, t, 7:135] + fp[e, t, 9:137] + fp[e - 1, t, 8:136] + fp[e + 1, t, 8:136]
                    beside = beside + z_beside(mid, 128)
                    res = (1.0 - DAMPING) * mid + scale * beside
                    total = res if total is None else total + res
                tmp[0:128, :] = total
                halves.append(tmp[pl.ds(0, 64, stride=2), :] + tmp[pl.ds(1, 64, stride=2), :])
            f1p[p, 2 + xc, 8:72] = dot_right(jnp.concatenate(halves, axis=1), r0_ref[...])
            return carry

        lax.fori_loop(0, 4, step, 0)

    def swap(buf, a, c):
        def part(x0, nx, y0, ny):
            return buf.at[pl.ds(x0, nx), pl.ds(y0, ny)]

        near = [
            copy(part(a + 1, 1, 8, c), part(1, 1, 8, c), east, gy),
            copy(part(2, 1, 8, c), part(a + 2, 1, 8, c), west, gy),
            copy(part(2, a, c, 8), part(2, a, 0, 8), gx, north),
            copy(part(2, a, 8, 8), part(2, a, c + 8, 8), gx, south),
        ]
        far = [
            copy(part(a, 1, 8, c), part(0, 1, 8, c), east, gy),
            copy(part(3, 1, 8, c), part(a + 3, 1, 8, c), west, gy),
            copy(part(a, 2, c, 8), part(0, 2, 0, 8), east, north),
            copy(part(a, 2, 8, 8), part(0, 2, c + 8, 8), east, south),
            copy(part(2, 2, c, 8), part(a + 2, 2, 0, 8), west, north),
            copy(part(2, 2, 8, 8), part(a + 2, 2, c + 8, 8), west, south),
        ]
        for one in near + far:
            one.start()
        unsent.extend(near + far)
        return near, far

    moves[0].arrive()
    accumulate(0)
    rims0 = send_rim(0)
    moves[1].pass_on()
    join_rim(0, rims0)
    down0(0)
    near0, far0 = swap(f1p.at[0], 4, 64)
    moves[1].arrive()
    accumulate(1)
    rims1 = send_rim(1)
    join_rim(1, rims1)
    down0(1)
    near1, far1 = swap(f1p.at[1], 4, 64)

    def down1(p, xc):
        scale = DAMPING / center_of(1) / 4.0
        both = None
        for x in range(2):
            e = 2 + 2 * xc + x
            mid = f1p[p, e, 8:72]
            beside = f1p[p, e, 7:71] + f1p[p, e, 9:73] + f1p[p, e - 1, 8:72] + f1p[p, e + 1, 8:72]
            beside = beside + z_beside(mid, 64)
            res = (1.0 - DAMPING) * mid + scale * beside
            both = res if both is None else both + res
        tmp[0:64, :] = both
        pair = tmp[pl.ds(0, 32, stride=2), :] + tmp[pl.ds(1, 32, stride=2), :]
        return dot_right(pair, r1_ref[p])

    for c in near0:
        c.wait_recv()
    held = [down1(0, xc) for xc in range(2)]
    for c in near1:
        c.wait_recv()
    for xc in range(2):
        f2p[2 + xc, 8:40] = held[xc] + down1(1, xc)
    near2, far2 = swap(f2p, 2, 32)
    for c in near2:
        c.wait_recv()

    scale = DAMPING / center_of(2) / 16.0
    total = None
    for x in range(2):
        e = 2 + x
        mid = f2p[e, 8:40]
        beside = f2p[e, 7:39] + f2p[e, 9:41] + f2p[e - 1, 8:40] + f2p[e + 1, 8:40]
        beside = beside + z_beside(mid, 32)
        res = (1.0 - DAMPING) * mid + scale * beside
        total = res if total is None else total + res
    modes = dot_high(total, fz_ref[...])
    modes = jnp.concatenate([modes, jnp.zeros((96, 128), F32)], axis=0)
    modes = dot_high(fy_ref[gy], modes)
    for q in range(m):
        qs[q] = modes[16 * q : 16 * q + 8] + pltpu.roll(modes[16 * q + 8 : 16 * q + 16], 64, 1)
    copies = []
    for d in range(1, m):
        to = lax.rem(gy + d, m)
        copies.append(copy(qs.at[to], qr.at[d - 1], gx, to))
    for c in copies:
        c.start()
    unsent.extend(copies)
    mine = qs[gy]
    for d, c in enumerate(copies):
        c.wait_recv()
        mine = mine + qr[d]
    gs[...] = mine

    def shout(d):
        return pltpu.make_async_remote_copy(
            src_ref=gs, dst_ref=gall.at[gx], send_sem=gsend.at[d], recv_sem=grecv.at[d],
            device_id=(lax.rem(gx + d, n), gy), device_id_type=MESH,
        )

    def begin(d, carry):
        shout(d).start()
        return carry

    def end(d, carry):
        shout(d).wait()
        return carry

    lax.fori_loop(1, n, begin, 0)
    gall[gx] = mine
    lax.fori_loop(1, n, end, 0)
    spectrum = dot_high(kx_ref[...], gall[...].reshape(8 * n, 128)) * inv_ref[gy]
    for s, x in enumerate((west, gx, east)):
        us[s] = dot_high(kx_ref[pl.ds(pl.multiple_of(8 * x, 8), 8), :], spectrum)

    copies = []
    for d in range(1, m):
        to = lax.rem(gy + d, m)
        copies.append(copy(us, ur.at[gy], gx, to))
    for c in copies:
        c.start()
    unsent.extend(copies)
    ur[gy] = us[...]
    for c in copies:
        c.wait_recv()

    for c in far2:
        c.wait_recv()
    scale = DAMPING / center_of(2)
    for s in range(3):
        rows = []
        for q in range(m):
            half = ur[q, s]
            rows += [half, pltpu.roll(half, 64, 1)]
        if m < 8:
            rows.append(jnp.zeros((128 - 16 * m, 128), F32))
        ahead = dot_high(by_ref[gy], jnp.concatenate(rows, axis=0))
        ahead = dot_high(ahead, bz_ref[...])
        for x in range(2):
            v2p[2 * s + x] = scale * f2p[2 * s + x] + ahead
    for e in range(1, 5):
        mid = v2p[e]
        beside = v2p[e - 1] + v2p[e + 1] + pltpu.roll(mid, 1, 0) + pltpu.roll(mid, 47, 0)
        beside = beside + z_beside(mid, 32)
        w2[e - 1] = (1.0 - DAMPING) * mid + scale * f2p[e] + (scale / 16.0) * beside

    def rise1(p):
        scale = DAMPING / center_of(1)
        for e in range(4):
            wide = dot_right(w2[e, 4:44], p1_ref[p])
            tmp[pl.ds(0, 40, stride=2), :] = wide
            tmp[pl.ds(1, 40, stride=2), :] = wide
            for x in range(2):
                v1p[2 * e + x] = scale * f1p[p, 2 * e + x] + tmp[0:80, :]

        def step(e, carry):
            mid = v1p[e]
            beside = v1p[e - 1] + v1p[e + 1] + pltpu.roll(mid, 1, 0) + pltpu.roll(mid, 79, 0)
            beside = beside + z_beside(mid, 64)
            w1[e - 1] = (1.0 - DAMPING) * mid + scale * f1p[p, e] + (scale / 4.0) * beside
            return carry

        lax.fori_loop(1, 7, step, 0)

    def rise0(p):
        scale = DAMPING / center_of(0)

        def widen(i):
            wide = dot_right(w1[i, 4:76], p0_ref[...])
            for t in range(2):
                tmp1[t, pl.ds(0, 72, stride=2), :] = wide[:, 128 * t : 128 * t + 128]
                tmp1[t, pl.ds(1, 72, stride=2), :] = wide[:, 128 * t : 128 * t + 128]

        for i, e in ((0, 0), (5, 9)):
            widen(i)
            for t in range(2):
                v0[e, t] = scale * fp[e, 2 * p + t] + tmp1[t]

        def lift(i, carry):
            widen(i)
            for x in range(2):
                for t in range(2):
                    v0[2 * i - 1 + x, t] = scale * fp[2 * i - 1 + x, 2 * p + t] + tmp1[t]
            return carry

        lax.fori_loop(1, 5, lift, 0)

        def step(e, carry):
            for t in range(2):
                mid = v0[e, t, 8:136]
                beside = v0[e, t, 7:135] + v0[e, t, 9:137] + v0[e - 1, t, 8:136] + v0[e + 1, t, 8:136]
                beside = beside + z_beside(mid, 128)
                pot[2 * p + t, e - 1] = (1.0 - DAMPING) * mid + scale * (fp[e, 2 * p + t, 8:136] + beside)
            return carry

        lax.fori_loop(1, 9, step, 0)

    def send_margin(p):
        pair = pl.ds(2 * p, 2)
        c = copy(pot.at[pair, :, pl.ds(0, 32), :], margin.at[pair], gx, south)
        c.start()
        unsent.append(c)
        keep = pltpu.make_async_copy(pot.at[pair], out_ref.at[pair], local.at[1 + p])
        keep.start()
        return c, keep

    group = lax.broadcasted_iota(jnp.int32, (8, 128), 1) // 32

    def windows(p):
        def step(x, carry):
            columns = [
                jnp.concatenate([pot[2 * p + t, x], margin[2 * p + t, x]], axis=0) for t in range(2)
            ]
            taken = dot_left(selt[...], jnp.concatenate(columns, axis=1))
            for t in range(2):
                for k in range(10):
                    total = None
                    for j in range(4):
                        piece = taken[32 * k + 8 * j : 32 * k + 8 * j + 8, 128 * t : 128 * t + 128]
                        piece = pltpu.roll(piece, lax.rem(128 + 32 * j - usual[k][1], 128), 1)
                        total = piece if total is None else jnp.where(group == j, piece, total)
                    if k < 2:
                        wins[p][x, k, t] = total
                    else:
                        cut[p, k // 2 - 1, x, k % 2, t] = total
            return carry

        lax.fori_loop(0, 8, step, 0)

    def give_back(p):
        c, w = cut.at[p], wins[p]
        pieces = [
            (4, c.at[3], w.at[pl.ds(32, 8)]),
            (3, c.at[2], w.at[pl.ds(24, 8)]),
            (2, c.at[1, :, 0], w.at[pl.ds(16, 8), 0]),
        ]
        relays = [
            (1, c.at[0], w.at[pl.ds(8, 8)], hold3.at[p], 3),
            (2, c.at[1, :, 1], w.at[pl.ds(16, 8), 1], hold4.at[p], 2),
        ]
        return Shift(-1, pieces, relays, send, recv, slots(7))

    def project(p):
        for b in range(2):

            def step(s, total, b=b):
                left, right = [], []
                for h in range(4):
                    rows = pl.ds(pl.multiple_of(s * 64 + 16 * h, 16), 16)
                    occ = occ_ref[b, :, rows, :].astype(F32)
                    vir = vir_ref[b, :, rows, :].astype(F32)
                    for g in range(2):
                        cells = wins[p][ax_ref[b] + s * 8 + 2 * h + g, b]
                        weighted = occ[None, :, 8 * g : 8 * g + 8] * cells[:, None]
                        left.append(weighted.reshape(128, 128).astype(BF16))
                        right.append(vir[:, 8 * g : 8 * g + 8].reshape(64, 128).astype(BF16))
                left, right = jnp.concatenate(left, axis=1), jnp.concatenate(right, axis=1)
                return total + lax.dot_general(
                    left, right, (((1,), (1,)), ((), ())), preferred_element_type=F32
                )

            total = lax.fori_loop(0, 4, step, jnp.zeros((128, 64), F32))
            row = lax.broadcasted_iota(jnp.int32, (128, 64), 0) % 8
            col = lax.broadcasted_iota(jnp.int32, (128, 64), 1) % 8
            total = jnp.where(row == col, total, 0.0)
            total = jnp.sum(total.reshape(16, 8, 64), axis=1)
            col = lax.broadcasted_iota(jnp.int32, (64, 128), 1)
            row = lax.broadcasted_iota(jnp.int32, (64, 128), 0) // 8
            pick = jnp.where(row == col, float(BOX) ** (-1.5), 0.0)
            coup_ref[b, 16 * p : 16 * p + 16] = dot_high(total, pick)

    for c in far0:
        c.wait_recv()
    rise1(0)
    rise0(0)
    edge0, keep0 = send_margin(0)
    for c in far1:
        c.wait_recv()
    rise1(1)
    rise0(1)
    edge1, keep1 = send_margin(1)
    backs = [give_back(0), give_back(1)]
    edge0.wait_recv()
    windows(0)
    backs[0].start()
    edge1.wait_recv()
    windows(1)
    backs[1].start()
    backs[0].pass_on()
    backs[0].arrive()
    backs[1].pass_on()
    project(0)
    backs[1].arrive()
    project(1)
    keep0.wait()
    keep1.wait()
    for c in unsent:
        c.wait_send()
    for c in moves + backs:
        c.settle()


def params(**more):
    return pltpu.CompilerParams(vmem_limit_bytes=40 * 1024 * 1024, **more)


def shaped(shape, dtype=F32):
    return jax.ShapeDtypeStruct(shape, dtype)


def per_device(slabs, tiles, occupied, virtual, trials, anchor_x, anchor_y, anchor_z):
    occ = occupied.reshape(2, 8, 256, 128)
    vir = virtual.reshape(2, 8, 256, 128)
    mix = jnp.einsum("bpsia,mn->bpisman", trials.reshape(2, 2, 2, 8, 8), jnp.eye(8, dtype=BF16))
    mix = mix.reshape(2, 2, 128, 64)
    anchors = jnp.concatenate([anchor_y, anchor_z, jnp.zeros((124,), jnp.int32)])
    anchors = jnp.broadcast_to(anchors[None], (8, 128))
    tab = tables(slabs, tiles)
    exact = [jnp.asarray(tab[k], BF16) for k in ("r0", "r1", "p1", "p0")]
    wide = [jnp.asarray(tab[k], F32) for k in ("fz", "bz", "fy", "by", "kx", "inv")]
    potential, coupling = pl.pallas_call(
        whole_kernel,
        out_shape=(shaped((4, 8, 128, 128)), shaped((2, 32, 128))),
        in_specs=[SMEM, SMEM] + [VMEM] * 14,
        out_specs=(ANY, VMEM),
        scratch_shapes=[
            pltpu.VMEM((2, 48, 2, 8, 128), F32),
            pltpu.VMEM((2, 40, 2, 2, 8, 128), F32),
            pltpu.VMEM((2, 5, 10, 2, 2, 8, 128), F32),
            pltpu.VMEM((5, 8, 128), jnp.int32),
            pltpu.SMEM((5, 8, 128), jnp.int32),
            pltpu.VMEM((2, 160, 320), BF16),
            pltpu.VMEM((320, 160), BF16),
            pltpu.VMEM((2, 10, 2, 2, 8, 128), F32),
            pltpu.VMEM((2, 10, 2, 8, 128), F32),
            pltpu.VMEM((2, 10, 2, 160, 128), F32),
            pltpu.VMEM((2, 10, 2, 32, 128), F32),
            pltpu.VMEM((2, 2, 8, 8, 128), F32),
            pltpu.VMEM((2, 2, 8, 8, 128), F32),
            pltpu.VMEM((10, 4, 144, 128), F32),
            pltpu.VMEM((2, 8, 80, 128), F32),
            pltpu.VMEM((6, 48, 128), F32),
            pltpu.VMEM((10, 2, 144, 128), F32),
            pltpu.VMEM((8, 80, 128), F32),
            pltpu.VMEM((6, 80, 128), F32),
            pltpu.VMEM((6, 48, 128), F32),
            pltpu.VMEM((4, 48, 128), F32),
            pltpu.VMEM((144, 128), F32),
            pltpu.VMEM((2, 144, 128), F32),
            pltpu.VMEM((tiles, 8, 128), F32),
            pltpu.VMEM((tiles, 8, 128), F32),
            pltpu.VMEM((8, 128), F32),
            pltpu.VMEM((slabs, 8, 128), F32),
            pltpu.VMEM((3, 8, 128), F32),
            pltpu.VMEM((tiles, 3, 8, 128), F32),
            pltpu.VMEM((4, 8, 128, 128), F32),
            pltpu.VMEM((4, 8, 32, 128), F32),
            pltpu.VMEM((2, 4, 8, 2, 2, 8, 128), F32),
            pltpu.VMEM((40, 2, 2, 8, 128), F32),
            pltpu.VMEM((40, 2, 2, 8, 128), F32),
            pltpu.VMEM((2, 8, 2, 2, 8, 128), F32),
            pltpu.VMEM((2, 8, 2, 8, 128), F32),
            pltpu.SemaphoreType.DMA((96,)),
            pltpu.SemaphoreType.DMA((96,)),
            pltpu.SemaphoreType.DMA((slabs,)),
            pltpu.SemaphoreType.DMA((slabs,)),
            pltpu.SemaphoreType.DMA((3,)),
        ],
        compiler_params=params(collective_id=0, has_side_effects=True),
        name="whole",
    )(anchor_x, anchors, anchors, occ, vir, mix, *exact, *wide)
    return potential, coupling[:, :, :8].reshape(2, 4, 8, 8)


def solution(mesh):
    placed = (
        P(("gx", "gy"), None, None),
        P(("gx", "gy"), None, None),
        P(("gx", "gy"), None, None, None),
        P(("gx", "gy")),
        P(("gx", "gy")),
        P(("gx", "gy")),
    )
    return jax.shard_map(
        functools.partial(per_device, mesh.shape["gx"], mesh.shape["gy"]),
        mesh=mesh,
        in_specs=placed,
        out_specs=(P(None, "gx", "gy", None), P(("gx", "gy"), None, None, None)),
        check_vma=False,
    )
```

```python
import functools

import jax
import jax.numpy as jnp
import numpy as np
from jax import lax
from jax.experimental import pallas as pl
from jax.experimental.pallas import tpu as pltpu
from jax.sharding import PartitionSpec as P

BOX = 32
TRIALS = 4
CX = 8
CY = 128
NZ = 128
SCREEN = 0.05
DAMPING = 2.0 / 3.0
MESH = pl.DeviceIdType.MESH
F32 = jnp.float32
BF16 = jnp.bfloat16
HIGH = lax.Precision.HIGHEST
VMEM = pl.BlockSpec(memory_space=pltpu.VMEM)
SMEM = pl.BlockSpec(memory_space=pltpu.SMEM)
ANY = pl.BlockSpec(memory_space=pl.ANY)


def center_of(level):
    spacing = 2.0**level
    return 6.0 / spacing**2 + SCREEN**2


def split2(x):
    hi = x.astype(BF16)
    lo = (x - hi.astype(F32)).astype(BF16)
    return hi, lo


def dot(a, b):
    return jnp.dot(a, b, preferred_element_type=F32)


def dot_right(x, w):
    hi, lo = split2(x)
    return dot(hi, w) + dot(lo, w)


def dot_left(w, x):
    hi, lo = split2(x)
    return dot(w, hi) + dot(w, lo)


def dot_high(a, b):
    return jnp.dot(a, b, preferred_element_type=F32, precision=HIGH)


def z_beside(x, n):
    if n == 128:
        return pltpu.roll(x, 1, 1) + pltpu.roll(x, 127, 1)
    lane = lax.broadcasted_iota(jnp.int32, x.shape, 1) % n
    below = jnp.where(lane == 0, pltpu.roll(x, 129 - n, 1), pltpu.roll(x, 1, 1))
    above = jnp.where(lane == n - 1, pltpu.roll(x, n - 1, 1), pltpu.roll(x, 127, 1))
    return below + above


def hartley_np(count):
    index = np.arange(count)
    angle = 2.0 * np.pi / count * ((index[:, None] * index[None, :]) % count)
    return (np.cos(angle) + np.sin(angle)) / np.sqrt(count)


def eigen_np(count, spacing):
    return (2.0 - 2.0 * np.cos(2.0 * np.pi / count * np.arange(count))) / (spacing * spacing)


@functools.lru_cache(None)
def tables(slabs, tiles):
    out = {}
    r0 = np.zeros((2, 128, 2, 64))
    r1 = np.zeros((2, 2, 64, 4, 32))
    p1 = np.zeros((2, 4, 32, 2, 64))
    p0 = np.zeros((2, 64, 2, 128))
    for t in range(2):
        for z in range(128):
            r0[t, z, t, z // 2] = 0.125
            p0[t, z // 2, t, z] = 1.0
        for z in range(64):
            for p in range(2):
                r1[p, t, z, 2 * p + t, z // 2] = 0.125
                p1[p, 2 * p + t, z // 2, t, z] = 1.0
    out["r0"] = r0.reshape(256, 128)
    out["r1"] = r1.reshape(2, 128, 128)
    out["p1"] = p1.reshape(2, 128, 128)
    out["p0"] = p0.reshape(128, 256)
    hz = hartley_np(16)
    mean_z = np.zeros((32, 16))
    mean_z[np.arange(32), np.arange(32) // 2] = 1.0
    fz = np.zeros((4, 32, 128))
    bz = np.zeros((128, 4, 32))
    for t in range(4):
        fz[t, :, t * 16 : t * 16 + 16] = 0.125 * mean_z @ hz
        bz[t * 16 : t * 16 + 16, t, :] = hz @ mean_z.T
    out["fz"] = fz.reshape(128, 128)
    out["bz"] = bz.reshape(128, 128)
    size_y = 16 * tiles
    hy = hartley_np(size_y)
    mean_y = np.zeros((16, 32))
    mean_y[np.arange(32) // 2, np.arange(32)] = 1.0
    fy = np.zeros((tiles, size_y, 128))
    by = np.zeros((tiles, 48, 128))
    for q in range(tiles):
        fy[q, :, :32] = hy[:, q * 16 : q * 16 + 16] @ mean_y
        for y in range(-2, 34):
            by[q, 8 + y, :size_y] = hy[(q * 16 + y // 2) % size_y]
    out["fy"] = fy
    out["by"] = by
    out["kx"] = np.kron(hartley_np(slabs), np.eye(8))
    lam_x, lam_y, lam_z = eigen_np(slabs, 8.0), eigen_np(size_y, 8.0), eigen_np(16, 8.0)
    inv = np.zeros((tiles, slabs, 8, 2, 4, 16))
    for q in range(tiles):
        ky = lam_y[q * 16 : q * 16 + 16].reshape(2, 8)
        total = (
            SCREEN * SCREEN
            + lam_x[:, None, None, None, None]
            + ky.T[None, :, :, None, None]
            + lam_z[None, None, None, None, :]
        )
        inv[q] = np.broadcast_to(1.0 / total, (slabs, 8, 2, 4, 16))
    out["inv"] = inv.reshape(tiles, slabs * 8, 128)
    return out


class Shift:
    def __init__(self, sign, pieces, relays, send, recv, slot):
        gx, gy = lax.axis_index("gx"), lax.axis_index("gy")
        n = lax.axis_size("gx")
        place = lax.rem(gx, 4) if sign > 0 else 3 - lax.rem(gx, 4)

        def copy(src, dst, at, k):
            return pltpu.make_async_remote_copy(
                src_ref=src, dst_ref=dst, send_sem=send.at[slot + at], recv_sem=recv.at[slot + at],
                device_id=(lax.rem(gx + sign * k + n, n), gy), device_id_type=MESH,
            )

        held = len(pieces)
        count = held + len(relays)
        self.relays = []
        for r, (k, src, dst, hold, least) in enumerate(relays):
            straight = copy(src, dst, held + r, k)
            first = copy(src, hold, count + r, 4)
            second = copy(hold, dst, held + r, k - 4)
            self.relays.append((straight, first, second, place >= least))
        self.whole = [copy(src, dst, p, k) for p, (k, src, dst) in enumerate(pieces)]

    def start(self):
        for straight, first, second, bent in self.relays:
            pl.when(bent)(first.start)
        for c in self.whole:
            c.start()
        for straight, first, second, bent in self.relays:
            pl.when(jnp.logical_not(bent))(straight.start)

    def pass_on(self):
        for straight, first, second, bent in self.relays:

            def onward(first=first, second=second):
                first.wait_recv()
                second.start()

            pl.when(bent)(onward)

    def arrive(self):
        for straight, first, second, bent in self.relays:
            straight.wait_recv()
        for c in self.whole:
            c.wait_recv()

    def settle(self):
        for straight, first, second, bent in self.relays:

            def sent(first=first, second=second):
                first.wait_send()
                second.wait_send()

            pl.when(bent)(sent)
            pl.when(jnp.logical_not(bent))(straight.wait_send)
        for c in self.whole:
            c.wait_send()


def box_anchors(ay_ref, az_ref, ganc_ref, sources):
    pairs = []
    for s in sources:
        for b in range(2):
            if s < 0:
                pairs.append((ay_ref[b], az_ref[b]))
            else:
                pairs.append((ganc_ref[s, 0, b], ganc_ref[s, 0, 2 + b]))
    return pairs


def select_rows(pairs, axis):
    shape = (160, 320) if axis == 0 else (320, 160)
    row = lax.broadcasted_iota(jnp.int32, shape, axis)
    col = lax.broadcasted_iota(jnp.int32, shape, 1 - axis)
    want = 4 * (col % 8) + (col // 8) % 4
    box = col // 32
    for k, (ay, _) in enumerate(pairs):
        want = want + jnp.where(box == k, ay, 0)
    return jnp.where(row == want, 1.0, 0.0).astype(BF16)


def halve(x):
    return lax.div(x, 2)


def one_hot(hit):
    return jnp.where(hit, 1.0, 0.0)


def select_coarse(pairs):
    row = lax.broadcasted_iota(jnp.int32, (320, 96), 0)
    col = lax.broadcasted_iota(jnp.int32, (320, 96), 1)
    want = row % 32 + 7
    for k, (ay, _) in enumerate(pairs):
        want = want + jnp.where(row // 32 == k, halve(ay + 1), 0)
    return one_hot(col == want).astype(BF16)


def select_coarse_z(az):
    row = lax.broadcasted_iota(jnp.int32, (256, 128), 0)
    col = lax.broadcasted_iota(jnp.int32, (256, 128), 1)
    want = (halve(az + 1) + 63 + col % 32) % 64
    return one_hot((row // 64 == col // 32) & (row % 64 == want)).astype(BF16)


def widen_rows(ay):
    row = lax.broadcasted_iota(jnp.int32, (64, 32), 0)
    col = lax.broadcasted_iota(jnp.int32, (64, 32), 1)
    cell = 4 * (row % 8) + (row // 8) % 4 + ay
    first = halve(ay + 1) - 1
    at = [jnp.right_shift(cell + d, 1) - first for d in (0, -1, 1)]
    beside = one_hot(col == at[1]) + one_hot(col == at[2])
    return jnp.where(row < 32, one_hot(col == at[0]), beside).astype(BF16)


def widen_lanes(az, j):
    row = lax.broadcasted_iota(jnp.int32, (128, 512), 0)
    col = lax.broadcasted_iota(jnp.int32, (128, 512), 1)
    cell = col % 32 + az
    first = halve(az + 1) - 1
    same = (row // 32 == col // 128) & ((col // 32) % 4 == j)
    at = [jnp.right_shift(cell + d, 1) - first for d in (0, -1, 1)]
    hits = [one_hot(same & (row % 32 == a)) for a in at]
    return hits[0].astype(BF16), (hits[1] + hits[2]).astype(BF16)


def mixing(pair_of_trials, p):
    row = lax.broadcasted_iota(jnp.int32, (128, 32), 0)
    col = lax.broadcasted_iota(jnp.int32, (128, 32), 1)
    rows = one_hot(col == (2 * p + (row // 8) % 2) * 8 + row // 16).astype(BF16)
    taken = dot(rows, pair_of_trials).astype(BF16)
    row = lax.broadcasted_iota(jnp.int32, (8, 64), 0)
    col = lax.broadcasted_iota(jnp.int32, (8, 64), 1)
    spread = dot(taken, one_hot(row == col // 8).astype(BF16))
    row = lax.broadcasted_iota(jnp.int32, (128, 64), 0)
    col = lax.broadcasted_iota(jnp.int32, (128, 64), 1)
    return jnp.where(row % 8 == col % 8, spread, 0.0).astype(BF16)


def whole_kernel(
    ax_ref, ay_ref, az_ref, occ_ref, vir_ref, trial_ref,
    r0_ref, r1_ref, p1_ref, p0_ref, fz_ref, bz_ref, fy_ref, by_ref, kx_ref, inv_ref,
    out_ref, coup_ref,
    dens, src, got, ganc, sanc, sel, selt, hold1, hold2, f_ref,
    rim, sides, beyond, fp, f1p, f2p, v0, v1p, w1, v2p, w2, tmp, qs, qr, gs, gall, us, ur,
    pot, margin, cut, win0, win1, hold3, hold4,
    word, mar1, selc, selz, taken, cut1, cwin, hold5, hold6, lc1, lc2, zp, zs, ub, vb,
    send, recv, gsend, grecv, local,
):
    gx, gy = lax.axis_index("gx"), lax.axis_index("gy")
    n, m = lax.axis_size("gx"), lax.axis_size("gy")
    east, west = lax.rem(gx + 1, n), lax.rem(gx + n - 1, n)
    north, south = lax.rem(gy + 1, m), lax.rem(gy + m - 1, m)
    wins = (win0, win1)
    used = [0]

    def slots(count):
        used[0] += count
        return used[0] - count

    barrier = pltpu.get_barrier_semaphore()
    for d in range(1, m):
        pl.semaphore_signal(barrier, inc=1, device_id=(gx, lax.rem(gy + d, m)), device_id_type=MESH)
    for x in (east, west):
        for y in (north, south):
            pl.semaphore_signal(barrier, inc=1, device_id=(x, y), device_id_type=MESH)

    def greet(d, carry):
        pl.semaphore_signal(barrier, inc=1, device_id=(lax.rem(gx + d, n), gy), device_id_type=MESH)
        return carry

    lax.fori_loop(1, n, greet, 0)

    def copy(src_ref, dst_ref, x, y):
        slot = slots(1)
        return pltpu.make_async_remote_copy(
            src_ref=src_ref, dst_ref=dst_ref, send_sem=send.at[slot], recv_sem=recv.at[slot],
            device_id=(x, y), device_id_type=MESH,
        )

    unsent = []

    for b in range(2):
        for x in range(8):
            dens[b, x] = jnp.zeros((2, 8, 128), F32)
            dens[b, 40 + x] = jnp.zeros((2, 8, 128), F32)

    def density(p):
        for b in range(2):
            weights = mixing(trial_ref[b], p)

            def step(s, carry, b=b, weights=weights):
                rows = pl.ds(pl.multiple_of(s * 16, 16), 16)
                vir = vir_ref[b, :, rows, :].astype(F32)
                occ = occ_ref[b, :, rows, :].astype(F32)
                parts = [vir[:, 8 * h : 8 * h + 8].reshape(64, 128) for h in range(2)]
                mixed = dot(weights, jnp.concatenate(parts, axis=1).astype(BF16))
                mixed = mixed.reshape(8, 2, 8, 256)
                for h in range(2):
                    part = mixed[..., 128 * h : 128 * h + 128]
                    dens[b, 8 + 2 * s + h] = jnp.sum(occ[:, None, 8 * h : 8 * h + 8] * part, axis=0)
                return carry

            lax.fori_loop(0, 16, step, 0)

        def place(x, carry):
            for b in range(2):
                src[p, x, b] = dens[b, x + 8 - ax_ref[b]]
            return carry

        lax.fori_loop(0, 40, place, 0)

    def deposit(p):
        s, g = src.at[p], got.at[p]
        pieces = [
            (4, s.at[pl.ds(31, 8)], g.at[3, pl.ds(0, 8)]),
            (3, s.at[pl.ds(23, 10)], g.at[2]),
            (2, s.at[pl.ds(15, 10), 0], g.at[1, :, 0]),
            (-1, s.at[pl.ds(0, 1)], g.at[4, pl.ds(9, 1)]),
        ]
        relays = [
            (1, s.at[pl.ds(7, 10)], g.at[0], hold1.at[p], 3),
            (2, s.at[pl.ds(15, 10), 1], g.at[1, :, 1], hold2.at[p], 2),
        ]
        return Shift(1, pieces, relays, send, recv, slots(8))

    density(0)
    pl.semaphore_wait(barrier, m - 1 + 4 + n - 1)
    lane = lax.broadcasted_iota(jnp.int32, (8, 128), 1)
    value = jnp.zeros((8, 128), jnp.int32)
    for k, anchor in enumerate((ay_ref[0], ay_ref[1], az_ref[0], az_ref[1])):
        value = jnp.where(lane == k, anchor, value)
    word[...] = value
    words = [copy(word, ganc.at[s], lax.rem(gx + k + n, n), gy) for s, k in enumerate((1, 2, 3, 4, -1))]
    moves = [deposit(0), deposit(1)]
    moves[0].start()
    for c in words:
        c.start()
    density(1)
    moves[1].start()
    moves[0].pass_on()
    for c in words:
        c.wait()
    read = pltpu.make_async_copy(ganc, sanc, local.at[0])
    read.start()
    read.wait()
    usual = box_anchors(ay_ref, az_ref, sanc, [-1, 0, 1, 2, 3])
    last = box_anchors(ay_ref, az_ref, sanc, [-1, 0, 1, 2, 4])
    sel[0] = select_rows(usual, 0)
    sel[1] = select_rows(last, 0)
    selt[...] = select_rows(usual, 1)
    blank = jnp.zeros((8, 128), F32)

    def plane(p, e, own, takes, edge):
        pairs = last if edge else usual
        loads = []
        for s in range(5):
            for b in range(2):
                if s == 0:
                    loads.append((lambda t, b=b: src[p, e - 1, b, t]) if own else None)
                elif s == 4 and edge:
                    loads.append(lambda t, b=b: got[p, 4, 9, b, t])
                elif s in takes:
                    loads.append(lambda t, s=s, b=b: got[p, s - 1, e, b, t])
                else:
                    loads.append(None)
        masks = [(lane >= az) & (lane < az + 32) for _, az in pairs]
        columns = []
        for t in range(2):
            rows = []
            for k, load in enumerate(loads):
                if load is None:
                    rows += [blank] * 4
                    continue
                value = load(t)
                for j in range(4):
                    moved = pltpu.roll(value, lax.rem(pairs[k][1] + 128 - 32 * j, 128), 1)
                    rows.append(jnp.where(masks[k], moved, 0.0))
            columns.append(jnp.concatenate(rows, axis=0))
        placed = dot_left(sel[1 if edge else 0], jnp.concatenate(columns, axis=1))
        f_ref[p, e, 0] = placed[:, :128]
        f_ref[p, e, 1] = placed[:, 128:]

    def accumulate(p):
        plane(p, 0, False, (1, 2, 3, 4), False)

        def step(e, carry):
            plane(p, e, True, (1, 2, 3, 4), False)
            return carry

        lax.fori_loop(1, 8, step, 0)
        plane(p, 8, True, (1, 2, 3), False)
        plane(p, 9, True, (1, 2, 3), True)

    def send_rim(p):
        copies = [copy(f_ref.at[p, :, :, pl.ds(128, 32), :], rim.at[p], gx, north)]
        copies[0].start()

        def edge(e, carry):
            for t in range(2):
                sides[p, 0, e, t : t + 1] = f_ref[p, e + 1, t, 127:128]
                sides[p, 1, e, t : t + 1] = f_ref[p, e + 1, t, 0:1]
            return carry

        lax.fori_loop(0, 8, edge, 0)
        copies += [
            copy(sides.at[p, 0], beyond.at[p, 0], gx, north),
            copy(sides.at[p, 1], beyond.at[p, 1], gx, south),
        ]
        for c in copies[1:]:
            c.start()

        def early(e, carry):
            for t in range(2):
                fp[e, 2 * p + t, 40:136] = f_ref[p, e, t, 32:128]
            return carry

        lax.fori_loop(0, 10, early, 0)
        return copies

    def join_rim(p, copies):
        for c in copies:
            c.wait_recv()
        unsent.extend(copies)

        def join(e, carry):
            for t in range(2):
                fp[e, 2 * p + t, 8:40] = f_ref[p, e, t, 0:32] + rim[p, e, t]
            return carry

        def rims(e, carry):
            for t in range(2):
                fp[e, 2 * p + t, 7:8] = beyond[p, 0, e - 1, t : t + 1]
                fp[e, 2 * p + t, 136:137] = f_ref[p, e, t, 128:129] + beyond[p, 1, e - 1, t : t + 1]
            return carry

        lax.fori_loop(1, 9, rims, 0)
        lax.fori_loop(0, 10, join, 0)

    def down0(p):
        scale = DAMPING / center_of(0)

        def step(xc, carry):
            halves = []
            for t in (2 * p, 2 * p + 1):
                total = None
                for x in range(2):
                    e = 2 * xc + 1 + x
                    mid = fp[e, t, 8:136]
                    beside = fp[e, t, 7:135] + fp[e, t, 9:137] + fp[e - 1, t, 8:136] + fp[e + 1, t, 8:136]
                    beside = beside + z_beside(mid, 128)
                    res = (1.0 - DAMPING) * mid + scale * beside
                    pot[t, e - 1] = scale * (mid + res)
                    total = res if total is None else total + res
                tmp[0:128, :] = total
                halves.append(tmp[pl.ds(0, 64, stride=2), :] + tmp[pl.ds(1, 64, stride=2), :])
            f1p[p, 2 + xc, 8:72] = dot_right(jnp.concatenate(halves, axis=1), r0_ref[...])
            return carry

        lax.fori_loop(0, 4, step, 0)

    def swap(buf, a, c):
        def part(x0, nx, y0, ny):
            return buf.at[pl.ds(x0, nx), pl.ds(y0, ny)]

        near = [
            copy(part(a + 1, 1, 8, c), part(1, 1, 8, c), east, gy),
            copy(part(2, 1, 8, c), part(a + 2, 1, 8, c), west, gy),
            copy(part(2, a, c, 8), part(2, a, 0, 8), gx, north),
            copy(part(2, a, 8, 8), part(2, a, c + 8, 8), gx, south),
        ]
        far = [
            copy(part(a, 1, 8, c), part(0, 1, 8, c), east, gy),
            copy(part(3, 1, 8, c), part(a + 3, 1, 8, c), west, gy),
            copy(part(a, 2, c, 8), part(0, 2, 0, 8), east, north),
            copy(part(a, 2, 8, 8), part(0, 2, c + 8, 8), east, south),
            copy(part(2, 2, c, 8), part(a + 2, 2, 0, 8), west, north),
            copy(part(2, 2, 8, 8), part(a + 2, 2, c + 8, 8), west, south),
        ]
        for one in near + far:
            one.start()
        unsent.extend(near + far)
        return near, far

    def send_margin(p):
        pair = pl.ds(2 * p, 2)
        c = copy(pot.at[pair, :, pl.ds(0, 32), :], margin.at[pair], gx, south)
        c.start()
        return c

    group = lax.broadcasted_iota(jnp.int32, (8, 128), 1) // 32

    def windows(p):
        def step(x, carry):
            columns = [
                jnp.concatenate([pot[2 * p + t, x], margin[2 * p + t, x]], axis=0) for t in range(2)
            ]
            taken = dot_left(selt[...], jnp.concatenate(columns, axis=1))
            for t in range(2):
                for k in range(10):
                    total = None
                    for j in range(4):
                        piece = taken[32 * k + 8 * j : 32 * k + 8 * j + 8, 128 * t : 128 * t + 128]
                        piece = pltpu.roll(piece, lax.rem(128 + 32 * j - usual[k][1], 128), 1)
                        total = piece if total is None else jnp.where(group == j, piece, total)
                    if k < 2:
                        wins[p][x, k, t] = total
                    else:
                        cut[p, k // 2 - 1, x, k % 2, t] = total
            return carry

        lax.fori_loop(0, 8, step, 0)

    def give_back(p):
        c, w = cut.at[p], wins[p]
        pieces = [
            (4, c.at[3], w.at[pl.ds(32, 8)]),
            (3, c.at[2], w.at[pl.ds(24, 8)]),
            (2, c.at[1, :, 0], w.at[pl.ds(16, 8), 0]),
        ]
        relays = [
            (1, c.at[0], w.at[pl.ds(8, 8)], hold3.at[p], 3),
            (2, c.at[1, :, 1], w.at[pl.ds(16, 8), 1], hold4.at[p], 2),
        ]
        return Shift(-1, pieces, relays, send, recv, slots(7))

    moves[0].arrive()
    accumulate(0)
    rims0 = send_rim(0)
    moves[1].pass_on()
    join_rim(0, rims0)
    down0(0)
    near0, far0 = swap(f1p.at[0], 4, 64)
    edge0 = send_margin(0)
    moves[1].arrive()
    accumulate(1)
    rims1 = send_rim(1)
    backs = [give_back(0), give_back(1)]
    edge0.wait_recv()
    windows(0)
    join_rim(1, rims1)
    down0(1)
    near1, far1 = swap(f1p.at[1], 4, 64)
    edge1 = send_margin(1)
    backs[0].start()
    selc[...] = select_coarse(usual)

    def down1(p, xc):
        scale = DAMPING / center_of(1) / 4.0
        both = None
        for x in range(2):
            e = 2 + 2 * xc + x
            mid = f1p[p, e, 8:72]
            beside = f1p[p, e, 7:71] + f1p[p, e, 9:73] + f1p[p, e - 1, 8:72] + f1p[p, e + 1, 8:72]
            beside = beside + z_beside(mid, 64)
            res = (1.0 - DAMPING) * mid + scale * beside
            both = res if both is None else both + res
        tmp[0:64, :] = both
        pair = tmp[pl.ds(0, 32, stride=2), :] + tmp[pl.ds(1, 32, stride=2), :]
        return dot_right(pair, r1_ref[p])

    for c in near0:
        c.wait_recv()
    held = [down1(0, xc) for xc in range(2)]
    for c in near1:
        c.wait_recv()
    for xc in range(2):
        f2p[2 + xc, 8:40] = held[xc] + down1(1, xc)
    near2, far2 = swap(f2p, 2, 32)
    edge1.wait_recv()
    windows(1)
    backs[1].start()
    for c in near2:
        c.wait_recv()

    scale = DAMPING / center_of(2) / 16.0
    total = None
    for x in range(2):
        e = 2 + x
        mid = f2p[e, 8:40]
        beside = f2p[e, 7:39] + f2p[e, 9:41] + f2p[e - 1, 8:40] + f2p[e + 1, 8:40]
        beside = beside + z_beside(mid, 32)
        res = (1.0 - DAMPING) * mid + scale * beside
        total = res if total is None else total + res
    modes = dot_high(total, fz_ref[...])
    modes = jnp.concatenate([modes, jnp.zeros((96, 128), F32)], axis=0)
    modes = dot_high(fy_ref[gy], modes)
    for q in range(m):
        qs[q] = modes[16 * q : 16 * q + 8] + pltpu.roll(modes[16 * q + 8 : 16 * q + 16], 64, 1)
    copies = []
    for d in range(1, m):
        to = lax.rem(gy + d, m)
        copies.append(copy(qs.at[to], qr.at[d - 1], gx, to))
    for c in copies:
        c.start()
    unsent.extend(copies)
    for k in range(10):
        selz[k] = select_coarse_z(usual[k][1])
    mine = qs[gy]
    for d, c in enumerate(copies):
        c.wait_recv()
        mine = mine + qr[d]
    gs[...] = mine

    def shout(d):
        return pltpu.make_async_remote_copy(
            src_ref=gs, dst_ref=gall.at[gx], send_sem=gsend.at[d], recv_sem=grecv.at[d],
            device_id=(lax.rem(gx + d, n), gy), device_id_type=MESH,
        )

    def begin(d, carry):
        shout(d).start()
        return carry

    def end(d, carry):
        shout(d).wait()
        return carry

    lax.fori_loop(1, n, begin, 0)
    gall[gx] = mine
    for b in range(2):
        for j in range(4):
            zp[b, 128 * j : 128 * j + 128], zs[b, 128 * j : 128 * j + 128] = widen_lanes(az_ref[b], j)
    lax.fori_loop(1, n, end, 0)
    spectrum = dot_high(kx_ref[...], gall[...].reshape(8 * n, 128)) * inv_ref[gy]
    for s, x in enumerate((west, gx, east)):
        us[s] = dot_high(kx_ref[pl.ds(pl.multiple_of(8 * x, 8), 8), :], spectrum)

    copies = []
    for d in range(1, m):
        to = lax.rem(gy + d, m)
        copies.append(copy(us, ur.at[gy], gx, to))
    for c in copies:
        c.start()
    unsent.extend(copies)
    ur[gy] = us[...]
    backs[0].pass_on()
    for c in copies:
        c.wait_recv()

    for c in far2:
        c.wait_recv()
    scale = DAMPING / center_of(2)
    for s in range(3):
        rows = []
        for q in range(m):
            half = ur[q, s]
            rows += [half, pltpu.roll(half, 64, 1)]
        if m < 8:
            rows.append(jnp.zeros((128 - 16 * m, 128), F32))
        ahead = dot_high(by_ref[gy], jnp.concatenate(rows, axis=0))
        ahead = dot_high(ahead, bz_ref[...])
        for x in range(2):
            v2p[2 * s + x] = scale * f2p[2 * s + x] + ahead
    for e in range(1, 5):
        mid = v2p[e]
        beside = v2p[e - 1] + v2p[e + 1] + pltpu.roll(mid, 1, 0) + pltpu.roll(mid, 47, 0)
        beside = beside + z_beside(mid, 32)
        w2[e - 1] = (1.0 - DAMPING) * mid + scale * f2p[e] + (scale / 16.0) * beside

    def rise1(p):
        scale = DAMPING / center_of(1)
        for e in range(4):
            wide = dot_right(w2[e, 4:44], p1_ref[p])
            tmp[pl.ds(0, 40, stride=2), :] = wide
            tmp[pl.ds(1, 40, stride=2), :] = wide
            for x in range(2):
                v1p[2 * e + x] = scale * f1p[p, 2 * e + x] + tmp[0:80, :]

        def step(e, carry):
            mid = v1p[e]
            beside = v1p[e - 1] + v1p[e + 1] + pltpu.roll(mid, 1, 0) + pltpu.roll(mid, 79, 0)
            beside = beside + z_beside(mid, 64)
            w1[p, e - 1] = (1.0 - DAMPING) * mid + scale * f1p[p, e] + (scale / 4.0) * beside
            return carry

        lax.fori_loop(1, 7, step, 0)

    def rise0(p):
        scale = DAMPING / center_of(0)

        def widen(i, planes):
            wide = dot_right(w1[p, i, 4:76], p0_ref[...])
            for t in range(2):
                value = wide[:, 128 * t : 128 * t + 128]
                for e in planes:
                    v0[e, t, pl.ds(0, 72, stride=2), :] = value
                    v0[e, t, pl.ds(1, 72, stride=2), :] = value

        widen(0, (0,))

        def lift(i, carry):
            widen(i, (2 * i - 1, 2 * i))
            return carry

        lax.fori_loop(1, 5, lift, 0)
        widen(5, (9,))

        def step(e, carry):
            for t in range(2):
                mid = v0[e, t, 8:136]
                beside = v0[e, t, 7:135] + v0[e, t, 9:137] + v0[e - 1, t, 8:136] + v0[e + 1, t, 8:136]
                beside = beside + z_beside(mid, 128)
                pot[2 * p + t, e - 1] = pot[2 * p + t, e - 1] + (1.0 - DAMPING) * mid + scale * beside
            return carry

        lax.fori_loop(1, 9, step, 0)
        pair = pl.ds(2 * p, 2)
        keep = pltpu.make_async_copy(pot.at[pair], out_ref.at[pair], local.at[1 + p])
        keep.start()
        return keep

    def windows1():
        for i in range(5):
            columns = [jnp.concatenate([w1[p, i, 0:72], mar1[p, i]], axis=0) for p in range(2)]
            hi, lo = split2(jnp.concatenate(columns, axis=1))
            taken[2 * i] = dot(selc[...], hi).astype(BF16)
            taken[2 * i + 1] = dot(selc[...], lo).astype(BF16)
        for k in range(10):
            rows = jnp.concatenate([taken[i, 32 * k : 32 * k + 32] for i in range(10)], axis=0)
            rows = dot(rows, selz[k])
            for i in range(5):
                part = rows[64 * i : 64 * i + 24] + rows[64 * i + 32 : 64 * i + 56]
                if k < 2:
                    cwin[i, k] = part
                elif i > 0:
                    cut1[k // 2 - 1, i - 1, k % 2] = part

    def give_back1():
        pieces = [
            (4, cut1.at[3], cwin.at[pl.ds(17, 4)]),
            (3, cut1.at[2], cwin.at[pl.ds(13, 4)]),
            (2, cut1.at[1, :, 0], cwin.at[pl.ds(9, 4), 0]),
        ]
        relays = [
            (1, cut1.at[0], cwin.at[pl.ds(5, 4)], hold5, 3),
            (2, cut1.at[1, :, 1], cwin.at[pl.ds(9, 4), 1], hold6, 2),
        ]
        return Shift(-1, pieces, relays, send, recv, slots(7))

    def expand(b):
        rows = widen_rows(ay_ref[b])
        blank = jnp.zeros((8, 128), F32)
        for g in range(11):
            planes = [x for x in (2 * g, 2 * g + 1) if x < 21]
            columns = [jnp.concatenate([cwin[x, b], blank], axis=0) for x in planes]
            wide = dot_left(rows, jnp.concatenate(columns, axis=1))
            for i, x in enumerate(planes):
                for j in range(4):
                    here = wide[:, 128 * i : 128 * i + 128]
                    lc1[8 * x : 8 * x + 8, 128 * j : 128 * j + 128] = here[8 * j : 8 * j + 8]
                    lc2[8 * x : 8 * x + 8, 128 * j : 128 * j + 128] = here[32 + 8 * j : 40 + 8 * j]
        ub[b] = dot_right(lc1[...], zp[b]).reshape(21, 8, 512)
        vb[b] = (dot_right(lc2[...], zp[b]) + dot_right(lc1[...], zs[b])).reshape(21, 8, 512)

    def project():
        scale = DAMPING / center_of(0)
        for b in range(2):

            def step(s, total, b=b):
                left, right = [], []
                for h in range(4):
                    rows = pl.ds(pl.multiple_of(s * 64 + 16 * h, 16), 16)
                    occ = occ_ref[b, :, rows, :].astype(F32)
                    vir = vir_ref[b, :, rows, :].astype(F32)
                    for g in range(2):
                        x = ax_ref[b] + s * 8 + 2 * h + g
                        mid = ub[b, halve(x + 2)]
                        late = (1.0 - DAMPING) * mid
                        late = late + scale * (ub[b, halve(x + 1)] + ub[b, halve(x + 3)] + vb[b, halve(x + 2)])
                        parts = []
                        for t in range(4):
                            cells = wins[t // 2][x, b, t % 2] + late[:, 128 * t : 128 * t + 128]
                            weighted = occ[:, 8 * g : 8 * g + 8] * cells[None]
                            parts.append(weighted.reshape(64, 128).astype(BF16))
                        left.append(jnp.concatenate(parts, axis=0))
                        right.append(vir[:, 8 * g : 8 * g + 8].reshape(64, 128).astype(BF16))
                left, right = jnp.concatenate(left, axis=1), jnp.concatenate(right, axis=1)
                return total + lax.dot_general(
                    left, right, (((1,), (1,)), ((), ())), preferred_element_type=F32
                )

            total = lax.fori_loop(0, 4, step, jnp.zeros((256, 64), F32))
            row = lax.broadcasted_iota(jnp.int32, (256, 64), 0) % 8
            col = lax.broadcasted_iota(jnp.int32, (256, 64), 1) % 8
            total = jnp.where(row == col, total, 0.0)
            total = jnp.sum(total.reshape(32, 8, 64), axis=1)
            col = lax.broadcasted_iota(jnp.int32, (64, 128), 1)
            row = lax.broadcasted_iota(jnp.int32, (64, 128), 0) // 8
            pick = jnp.where(row == col, float(BOX) ** (-1.5), 0.0)
            coup_ref[b] = dot_high(total, pick)

    for c in far0:
        c.wait_recv()
    rise1(0)
    for c in far1:
        c.wait_recv()
    rise1(1)
    margins = [copy(w1.at[p, pl.ds(0, 5), pl.ds(8, 24)], mar1.at[p], gx, south) for p in range(2)]
    for c in margins:
        c.start()
    edge0.wait_send()
    edge1.wait_send()
    backs[1].pass_on()
    keeps = [rise0(0)]
    for c in margins:
        c.wait_recv()
    windows1()
    late = give_back1()
    late.start()
    keeps.append(rise0(1))
    late.pass_on()
    backs[0].arrive()
    backs[1].arrive()
    late.arrive()
    expand(0)
    expand(1)
    project()
    for c in keeps:
        c.wait()
    for c in unsent + margins:
        c.wait_send()
    for c in moves + backs + [late]:
        c.settle()


def params(**more):
    return pltpu.CompilerParams(vmem_limit_bytes=40 * 1024 * 1024, **more)


def shaped(shape, dtype=F32):
    return jax.ShapeDtypeStruct(shape, dtype)


def per_device(slabs, tiles, occupied, virtual, trials, anchor_x, anchor_y, anchor_z):
    occ = occupied.reshape(2, 8, 256, 128)
    vir = virtual.reshape(2, 8, 256, 128)
    tab = tables(slabs, tiles)
    exact = [jnp.asarray(tab[k], BF16) for k in ("r0", "r1", "p1", "p0")]
    wide = [jnp.asarray(tab[k], F32) for k in ("fz", "bz", "fy", "by", "kx", "inv")]
    potential, coupling = pl.pallas_call(
        whole_kernel,
        out_shape=(shaped((4, 8, 128, 128)), shaped((2, 32, 128))),
        in_specs=[SMEM] * 3 + [VMEM] * 13,
        out_specs=(ANY, VMEM),
        scratch_shapes=[
            pltpu.VMEM((2, 48, 2, 8, 128), F32),
            pltpu.VMEM((2, 40, 2, 2, 8, 128), F32),
            pltpu.VMEM((2, 5, 10, 2, 2, 8, 128), F32),
            pltpu.VMEM((5, 8, 128), jnp.int32),
            pltpu.SMEM((5, 8, 128), jnp.int32),
            pltpu.VMEM((2, 160, 320), BF16),
            pltpu.VMEM((320, 160), BF16),
            pltpu.VMEM((2, 10, 2, 2, 8, 128), F32),
            pltpu.VMEM((2, 10, 2, 8, 128), F32),
            pltpu.VMEM((2, 10, 2, 160, 128), F32),
            pltpu.VMEM((2, 10, 2, 32, 128), F32),
            pltpu.VMEM((2, 2, 8, 8, 128), F32),
            pltpu.VMEM((2, 2, 8, 8, 128), F32),
            pltpu.VMEM((10, 4, 144, 128), F32),
            pltpu.VMEM((2, 8, 80, 128), F32),
            pltpu.VMEM((6, 48, 128), F32),
            pltpu.VMEM((10, 2, 144, 128), F32),
            pltpu.VMEM((8, 80, 128), F32),
            pltpu.VMEM((2, 6, 80, 128), F32),
            pltpu.VMEM((6, 48, 128), F32),
            pltpu.VMEM((4, 48, 128), F32),
            pltpu.VMEM((144, 128), F32),
            pltpu.VMEM((tiles, 8, 128), F32),
            pltpu.VMEM((tiles, 8, 128), F32),
            pltpu.VMEM((8, 128), F32),
            pltpu.VMEM((slabs, 8, 128), F32),
            pltpu.VMEM((3, 8, 128), F32),
            pltpu.VMEM((tiles, 3, 8, 128), F32),
            pltpu.VMEM((4, 8, 128, 128), F32),
            pltpu.VMEM((4, 8, 32, 128), F32),
            pltpu.VMEM((2, 4, 8, 2, 2, 8, 128), F32),
            pltpu.VMEM((40, 2, 2, 8, 128), F32),
            pltpu.VMEM((40, 2, 2, 8, 128), F32),
            pltpu.VMEM((2, 8, 2, 2, 8, 128), F32),
            pltpu.VMEM((2, 8, 2, 8, 128), F32),
            pltpu.VMEM((8, 128), jnp.int32),
            pltpu.VMEM((2, 5, 24, 128), F32),
            pltpu.VMEM((320, 96), BF16),
            pltpu.VMEM((10, 256, 128), BF16),
            pltpu.VMEM((10, 320, 256), BF16),
            pltpu.VMEM((4, 4, 2, 24, 128), F32),
            pltpu.VMEM((21, 2, 24, 128), F32),
            pltpu.VMEM((4, 2, 24, 128), F32),
            pltpu.VMEM((4, 24, 128), F32),
            pltpu.VMEM((168, 512), F32),
            pltpu.VMEM((168, 512), F32),
            pltpu.VMEM((2, 512, 512), BF16),
            pltpu.VMEM((2, 512, 512), BF16),
            pltpu.VMEM((2, 21, 8, 512), F32),
            pltpu.VMEM((2, 21, 8, 512), F32),
            pltpu.SemaphoreType.DMA((96,)),
            pltpu.SemaphoreType.DMA((96,)),
            pltpu.SemaphoreType.DMA((slabs,)),
            pltpu.SemaphoreType.DMA((slabs,)),
            pltpu.SemaphoreType.DMA((3,)),
        ],
        compiler_params=params(collective_id=0, has_side_effects=True),
        name="whole",
    )(anchor_x, anchor_y, anchor_z, occ, vir, trials.reshape(2, 32, 8), *exact, *wide)
    return potential, coupling[:, :, :8].reshape(2, 4, 8, 8)


def solution(mesh):
    placed = (
        P(("gx", "gy"), None, None),
        P(("gx", "gy"), None, None),
        P(("gx", "gy"), None, None, None),
        P(("gx", "gy")),
        P(("gx", "gy")),
        P(("gx", "gy")),
    )
    return jax.shard_map(
        functools.partial(per_device, mesh.shape["gx"], mesh.shape["gy"]),
        mesh=mesh,
        in_specs=placed,
        out_specs=(P(None, "gx", "gy", None), P(("gx", "gy"), None, None, None)),
        check_vma=False,
    )
```

```python
import functools

import jax
import jax.numpy as jnp
import numpy as np
from jax import lax
from jax.experimental import pallas as pl
from jax.experimental.pallas import tpu as pltpu
from jax.sharding import PartitionSpec as P

BOX = 32
TRIALS = 4
CX = 8
CY = 128
NZ = 128
SCREEN = 0.05
DAMPING = 2.0 / 3.0
MESH = pl.DeviceIdType.MESH
F32 = jnp.float32
BF16 = jnp.bfloat16
HIGH = lax.Precision.HIGHEST
VMEM = pl.BlockSpec(memory_space=pltpu.VMEM)
SMEM = pl.BlockSpec(memory_space=pltpu.SMEM)
ANY = pl.BlockSpec(memory_space=pl.ANY)


def center_of(level):
    spacing = 2.0**level
    return 6.0 / spacing**2 + SCREEN**2


def split2(x):
    hi = x.astype(BF16)
    lo = (x - hi.astype(F32)).astype(BF16)
    return hi, lo


def dot(a, b):
    return jnp.dot(a, b, preferred_element_type=F32)


def dot_right(x, w):
    hi, lo = split2(x)
    return dot(hi, w) + dot(lo, w)


def dot_left(w, x):
    hi, lo = split2(x)
    return dot(w, hi) + dot(w, lo)


def dot_high(a, b):
    return jnp.dot(a, b, preferred_element_type=F32, precision=HIGH)


def z_beside(x, n):
    if n == 128:
        return pltpu.roll(x, 1, 1) + pltpu.roll(x, 127, 1)
    lane = lax.broadcasted_iota(jnp.int32, x.shape, 1) % n
    below = jnp.where(lane == 0, pltpu.roll(x, 129 - n, 1), pltpu.roll(x, 1, 1))
    above = jnp.where(lane == n - 1, pltpu.roll(x, n - 1, 1), pltpu.roll(x, 127, 1))
    return below + above


def hartley_np(count):
    index = np.arange(count)
    angle = 2.0 * np.pi / count * ((index[:, None] * index[None, :]) % count)
    return (np.cos(angle) + np.sin(angle)) / np.sqrt(count)


def eigen_np(count, spacing):
    return (2.0 - 2.0 * np.cos(2.0 * np.pi / count * np.arange(count))) / (spacing * spacing)


@functools.lru_cache(None)
def tables(slabs, tiles):
    out = {}
    r0 = np.zeros((2, 128, 2, 64))
    r1 = np.zeros((2, 2, 64, 4, 32))
    p1 = np.zeros((2, 4, 32, 2, 64))
    p0 = np.zeros((2, 64, 2, 128))
    for t in range(2):
        for z in range(128):
            r0[t, z, t, z // 2] = 0.125
            p0[t, z // 2, t, z] = 1.0
        for z in range(64):
            for p in range(2):
                r1[p, t, z, 2 * p + t, z // 2] = 0.125
                p1[p, 2 * p + t, z // 2, t, z] = 1.0
    out["r0"] = r0.reshape(256, 128)
    out["r1"] = r1.reshape(2, 128, 128)
    out["p1"] = p1.reshape(2, 128, 128)
    out["p0"] = p0.reshape(128, 256)
    hz = hartley_np(16)
    mean_z = np.zeros((32, 16))
    mean_z[np.arange(32), np.arange(32) // 2] = 1.0
    fz = np.zeros((4, 32, 128))
    bz = np.zeros((128, 4, 32))
    for t in range(4):
        fz[t, :, t * 16 : t * 16 + 16] = 0.125 * mean_z @ hz
        bz[t * 16 : t * 16 + 16, t, :] = hz @ mean_z.T
    out["fz"] = fz.reshape(128, 128)
    out["bz"] = bz.reshape(128, 128)
    size_y = 16 * tiles
    hy = hartley_np(size_y)
    mean_y = np.zeros((16, 32))
    mean_y[np.arange(32) // 2, np.arange(32)] = 1.0
    fy = np.zeros((tiles, size_y, 128))
    by = np.zeros((tiles, 48, 128))
    for q in range(tiles):
        fy[q, :, :32] = hy[:, q * 16 : q * 16 + 16] @ mean_y
        for y in range(-2, 34):
            by[q, 8 + y, :size_y] = hy[(q * 16 + y // 2) % size_y]
    out["fy"] = fy
    out["by"] = by
    out["kx"] = np.kron(hartley_np(slabs), np.eye(8))
    lam_x, lam_y, lam_z = eigen_np(slabs, 8.0), eigen_np(size_y, 8.0), eigen_np(16, 8.0)
    inv = np.zeros((tiles, slabs, 8, 2, 4, 16))
    for q in range(tiles):
        ky = lam_y[q * 16 : q * 16 + 16].reshape(2, 8)
        total = (
            SCREEN * SCREEN
            + lam_x[:, None, None, None, None]
            + ky.T[None, :, :, None, None]
            + lam_z[None, None, None, None, :]
        )
        inv[q] = np.broadcast_to(1.0 / total, (slabs, 8, 2, 4, 16))
    out["inv"] = inv.reshape(tiles, slabs * 8, 128)
    return out


class Shift:
    def __init__(self, sign, pieces, relays, send, recv, slot):
        gx, gy = lax.axis_index("gx"), lax.axis_index("gy")
        n = lax.axis_size("gx")
        place = lax.rem(gx, 4) if sign > 0 else 3 - lax.rem(gx, 4)

        def copy(src, dst, at, k):
            return pltpu.make_async_remote_copy(
                src_ref=src, dst_ref=dst, send_sem=send.at[slot + at], recv_sem=recv.at[slot + at],
                device_id=(lax.rem(gx + sign * k + n, n), gy), device_id_type=MESH,
            )

        held = len(pieces)
        count = held + len(relays)
        self.relays = []
        for r, (k, src, dst, hold, least) in enumerate(relays):
            straight = copy(src, dst, held + r, k)
            first = copy(src, hold, count + r, 4)
            second = copy(hold, dst, held + r, k - 4)
            self.relays.append((straight, first, second, place >= least))
        self.whole = [copy(src, dst, p, k) for p, (k, src, dst) in enumerate(pieces)]

    def start(self):
        for straight, first, second, bent in self.relays:
            pl.when(bent)(first.start)
        for c in self.whole:
            c.start()
        for straight, first, second, bent in self.relays:
            pl.when(jnp.logical_not(bent))(straight.start)

    def pass_on(self):
        for straight, first, second, bent in self.relays:

            def onward(first=first, second=second):
                first.wait_recv()
                second.start()

            pl.when(bent)(onward)

    def arrive(self):
        for straight, first, second, bent in self.relays:
            straight.wait_recv()
        for c in self.whole:
            c.wait_recv()

    def settle(self):
        for straight, first, second, bent in self.relays:

            def sent(first=first, second=second):
                first.wait_send()
                second.wait_send()

            pl.when(bent)(sent)
            pl.when(jnp.logical_not(bent))(straight.wait_send)
        for c in self.whole:
            c.wait_send()


def box_anchors(ay_ref, az_ref, ganc_ref, sources):
    pairs = []
    for s in sources:
        for b in range(2):
            if s < 0:
                pairs.append((ay_ref[b], az_ref[b]))
            else:
                pairs.append((ganc_ref[s, 0, b], ganc_ref[s, 0, 2 + b]))
    return pairs


def select_rows(pairs, axis):
    shape = (160, 320) if axis == 0 else (320, 160)
    row = lax.broadcasted_iota(jnp.int32, shape, axis)
    col = lax.broadcasted_iota(jnp.int32, shape, 1 - axis)
    want = 4 * (col % 8) + (col // 8) % 4
    box = col // 32
    for k, (ay, _) in enumerate(pairs):
        want = want + jnp.where(box == k, ay, 0)
    return jnp.where(row == want, 1.0, 0.0).astype(BF16)


def halve(x):
    return lax.div(x, 2)


def one_hot(hit):
    return jnp.where(hit, 1.0, 0.0)


def select_coarse(pairs):
    row = lax.broadcasted_iota(jnp.int32, (320, 96), 0)
    col = lax.broadcasted_iota(jnp.int32, (320, 96), 1)
    want = row % 32 + 7
    for k, (ay, _) in enumerate(pairs):
        want = want + jnp.where(row // 32 == k, halve(ay + 1), 0)
    return one_hot(col == want).astype(BF16)


def select_coarse_z(az):
    row = lax.broadcasted_iota(jnp.int32, (256, 128), 0)
    col = lax.broadcasted_iota(jnp.int32, (256, 128), 1)
    want = (halve(az + 1) + 63 + col % 32) % 64
    return one_hot((row // 64 == col // 32) & (row % 64 == want)).astype(BF16)


def widen_rows(ay):
    row = lax.broadcasted_iota(jnp.int32, (64, 32), 0)
    col = lax.broadcasted_iota(jnp.int32, (64, 32), 1)
    cell = 4 * (row % 8) + (row // 8) % 4 + ay
    first = halve(ay + 1) - 1
    at = [jnp.right_shift(cell + d, 1) - first for d in (0, -1, 1)]
    beside = one_hot(col == at[1]) + one_hot(col == at[2])
    return jnp.where(row < 32, one_hot(col == at[0]), beside).astype(BF16)


def widen_lanes(az, j):
    row = lax.broadcasted_iota(jnp.int32, (128, 512), 0)
    col = lax.broadcasted_iota(jnp.int32, (128, 512), 1)
    cell = col % 32 + az
    first = halve(az + 1) - 1
    same = (row // 32 == col // 128) & ((col // 32) % 4 == j)
    at = [jnp.right_shift(cell + d, 1) - first for d in (0, -1, 1)]
    hits = [one_hot(same & (row % 32 == a)) for a in at]
    return hits[0].astype(BF16), (hits[1] + hits[2]).astype(BF16)


def mixing(pair_of_trials, p):
    row = lax.broadcasted_iota(jnp.int32, (128, 32), 0)
    col = lax.broadcasted_iota(jnp.int32, (128, 32), 1)
    rows = one_hot(col == (2 * p + (row // 8) % 2) * 8 + row // 16).astype(BF16)
    taken = dot(rows, pair_of_trials).astype(BF16)
    row = lax.broadcasted_iota(jnp.int32, (8, 64), 0)
    col = lax.broadcasted_iota(jnp.int32, (8, 64), 1)
    spread = dot(taken, one_hot(row == col // 8).astype(BF16))
    row = lax.broadcasted_iota(jnp.int32, (128, 64), 0)
    col = lax.broadcasted_iota(jnp.int32, (128, 64), 1)
    return jnp.where(row % 8 == col % 8, spread, 0.0).astype(BF16)


def whole_kernel(
    ax_ref, ay_ref, az_ref, occ_ref, vir_ref, trial_ref,
    r0_ref, r1_ref, p1_ref, p0_ref, fz_ref, bz_ref, fy_ref, by_ref, kx_ref, inv_ref,
    out_ref, coup_ref,
    dens, src, got, ganc, sanc, sel, selt, hold1, hold2, f_ref,
    rim, sides, beyond, fp, f1p, f2p, v0, v1p, w1, v2p, w2, tmp, qs, qr, gs, gall, us, ur,
    pot, margin, cut, win0, win1, hold3, hold4,
    word, mar1, selc, selz, taken, cut1, cwin, hold5, hold6, lc1, lc2, zp, zs, ub, vb,
    send, recv, gsend, grecv, local,
):
    gx, gy = lax.axis_index("gx"), lax.axis_index("gy")
    n, m = lax.axis_size("gx"), lax.axis_size("gy")
    east, west = lax.rem(gx + 1, n), lax.rem(gx + n - 1, n)
    north, south = lax.rem(gy + 1, m), lax.rem(gy + m - 1, m)
    wins = (win0, win1)
    used = [0]

    def slots(count):
        used[0] += count
        return used[0] - count

    barrier = pltpu.get_barrier_semaphore()
    for d in range(1, m):
        pl.semaphore_signal(barrier, inc=1, device_id=(gx, lax.rem(gy + d, m)), device_id_type=MESH)
    for x in (east, west):
        for y in (north, south):
            pl.semaphore_signal(barrier, inc=1, device_id=(x, y), device_id_type=MESH)

    def greet(d, carry):
        pl.semaphore_signal(barrier, inc=1, device_id=(lax.rem(gx + d, n), gy), device_id_type=MESH)
        return carry

    lax.fori_loop(1, n, greet, 0)

    def copy(src_ref, dst_ref, x, y):
        slot = slots(1)
        return pltpu.make_async_remote_copy(
            src_ref=src_ref, dst_ref=dst_ref, send_sem=send.at[slot], recv_sem=recv.at[slot],
            device_id=(x, y), device_id_type=MESH,
        )

    unsent = []

    for b in range(2):
        for x in range(8):
            dens[b, x] = jnp.zeros((2, 8, 128), F32)
            dens[b, 40 + x] = jnp.zeros((2, 8, 128), F32)

    def density(p):
        for b in range(2):
            weights = mixing(trial_ref[b], p)

            def step(s, carry, b=b, weights=weights):
                rows = pl.ds(pl.multiple_of(s * 16, 16), 16)
                vir = vir_ref[b, :, rows, :].astype(F32)
                occ = occ_ref[b, :, rows, :].astype(F32)
                parts = [vir[:, 8 * h : 8 * h + 8].reshape(64, 128) for h in range(2)]
                mixed = dot(weights, jnp.concatenate(parts, axis=1).astype(BF16))
                mixed = mixed.reshape(8, 2, 8, 256)
                for h in range(2):
                    part = mixed[..., 128 * h : 128 * h + 128]
                    dens[b, 8 + 2 * s + h] = jnp.sum(occ[:, None, 8 * h : 8 * h + 8] * part, axis=0)
                return carry

            lax.fori_loop(0, 16, step, 0)

        def place(x, carry):
            for b in range(2):
                src[p, x, b] = dens[b, x + 8 - ax_ref[b]]
            return carry

        lax.fori_loop(0, 40, place, 0)

    def deposit(p):
        s, g = src.at[p], got.at[p]
        pieces = [
            (4, s.at[pl.ds(31, 8)], g.at[3, pl.ds(0, 8)]),
            (3, s.at[pl.ds(23, 10)], g.at[2]),
            (2, s.at[pl.ds(15, 10), 0], g.at[1, :, 0]),
            (-1, s.at[pl.ds(0, 1)], g.at[4, pl.ds(9, 1)]),
        ]
        relays = [
            (1, s.at[pl.ds(7, 10)], g.at[0], hold1.at[p], 3),
            (2, s.at[pl.ds(15, 10), 1], g.at[1, :, 1], hold2.at[p], 2),
        ]
        return Shift(1, pieces, relays, send, recv, slots(8))

    density(0)
    pl.semaphore_wait(barrier, m - 1 + 4 + n - 1)
    lane = lax.broadcasted_iota(jnp.int32, (8, 128), 1)
    value = jnp.zeros((8, 128), jnp.int32)
    for k, anchor in enumerate((ay_ref[0], ay_ref[1], az_ref[0], az_ref[1])):
        value = jnp.where(lane == k, anchor, value)
    word[...] = value
    words = [copy(word, ganc.at[s], lax.rem(gx + k + n, n), gy) for s, k in enumerate((1, 2, 3, 4, -1))]
    moves = [deposit(0), deposit(1)]
    moves[0].start()
    for c in words:
        c.start()
    density(1)
    moves[1].start()
    moves[0].pass_on()
    for c in words:
        c.wait()
    read = pltpu.make_async_copy(ganc, sanc, local.at[0])
    read.start()
    read.wait()
    usual = box_anchors(ay_ref, az_ref, sanc, [-1, 0, 1, 2, 3])
    last = box_anchors(ay_ref, az_ref, sanc, [-1, 0, 1, 2, 4])
    sel[0] = select_rows(usual, 0)
    sel[1] = select_rows(last, 0)
    selt[...] = select_rows(usual, 1)
    blank = jnp.zeros((8, 128), F32)

    def plane(p, e, own, takes, edge):
        pairs = last if edge else usual
        loads = []
        for s in range(5):
            for b in range(2):
                if s == 0:
                    loads.append((lambda t, b=b: src[p, e - 1, b, t]) if own else None)
                elif s == 4 and edge:
                    loads.append(lambda t, b=b: got[p, 4, 9, b, t])
                elif s in takes:
                    loads.append(lambda t, s=s, b=b: got[p, s - 1, e, b, t])
                else:
                    loads.append(None)
        masks = [(lane >= az) & (lane < az + 32) for _, az in pairs]
        columns = []
        for t in range(2):
            rows = []
            for k, load in enumerate(loads):
                if load is None:
                    rows += [blank] * 4
                    continue
                value = load(t)
                for j in range(4):
                    moved = pltpu.roll(value, lax.rem(pairs[k][1] + 128 - 32 * j, 128), 1)
                    rows.append(jnp.where(masks[k], moved, 0.0))
            columns.append(jnp.concatenate(rows, axis=0))
        placed = dot_left(sel[1 if edge else 0], jnp.concatenate(columns, axis=1))
        f_ref[p, e, 0] = placed[:, :128]
        f_ref[p, e, 1] = placed[:, 128:]

    def accumulate(p):
        plane(p, 0, False, (1, 2, 3, 4), False)

        def step(e, carry):
            plane(p, e, True, (1, 2, 3, 4), False)
            return carry

        lax.fori_loop(1, 8, step, 0)
        plane(p, 8, True, (1, 2, 3), False)
        plane(p, 9, True, (1, 2, 3), True)

    def send_rim(p):
        copies = [copy(f_ref.at[p, :, :, pl.ds(128, 32), :], rim.at[p], gx, north)]
        copies[0].start()

        def edge(e, carry):
            for t in range(2):
                sides[p, 0, e, t : t + 1] = f_ref[p, e + 1, t, 127:128]
                sides[p, 1, e, t : t + 1] = f_ref[p, e + 1, t, 0:1]
            return carry

        lax.fori_loop(0, 8, edge, 0)
        copies += [
            copy(sides.at[p, 0], beyond.at[p, 0], gx, north),
            copy(sides.at[p, 1], beyond.at[p, 1], gx, south),
        ]
        for c in copies[1:]:
            c.start()

        def early(e, carry):
            for t in range(2):
                fp[e, 2 * p + t, 40:136] = f_ref[p, e, t, 32:128]
            return carry

        lax.fori_loop(0, 10, early, 0)
        return copies

    def join_rim(p, copies):
        for c in copies:
            c.wait_recv()
        unsent.extend(copies)

        def join(e, carry):
            for t in range(2):
                fp[e, 2 * p + t, 8:40] = f_ref[p, e, t, 0:32] + rim[p, e, t]
            return carry

        def rims(e, carry):
            for t in range(2):
                fp[e, 2 * p + t, 7:8] = beyond[p, 0, e - 1, t : t + 1]
                fp[e, 2 * p + t, 136:137] = f_ref[p, e, t, 128:129] + beyond[p, 1, e - 1, t : t + 1]
            return carry

        lax.fori_loop(1, 9, rims, 0)
        lax.fori_loop(0, 10, join, 0)

    def down0(p):
        scale = DAMPING / center_of(0)

        def step(xc, carry):
            halves = []
            for t in (2 * p, 2 * p + 1):
                total = None
                for x in range(2):
                    e = 2 * xc + 1 + x
                    mid = fp[e, t, 8:136]
                    beside = fp[e, t, 7:135] + fp[e, t, 9:137] + fp[e - 1, t, 8:136] + fp[e + 1, t, 8:136]
                    beside = beside + z_beside(mid, 128)
                    res = (1.0 - DAMPING) * mid + scale * beside
                    pot[t, e - 1] = scale * (mid + res)
                    total = res if total is None else total + res
                tmp[0:128, :] = total
                halves.append(tmp[pl.ds(0, 64, stride=2), :] + tmp[pl.ds(1, 64, stride=2), :])
            f1p[p, 2 + xc, 8:72] = dot_right(jnp.concatenate(halves, axis=1), r0_ref[...])
            return carry

        lax.fori_loop(0, 4, step, 0)

    def swap(buf, a, c):
        def part(x0, nx, y0, ny):
            return buf.at[pl.ds(x0, nx), pl.ds(y0, ny)]

        near = [
            copy(part(a + 1, 1, 8, c), part(1, 1, 8, c), east, gy),
            copy(part(2, 1, 8, c), part(a + 2, 1, 8, c), west, gy),
            copy(part(2, a, c, 8), part(2, a, 0, 8), gx, north),
            copy(part(2, a, 8, 8), part(2, a, c + 8, 8), gx, south),
        ]
        far = [
            copy(part(a, 1, 8, c), part(0, 1, 8, c), east, gy),
            copy(part(3, 1, 8, c), part(a + 3, 1, 8, c), west, gy),
            copy(part(a, 2, c, 8), part(0, 2, 0, 8), east, north),
            copy(part(a, 2, 8, 8), part(0, 2, c + 8, 8), east, south),
            copy(part(2, 2, c, 8), part(a + 2, 2, 0, 8), west, north),
            copy(part(2, 2, 8, 8), part(a + 2, 2, c + 8, 8), west, south),
        ]
        for one in near + far:
            one.start()
        unsent.extend(near + far)
        return near, far

    def send_margin(p):
        pair = pl.ds(2 * p, 2)
        c = copy(pot.at[pair, :, pl.ds(0, 32), :], margin.at[pair], gx, south)
        c.start()
        return c

    group = lax.broadcasted_iota(jnp.int32, (8, 128), 1) // 32

    def windows(p):
        def step(x, carry):
            columns = [
                jnp.concatenate([pot[2 * p + t, x], margin[2 * p + t, x]], axis=0) for t in range(2)
            ]
            taken = dot_left(selt[...], jnp.concatenate(columns, axis=1))
            for t in range(2):
                for k in range(10):
                    total = None
                    for j in range(4):
                        piece = taken[32 * k + 8 * j : 32 * k + 8 * j + 8, 128 * t : 128 * t + 128]
                        piece = pltpu.roll(piece, lax.rem(128 + 32 * j - usual[k][1], 128), 1)
                        total = piece if total is None else jnp.where(group == j, piece, total)
                    if k < 2:
                        wins[p][x, k, t] = total
                    else:
                        cut[p, k // 2 - 1, x, k % 2, t] = total
            return carry

        lax.fori_loop(0, 8, step, 0)

    def give_back(p):
        c, w = cut.at[p], wins[p]
        pieces = [
            (4, c.at[3], w.at[pl.ds(32, 8)]),
            (3, c.at[2], w.at[pl.ds(24, 8)]),
            (2, c.at[1, :, 0], w.at[pl.ds(16, 8), 0]),
        ]
        relays = [
            (1, c.at[0], w.at[pl.ds(8, 8)], hold3.at[p], 3),
            (2, c.at[1, :, 1], w.at[pl.ds(16, 8), 1], hold4.at[p], 2),
        ]
        return Shift(-1, pieces, relays, send, recv, slots(7))

    moves[0].arrive()
    accumulate(0)
    rims0 = send_rim(0)
    moves[1].pass_on()
    join_rim(0, rims0)
    down0(0)
    near0, far0 = swap(f1p.at[0], 4, 64)
    edge0 = send_margin(0)
    moves[1].arrive()
    accumulate(1)
    rims1 = send_rim(1)
    backs = [give_back(0), give_back(1)]
    edge0.wait_recv()
    windows(0)
    join_rim(1, rims1)
    down0(1)
    near1, far1 = swap(f1p.at[1], 4, 64)
    edge1 = send_margin(1)
    selc[...] = select_coarse(usual)

    def down1(p, xc):
        scale = DAMPING / center_of(1) / 4.0
        both = None
        for x in range(2):
            e = 2 + 2 * xc + x
            mid = f1p[p, e, 8:72]
            beside = f1p[p, e, 7:71] + f1p[p, e, 9:73] + f1p[p, e - 1, 8:72] + f1p[p, e + 1, 8:72]
            beside = beside + z_beside(mid, 64)
            res = (1.0 - DAMPING) * mid + scale * beside
            both = res if both is None else both + res
        tmp[0:64, :] = both
        pair = tmp[pl.ds(0, 32, stride=2), :] + tmp[pl.ds(1, 32, stride=2), :]
        return dot_right(pair, r1_ref[p])

    for c in near0:
        c.wait_recv()
    held = [down1(0, xc) for xc in range(2)]
    for c in near1:
        c.wait_recv()
    for xc in range(2):
        f2p[2 + xc, 8:40] = held[xc] + down1(1, xc)
    near2, far2 = swap(f2p, 2, 32)
    backs[0].start()
    for c in near2:
        c.wait_recv()

    scale = DAMPING / center_of(2) / 16.0
    total = None
    for x in range(2):
        e = 2 + x
        mid = f2p[e, 8:40]
        beside = f2p[e, 7:39] + f2p[e, 9:41] + f2p[e - 1, 8:40] + f2p[e + 1, 8:40]
        beside = beside + z_beside(mid, 32)
        res = (1.0 - DAMPING) * mid + scale * beside
        total = res if total is None else total + res
    modes = dot_high(total, fz_ref[...])
    modes = jnp.concatenate([modes, jnp.zeros((96, 128), F32)], axis=0)
    modes = dot_high(fy_ref[gy], modes)
    for q in range(m):
        qs[q] = modes[16 * q : 16 * q + 8] + pltpu.roll(modes[16 * q + 8 : 16 * q + 16], 64, 1)
    copies = []
    for d in range(1, m):
        to = lax.rem(gy + d, m)
        copies.append(copy(qs.at[to], qr.at[d - 1], gx, to))
    for c in copies:
        c.start()
    unsent.extend(copies)
    edge1.wait_recv()
    windows(1)
    backs[1].start()
    for k in range(10):
        selz[k] = select_coarse_z(usual[k][1])
    mine = qs[gy]
    for d, c in enumerate(copies):
        c.wait_recv()
        mine = mine + qr[d]
    gs[...] = mine

    def shout(d):
        return pltpu.make_async_remote_copy(
            src_ref=gs, dst_ref=gall.at[gx], send_sem=gsend.at[d], recv_sem=grecv.at[d],
            device_id=(lax.rem(gx + d, n), gy), device_id_type=MESH,
        )

    def begin(d, carry):
        shout(d).start()
        return carry

    def end(d, carry):
        shout(d).wait()
        return carry

    lax.fori_loop(1, n, begin, 0)
    gall[gx] = mine
    for b in range(2):
        for j in range(4):
            zp[b, 128 * j : 128 * j + 128], zs[b, 128 * j : 128 * j + 128] = widen_lanes(az_ref[b], j)
    lax.fori_loop(1, n, end, 0)
    spectrum = dot_high(kx_ref[...], gall[...].reshape(8 * n, 128)) * inv_ref[gy]
    for s, x in enumerate((west, gx, east)):
        us[s] = dot_high(kx_ref[pl.ds(pl.multiple_of(8 * x, 8), 8), :], spectrum)

    copies = []
    for d in range(1, m):
        to = lax.rem(gy + d, m)
        copies.append(copy(us, ur.at[gy], gx, to))
    for c in copies:
        c.start()
    unsent.extend(copies)
    ur[gy] = us[...]
    backs[0].pass_on()
    for c in copies:
        c.wait_recv()

    for c in far2:
        c.wait_recv()
    scale = DAMPING / center_of(2)
    for s in range(3):
        rows = []
        for q in range(m):
            half = ur[q, s]
            rows += [half, pltpu.roll(half, 64, 1)]
        if m < 8:
            rows.append(jnp.zeros((128 - 16 * m, 128), F32))
        ahead = dot_high(by_ref[gy], jnp.concatenate(rows, axis=0))
        ahead = dot_high(ahead, bz_ref[...])
        for x in range(2):
            v2p[2 * s + x] = scale * f2p[2 * s + x] + ahead
    for e in range(1, 5):
        mid = v2p[e]
        beside = v2p[e - 1] + v2p[e + 1] + pltpu.roll(mid, 1, 0) + pltpu.roll(mid, 47, 0)
        beside = beside + z_beside(mid, 32)
        w2[e - 1] = (1.0 - DAMPING) * mid + scale * f2p[e] + (scale / 16.0) * beside

    def rise1(p):
        scale = DAMPING / center_of(1)
        for e in range(4):
            wide = dot_right(w2[e, 4:44], p1_ref[p])
            tmp[pl.ds(0, 40, stride=2), :] = wide
            tmp[pl.ds(1, 40, stride=2), :] = wide
            for x in range(2):
                v1p[2 * e + x] = scale * f1p[p, 2 * e + x] + tmp[0:80, :]

        def step(e, carry):
            mid = v1p[e]
            beside = v1p[e - 1] + v1p[e + 1] + pltpu.roll(mid, 1, 0) + pltpu.roll(mid, 79, 0)
            beside = beside + z_beside(mid, 64)
            w1[p, e - 1] = (1.0 - DAMPING) * mid + scale * f1p[p, e] + (scale / 4.0) * beside
            return carry

        lax.fori_loop(1, 7, step, 0)

    def rise0(p):
        scale = DAMPING / center_of(0)

        def widen(i, planes):
            wide = dot_right(w1[p, i, 4:76], p0_ref[...])
            for t in range(2):
                value = wide[:, 128 * t : 128 * t + 128]
                for e in planes:
                    v0[e, t, pl.ds(0, 72, stride=2), :] = value
                    v0[e, t, pl.ds(1, 72, stride=2), :] = value

        widen(0, (0,))

        def lift(i, carry):
            widen(i, (2 * i - 1, 2 * i))
            return carry

        lax.fori_loop(1, 5, lift, 0)
        widen(5, (9,))

        def step(e, carry):
            for t in range(2):
                mid = v0[e, t, 8:136]
                beside = v0[e, t, 7:135] + v0[e, t, 9:137] + v0[e - 1, t, 8:136] + v0[e + 1, t, 8:136]
                beside = beside + z_beside(mid, 128)
                pot[2 * p + t, e - 1] = pot[2 * p + t, e - 1] + (1.0 - DAMPING) * mid + scale * beside
            return carry

        lax.fori_loop(1, 9, step, 0)
        pair = pl.ds(2 * p, 2)
        keep = pltpu.make_async_copy(pot.at[pair], out_ref.at[pair], local.at[1 + p])
        keep.start()
        return keep

    def windows1():
        for i in range(5):
            columns = [jnp.concatenate([w1[p, i, 0:72], mar1[p, i]], axis=0) for p in range(2)]
            hi, lo = split2(jnp.concatenate(columns, axis=1))
            taken[2 * i] = dot(selc[...], hi).astype(BF16)
            taken[2 * i + 1] = dot(selc[...], lo).astype(BF16)
        for k in range(10):
            rows = jnp.concatenate([taken[i, 32 * k : 32 * k + 32] for i in range(10)], axis=0)
            rows = dot(rows, selz[k])
            for i in range(5):
                part = rows[64 * i : 64 * i + 24] + rows[64 * i + 32 : 64 * i + 56]
                if k < 2:
                    cwin[i, k] = part
                elif i > 0:
                    cut1[k // 2 - 1, i - 1, k % 2] = part

    def give_back1():
        pieces = [
            (4, cut1.at[3], cwin.at[pl.ds(17, 4)]),
            (3, cut1.at[2], cwin.at[pl.ds(13, 4)]),
            (2, cut1.at[1, :, 0], cwin.at[pl.ds(9, 4), 0]),
        ]
        relays = [
            (1, cut1.at[0], cwin.at[pl.ds(5, 4)], hold5, 3),
            (2, cut1.at[1, :, 1], cwin.at[pl.ds(9, 4), 1], hold6, 2),
        ]
        return Shift(-1, pieces, relays, send, recv, slots(7))

    def expand(b):
        rows = widen_rows(ay_ref[b])
        blank = jnp.zeros((8, 128), F32)
        for g in range(11):
            planes = [x for x in (2 * g, 2 * g + 1) if x < 21]
            columns = [jnp.concatenate([cwin[x, b], blank], axis=0) for x in planes]
            wide = dot_left(rows, jnp.concatenate(columns, axis=1))
            for i, x in enumerate(planes):
                for j in range(4):
                    here = wide[:, 128 * i : 128 * i + 128]
                    lc1[8 * x : 8 * x + 8, 128 * j : 128 * j + 128] = here[8 * j : 8 * j + 8]
                    lc2[8 * x : 8 * x + 8, 128 * j : 128 * j + 128] = here[32 + 8 * j : 40 + 8 * j]
        ub[b] = dot_right(lc1[...], zp[b]).reshape(21, 8, 512)
        vb[b] = (dot_right(lc2[...], zp[b]) + dot_right(lc1[...], zs[b])).reshape(21, 8, 512)

    def project():
        scale = DAMPING / center_of(0)
        for b in range(2):

            def step(s, total, b=b):
                left, right = [], []
                for h in range(4):
                    rows = pl.ds(pl.multiple_of(s * 64 + 16 * h, 16), 16)
                    occ = occ_ref[b, :, rows, :].astype(F32)
                    vir = vir_ref[b, :, rows, :].astype(F32)
                    for g in range(2):
                        x = ax_ref[b] + s * 8 + 2 * h + g
                        mid = ub[b, halve(x + 2)]
                        late = (1.0 - DAMPING) * mid
                        late = late + scale * (ub[b, halve(x + 1)] + ub[b, halve(x + 3)] + vb[b, halve(x + 2)])
                        parts = []
                        for t in range(4):
                            cells = wins[t // 2][x, b, t % 2] + late[:, 128 * t : 128 * t + 128]
                            weighted = occ[:, 8 * g : 8 * g + 8] * cells[None]
                            parts.append(weighted.reshape(64, 128).astype(BF16))
                        left.append(jnp.concatenate(parts, axis=0))
                        right.append(vir[:, 8 * g : 8 * g + 8].reshape(64, 128).astype(BF16))
                left, right = jnp.concatenate(left, axis=1), jnp.concatenate(right, axis=1)
                return total + lax.dot_general(
                    left, right, (((1,), (1,)), ((), ())), preferred_element_type=F32
                )

            total = lax.fori_loop(0, 4, step, jnp.zeros((256, 64), F32))
            row = lax.broadcasted_iota(jnp.int32, (256, 64), 0) % 8
            col = lax.broadcasted_iota(jnp.int32, (256, 64), 1) % 8
            total = jnp.where(row == col, total, 0.0)
            total = jnp.sum(total.reshape(32, 8, 64), axis=1)
            col = lax.broadcasted_iota(jnp.int32, (64, 128), 1)
            row = lax.broadcasted_iota(jnp.int32, (64, 128), 0) // 8
            pick = jnp.where(row == col, float(BOX) ** (-1.5), 0.0)
            coup_ref[b] = dot_high(total, pick)

    for c in far0:
        c.wait_recv()
    rise1(0)
    for c in far1:
        c.wait_recv()
    rise1(1)
    margins = [copy(w1.at[p, pl.ds(0, 5), pl.ds(8, 24)], mar1.at[p], gx, south) for p in range(2)]
    for c in margins:
        c.start()
    edge0.wait_send()
    edge1.wait_send()
    backs[1].pass_on()
    keeps = [rise0(0)]
    for c in margins:
        c.wait_recv()
    windows1()
    late = give_back1()
    late.start()
    keeps.append(rise0(1))
    late.pass_on()
    backs[0].arrive()
    backs[1].arrive()
    late.arrive()
    expand(0)
    expand(1)
    project()
    for c in keeps:
        c.wait()
    for c in unsent + margins:
        c.wait_send()
    for c in moves + backs + [late]:
        c.settle()


def params(**more):
    return pltpu.CompilerParams(vmem_limit_bytes=40 * 1024 * 1024, **more)


def shaped(shape, dtype=F32):
    return jax.ShapeDtypeStruct(shape, dtype)


def per_device(slabs, tiles, occupied, virtual, trials, anchor_x, anchor_y, anchor_z):
    occ = occupied.reshape(2, 8, 256, 128)
    vir = virtual.reshape(2, 8, 256, 128)
    tab = tables(slabs, tiles)
    exact = [jnp.asarray(tab[k], BF16) for k in ("r0", "r1", "p1", "p0")]
    wide = [jnp.asarray(tab[k], F32) for k in ("fz", "bz", "fy", "by", "kx", "inv")]
    potential, coupling = pl.pallas_call(
        whole_kernel,
        out_shape=(shaped((4, 8, 128, 128)), shaped((2, 32, 128))),
        in_specs=[SMEM] * 3 + [VMEM] * 13,
        out_specs=(ANY, VMEM),
        scratch_shapes=[
            pltpu.VMEM((2, 48, 2, 8, 128), F32),
            pltpu.VMEM((2, 40, 2, 2, 8, 128), F32),
            pltpu.VMEM((2, 5, 10, 2, 2, 8, 128), F32),
            pltpu.VMEM((5, 8, 128), jnp.int32),
            pltpu.SMEM((5, 8, 128), jnp.int32),
            pltpu.VMEM((2, 160, 320), BF16),
            pltpu.VMEM((320, 160), BF16),
            pltpu.VMEM((2, 10, 2, 2, 8, 128), F32),
            pltpu.VMEM((2, 10, 2, 8, 128), F32),
            pltpu.VMEM((2, 10, 2, 160, 128), F32),
            pltpu.VMEM((2, 10, 2, 32, 128), F32),
            pltpu.VMEM((2, 2, 8, 8, 128), F32),
            pltpu.VMEM((2, 2, 8, 8, 128), F32),
            pltpu.VMEM((10, 4, 144, 128), F32),
            pltpu.VMEM((2, 8, 80, 128), F32),
            pltpu.VMEM((6, 48, 128), F32),
            pltpu.VMEM((10, 2, 144, 128), F32),
            pltpu.VMEM((8, 80, 128), F32),
            pltpu.VMEM((2, 6, 80, 128), F32),
            pltpu.VMEM((6, 48, 128), F32),
            pltpu.VMEM((4, 48, 128), F32),
            pltpu.VMEM((144, 128), F32),
            pltpu.VMEM((tiles, 8, 128), F32),
            pltpu.VMEM((tiles, 8, 128), F32),
            pltpu.VMEM((8, 128), F32),
            pltpu.VMEM((slabs, 8, 128), F32),
            pltpu.VMEM((3, 8, 128), F32),
            pltpu.VMEM((tiles, 3, 8, 128), F32),
            pltpu.VMEM((4, 8, 128, 128), F32),
            pltpu.VMEM((4, 8, 32, 128), F32),
            pltpu.VMEM((2, 4, 8, 2, 2, 8, 128), F32),
            pltpu.VMEM((40, 2, 2, 8, 128), F32),
            pltpu.VMEM((40, 2, 2, 8, 128), F32),
            pltpu.VMEM((2, 8, 2, 2, 8, 128), F32),
            pltpu.VMEM((2, 8, 2, 8, 128), F32),
            pltpu.VMEM((8, 128), jnp.int32),
            pltpu.VMEM((2, 5, 24, 128), F32),
            pltpu.VMEM((320, 96), BF16),
            pltpu.VMEM((10, 256, 128), BF16),
            pltpu.VMEM((10, 320, 256), BF16),
            pltpu.VMEM((4, 4, 2, 24, 128), F32),
            pltpu.VMEM((21, 2, 24, 128), F32),
            pltpu.VMEM((4, 2, 24, 128), F32),
            pltpu.VMEM((4, 24, 128), F32),
            pltpu.VMEM((168, 512), F32),
            pltpu.VMEM((168, 512), F32),
            pltpu.VMEM((2, 512, 512), BF16),
            pltpu.VMEM((2, 512, 512), BF16),
            pltpu.VMEM((2, 21, 8, 512), F32),
            pltpu.VMEM((2, 21, 8, 512), F32),
            pltpu.SemaphoreType.DMA((96,)),
            pltpu.SemaphoreType.DMA((96,)),
            pltpu.SemaphoreType.DMA((slabs,)),
            pltpu.SemaphoreType.DMA((slabs,)),
            pltpu.SemaphoreType.DMA((3,)),
        ],
        compiler_params=params(collective_id=0, has_side_effects=True),
        name="whole",
    )(anchor_x, anchor_y, anchor_z, occ, vir, trials.reshape(2, 32, 8), *exact, *wide)
    return potential, coupling[:, :, :8].reshape(2, 4, 8, 8)


def solution(mesh):
    placed = (
        P(("gx", "gy"), None, None),
        P(("gx", "gy"), None, None),
        P(("gx", "gy"), None, None, None),
        P(("gx", "gy")),
        P(("gx", "gy")),
        P(("gx", "gy")),
    )
    return jax.shard_map(
        functools.partial(per_device, mesh.shape["gx"], mesh.shape["gy"]),
        mesh=mesh,
        in_specs=placed,
        out_specs=(P(None, "gx", "gy", None), P(("gx", "gy"), None, None, None)),
        check_vma=False,
    )
```

```python
import functools

import jax
import jax.numpy as jnp
import numpy as np
from jax import lax
from jax.experimental import pallas as pl
from jax.experimental.pallas import tpu as pltpu
from jax.sharding import PartitionSpec as P

BOX = 32
TRIALS = 4
CX = 8
CY = 128
NZ = 128
SCREEN = 0.05
DAMPING = 2.0 / 3.0
MESH = pl.DeviceIdType.MESH
F32 = jnp.float32
BF16 = jnp.bfloat16
HIGH = lax.Precision.HIGHEST
VMEM = pl.BlockSpec(memory_space=pltpu.VMEM)
SMEM = pl.BlockSpec(memory_space=pltpu.SMEM)
ANY = pl.BlockSpec(memory_space=pl.ANY)


def center_of(level):
    spacing = 2.0**level
    return 6.0 / spacing**2 + SCREEN**2


def split2(x):
    hi = x.astype(BF16)
    lo = (x - hi.astype(F32)).astype(BF16)
    return hi, lo


def dot(a, b):
    return jnp.dot(a, b, preferred_element_type=F32)


def dot_right(x, w):
    hi, lo = split2(x)
    return dot(hi, w) + dot(lo, w)


def dot_left(w, x):
    hi, lo = split2(x)
    return dot(w, hi) + dot(w, lo)


def dot_high(a, b):
    return jnp.dot(a, b, preferred_element_type=F32, precision=HIGH)


def z_beside(x, n):
    if n == 128:
        return pltpu.roll(x, 1, 1) + pltpu.roll(x, 127, 1)
    lane = lax.broadcasted_iota(jnp.int32, x.shape, 1) % n
    below = jnp.where(lane == 0, pltpu.roll(x, 129 - n, 1), pltpu.roll(x, 1, 1))
    above = jnp.where(lane == n - 1, pltpu.roll(x, n - 1, 1), pltpu.roll(x, 127, 1))
    return below + above


def hartley_np(count):
    index = np.arange(count)
    angle = 2.0 * np.pi / count * ((index[:, None] * index[None, :]) % count)
    return (np.cos(angle) + np.sin(angle)) / np.sqrt(count)


def eigen_np(count, spacing):
    return (2.0 - 2.0 * np.cos(2.0 * np.pi / count * np.arange(count))) / (spacing * spacing)


@functools.lru_cache(None)
def tables(slabs, tiles):
    out = {}
    r0 = np.zeros((2, 128, 2, 64))
    r1 = np.zeros((2, 2, 64, 4, 32))
    p1 = np.zeros((2, 4, 32, 2, 64))
    p0 = np.zeros((2, 64, 2, 128))
    for t in range(2):
        for z in range(128):
            r0[t, z, t, z // 2] = 0.125
            p0[t, z // 2, t, z] = 1.0
        for z in range(64):
            for p in range(2):
                r1[p, t, z, 2 * p + t, z // 2] = 0.125
                p1[p, 2 * p + t, z // 2, t, z] = 1.0
    out["r0"] = r0.reshape(256, 128)
    out["r1"] = r1.reshape(2, 128, 128)
    out["p1"] = p1.reshape(2, 128, 128)
    out["p0"] = p0.reshape(128, 256)
    hz = hartley_np(16)
    mean_z = np.zeros((32, 16))
    mean_z[np.arange(32), np.arange(32) // 2] = 1.0
    fz = np.zeros((4, 32, 128))
    bz = np.zeros((128, 4, 32))
    for t in range(4):
        fz[t, :, t * 16 : t * 16 + 16] = 0.125 * mean_z @ hz
        bz[t * 16 : t * 16 + 16, t, :] = hz @ mean_z.T
    out["fz"] = fz.reshape(128, 128)
    out["bz"] = bz.reshape(128, 128)
    size_y = 16 * tiles
    hy = hartley_np(size_y)
    mean_y = np.zeros((16, 32))
    mean_y[np.arange(32) // 2, np.arange(32)] = 1.0
    fy = np.zeros((tiles, size_y, 128))
    by = np.zeros((tiles, 48, 128))
    for q in range(tiles):
        fy[q, :, :32] = hy[:, q * 16 : q * 16 + 16] @ mean_y
        for y in range(-2, 34):
            by[q, 8 + y, :size_y] = hy[(q * 16 + y // 2) % size_y]
    out["fy"] = fy
    out["by"] = by
    out["kx"] = np.kron(hartley_np(slabs), np.eye(8))
    lam_x, lam_y, lam_z = eigen_np(slabs, 8.0), eigen_np(size_y, 8.0), eigen_np(16, 8.0)
    inv = np.zeros((tiles, slabs, 8, 2, 4, 16))
    for q in range(tiles):
        ky = lam_y[q * 16 : q * 16 + 16].reshape(2, 8)
        total = (
            SCREEN * SCREEN
            + lam_x[:, None, None, None, None]
            + ky.T[None, :, :, None, None]
            + lam_z[None, None, None, None, :]
        )
        inv[q] = np.broadcast_to(1.0 / total, (slabs, 8, 2, 4, 16))
    out["inv"] = inv.reshape(tiles, slabs * 8, 128)
    return out


class Shift:
    def __init__(self, sign, pieces, relays, send, recv, slot):
        gx, gy = lax.axis_index("gx"), lax.axis_index("gy")
        n = lax.axis_size("gx")
        place = lax.rem(gx, 4) if sign > 0 else 3 - lax.rem(gx, 4)

        def copy(src, dst, at, k):
            return pltpu.make_async_remote_copy(
                src_ref=src, dst_ref=dst, send_sem=send.at[slot + at], recv_sem=recv.at[slot + at],
                device_id=(lax.rem(gx + sign * k + n, n), gy), device_id_type=MESH,
            )

        held = len(pieces)
        count = held + len(relays)
        self.relays = []
        for r, (k, src, dst, hold, least) in enumerate(relays):
            straight = copy(src, dst, held + r, k)
            first = copy(src, hold, count + r, 4)
            second = copy(hold, dst, held + r, k - 4)
            self.relays.append((straight, first, second, place >= least))
        self.whole = [copy(src, dst, p, k) for p, (k, src, dst) in enumerate(pieces)]

    def start(self):
        for straight, first, second, bent in self.relays:
            pl.when(bent)(first.start)
        for c in self.whole:
            c.start()
        for straight, first, second, bent in self.relays:
            pl.when(jnp.logical_not(bent))(straight.start)

    def pass_on(self):
        for straight, first, second, bent in self.relays:

            def onward(first=first, second=second):
                first.wait_recv()
                second.start()

            pl.when(bent)(onward)

    def arrive(self):
        for straight, first, second, bent in self.relays:
            straight.wait_recv()
        for c in self.whole:
            c.wait_recv()

    def settle(self):
        for straight, first, second, bent in self.relays:

            def sent(first=first, second=second):
                first.wait_send()
                second.wait_send()

            pl.when(bent)(sent)
            pl.when(jnp.logical_not(bent))(straight.wait_send)
        for c in self.whole:
            c.wait_send()


def box_anchors(ay_ref, az_ref, ganc_ref, sources):
    pairs = []
    for s in sources:
        for b in range(2):
            if s < 0:
                pairs.append((ay_ref[b], az_ref[b]))
            else:
                pairs.append((ganc_ref[s, 0, b], ganc_ref[s, 0, 2 + b]))
    return pairs


def select_rows(pairs, axis):
    shape = (160, 320) if axis == 0 else (320, 160)
    row = lax.broadcasted_iota(jnp.int32, shape, axis)
    col = lax.broadcasted_iota(jnp.int32, shape, 1 - axis)
    want = 4 * (col % 8) + (col // 8) % 4
    box = col // 32
    for k, (ay, _) in enumerate(pairs):
        want = want + jnp.where(box == k, ay, 0)
    return jnp.where(row == want, 1.0, 0.0).astype(BF16)


def halve(x):
    return lax.div(x, 2)


def one_hot(hit):
    return jnp.where(hit, 1.0, 0.0)


def select_coarse(pairs):
    row = lax.broadcasted_iota(jnp.int32, (320, 96), 0)
    col = lax.broadcasted_iota(jnp.int32, (320, 96), 1)
    want = row % 32 + 7
    for k, (ay, _) in enumerate(pairs):
        want = want + jnp.where(row // 32 == k, halve(ay + 1), 0)
    return one_hot(col == want).astype(BF16)


def select_coarse_z(az):
    row = lax.broadcasted_iota(jnp.int32, (256, 128), 0)
    col = lax.broadcasted_iota(jnp.int32, (256, 128), 1)
    want = (halve(az + 1) + 63 + col % 32) % 64
    return one_hot((row // 64 == col // 32) & (row % 64 == want)).astype(BF16)


def widen_rows(ay):
    row = lax.broadcasted_iota(jnp.int32, (64, 32), 0)
    col = lax.broadcasted_iota(jnp.int32, (64, 32), 1)
    cell = 4 * (row % 8) + (row // 8) % 4 + ay
    first = halve(ay + 1) - 1
    at = [jnp.right_shift(cell + d, 1) - first for d in (0, -1, 1)]
    beside = one_hot(col == at[1]) + one_hot(col == at[2])
    return jnp.where(row < 32, one_hot(col == at[0]), beside).astype(BF16)


def widen_lanes(az, j):
    row = lax.broadcasted_iota(jnp.int32, (128, 512), 0)
    col = lax.broadcasted_iota(jnp.int32, (128, 512), 1)
    cell = col % 32 + az
    first = halve(az + 1) - 1
    same = (row // 32 == col // 128) & ((col // 32) % 4 == j)
    at = [jnp.right_shift(cell + d, 1) - first for d in (0, -1, 1)]
    hits = [one_hot(same & (row % 32 == a)) for a in at]
    return hits[0].astype(BF16), (hits[1] + hits[2]).astype(BF16)


def mixing(pair_of_trials, p):
    row = lax.broadcasted_iota(jnp.int32, (128, 32), 0)
    col = lax.broadcasted_iota(jnp.int32, (128, 32), 1)
    rows = one_hot(col == (2 * p + (row // 8) % 2) * 8 + row // 16).astype(BF16)
    taken = dot(rows, pair_of_trials).astype(BF16)
    row = lax.broadcasted_iota(jnp.int32, (8, 64), 0)
    col = lax.broadcasted_iota(jnp.int32, (8, 64), 1)
    spread = dot(taken, one_hot(row == col // 8).astype(BF16))
    row = lax.broadcasted_iota(jnp.int32, (128, 64), 0)
    col = lax.broadcasted_iota(jnp.int32, (128, 64), 1)
    return jnp.where(row % 8 == col % 8, spread, 0.0).astype(BF16)


def whole_kernel(
    ax_ref, ay_ref, az_ref, occ_ref, vir_ref, trial_ref,
    r0_ref, r1_ref, p1_ref, p0_ref, fz_ref, bz_ref, fy_ref, by_ref, kx_ref, inv_ref,
    out_ref, coup_ref,
    dens, src, got, ganc, sanc, sel, selt, hold1, hold2, f_ref,
    rim, sides, beyond, fp, f1p, f2p, v0, v1p, w1, v2p, w2, tmp, qs, qr, gs, gall, us, ur,
    pot, margin, cut, win0, win1, hold3, hold4,
    word, mar1, selc, selz, taken, cut1, cwin, hold5, hold6, lc1, lc2, zp, zs, ub, vb,
    send, recv, gsend, grecv, local,
):
    gx, gy = lax.axis_index("gx"), lax.axis_index("gy")
    n, m = lax.axis_size("gx"), lax.axis_size("gy")
    east, west = lax.rem(gx + 1, n), lax.rem(gx + n - 1, n)
    north, south = lax.rem(gy + 1, m), lax.rem(gy + m - 1, m)
    wins = (win0, win1)
    used = [0]

    def slots(count):
        used[0] += count
        return used[0] - count

    barrier = pltpu.get_barrier_semaphore()
    for d in range(1, m):
        pl.semaphore_signal(barrier, inc=1, device_id=(gx, lax.rem(gy + d, m)), device_id_type=MESH)
    for x in (east, west):
        for y in (north, south):
            pl.semaphore_signal(barrier, inc=1, device_id=(x, y), device_id_type=MESH)

    def greet(d, carry):
        pl.semaphore_signal(barrier, inc=1, device_id=(lax.rem(gx + d, n), gy), device_id_type=MESH)
        return carry

    lax.fori_loop(1, n, greet, 0)

    def copy(src_ref, dst_ref, x, y):
        slot = slots(1)
        return pltpu.make_async_remote_copy(
            src_ref=src_ref, dst_ref=dst_ref, send_sem=send.at[slot], recv_sem=recv.at[slot],
            device_id=(x, y), device_id_type=MESH,
        )

    unsent = []

    for b in range(2):
        for x in range(8):
            dens[b, x] = jnp.zeros((2, 8, 128), F32)
            dens[b, 40 + x] = jnp.zeros((2, 8, 128), F32)

    def density(p):
        for b in range(2):
            weights = mixing(trial_ref[b], p)

            def step(s, carry, b=b, weights=weights):
                rows = pl.ds(pl.multiple_of(s * 16, 16), 16)
                vir = vir_ref[b, :, rows, :].astype(F32)
                occ = occ_ref[b, :, rows, :].astype(F32)
                parts = [vir[:, 8 * h : 8 * h + 8].reshape(64, 128) for h in range(2)]
                mixed = dot(weights, jnp.concatenate(parts, axis=1).astype(BF16))
                mixed = mixed.reshape(8, 2, 8, 256)
                for h in range(2):
                    part = mixed[..., 128 * h : 128 * h + 128]
                    dens[b, 8 + 2 * s + h] = jnp.sum(occ[:, None, 8 * h : 8 * h + 8] * part, axis=0)
                return carry

            lax.fori_loop(0, 16, step, 0)

        def place(x, carry):
            for b in range(2):
                src[p, x, b] = dens[b, x + 8 - ax_ref[b]]
            return carry

        lax.fori_loop(0, 40, place, 0)

    def deposit(p):
        s, g = src.at[p], got.at[p]
        pieces = [
            (4, s.at[pl.ds(31, 8)], g.at[3, pl.ds(0, 8)]),
            (3, s.at[pl.ds(23, 10)], g.at[2]),
            (2, s.at[pl.ds(15, 10), 0], g.at[1, :, 0]),
            (-1, s.at[pl.ds(0, 1)], g.at[4, pl.ds(9, 1)]),
        ]
        relays = [
            (1, s.at[pl.ds(7, 10)], g.at[0], hold1.at[p], 3),
            (2, s.at[pl.ds(15, 10), 1], g.at[1, :, 1], hold2.at[p], 2),
        ]
        return Shift(1, pieces, relays, send, recv, slots(8))

    density(0)
    pl.semaphore_wait(barrier, m - 1 + 4 + n - 1)
    lane = lax.broadcasted_iota(jnp.int32, (8, 128), 1)
    value = jnp.zeros((8, 128), jnp.int32)
    for k, anchor in enumerate((ay_ref[0], ay_ref[1], az_ref[0], az_ref[1])):
        value = jnp.where(lane == k, anchor, value)
    word[...] = value
    words = [copy(word, ganc.at[s], lax.rem(gx + k + n, n), gy) for s, k in enumerate((1, 2, 3, 4, -1))]
    moves = [deposit(0), deposit(1)]
    moves[0].start()
    for c in words:
        c.start()
    density(1)
    moves[1].start()
    moves[0].pass_on()
    for c in words:
        c.wait()
    read = pltpu.make_async_copy(ganc, sanc, local.at[0])
    read.start()
    read.wait()
    usual = box_anchors(ay_ref, az_ref, sanc, [-1, 0, 1, 2, 3])
    last = box_anchors(ay_ref, az_ref, sanc, [-1, 0, 1, 2, 4])
    sel[0] = select_rows(usual, 0)
    sel[1] = select_rows(last, 0)
    selt[...] = select_rows(usual, 1)
    blank = jnp.zeros((8, 128), F32)

    def plane(p, e, own, takes, edge):
        pairs = last if edge else usual
        loads = []
        for s in range(5):
            for b in range(2):
                if s == 0:
                    loads.append((lambda t, b=b: src[p, e - 1, b, t]) if own else None)
                elif s == 4 and edge:
                    loads.append(lambda t, b=b: got[p, 4, 9, b, t])
                elif s in takes:
                    loads.append(lambda t, s=s, b=b: got[p, s - 1, e, b, t])
                else:
                    loads.append(None)
        masks = [(lane >= az) & (lane < az + 32) for _, az in pairs]
        columns = []
        for t in range(2):
            rows = []
            for k, load in enumerate(loads):
                if load is None:
                    rows += [blank] * 4
                    continue
                value = load(t)
                for j in range(4):
                    moved = pltpu.roll(value, lax.rem(pairs[k][1] + 128 - 32 * j, 128), 1)
                    rows.append(jnp.where(masks[k], moved, 0.0))
            columns.append(jnp.concatenate(rows, axis=0))
        placed = dot_left(sel[1 if edge else 0], jnp.concatenate(columns, axis=1))
        f_ref[p, e, 0] = placed[:, :128]
        f_ref[p, e, 1] = placed[:, 128:]

    def accumulate(p):
        plane(p, 0, False, (1, 2, 3, 4), False)

        def step(e, carry):
            plane(p, e, True, (1, 2, 3, 4), False)
            return carry

        lax.fori_loop(1, 8, step, 0)
        plane(p, 8, True, (1, 2, 3), False)
        plane(p, 9, True, (1, 2, 3), True)

    def send_rim(p):
        copies = [copy(f_ref.at[p, :, :, pl.ds(128, 32), :], rim.at[p], gx, north)]
        copies[0].start()

        def edge(e, carry):
            for t in range(2):
                sides[p, 0, e, t : t + 1] = f_ref[p, e + 1, t, 127:128]
                sides[p, 1, e, t : t + 1] = f_ref[p, e + 1, t, 0:1]
            return carry

        lax.fori_loop(0, 8, edge, 0)
        copies += [
            copy(sides.at[p, 0], beyond.at[p, 0], gx, north),
            copy(sides.at[p, 1], beyond.at[p, 1], gx, south),
        ]
        for c in copies[1:]:
            c.start()

        def early(e, carry):
            for t in range(2):
                fp[e, 2 * p + t, 40:136] = f_ref[p, e, t, 32:128]
            return carry

        lax.fori_loop(0, 10, early, 0)
        return copies

    def join_rim(p, copies):
        for c in copies:
            c.wait_recv()
        unsent.extend(copies)

        def join(e, carry):
            for t in range(2):
                fp[e, 2 * p + t, 8:40] = f_ref[p, e, t, 0:32] + rim[p, e, t]
            return carry

        def rims(e, carry):
            for t in range(2):
                fp[e, 2 * p + t, 7:8] = beyond[p, 0, e - 1, t : t + 1]
                fp[e, 2 * p + t, 136:137] = f_ref[p, e, t, 128:129] + beyond[p, 1, e - 1, t : t + 1]
            return carry

        lax.fori_loop(1, 9, rims, 0)
        lax.fori_loop(0, 10, join, 0)

    def down0(p):
        scale = DAMPING / center_of(0)

        def step(xc, carry):
            halves = []
            for t in (2 * p, 2 * p + 1):
                total = None
                for x in range(2):
                    e = 2 * xc + 1 + x
                    mid = fp[e, t, 8:136]
                    beside = fp[e, t, 7:135] + fp[e, t, 9:137] + fp[e - 1, t, 8:136] + fp[e + 1, t, 8:136]
                    beside = beside + z_beside(mid, 128)
                    res = (1.0 - DAMPING) * mid + scale * beside
                    pot[t, e - 1] = scale * (mid + res)
                    total = res if total is None else total + res
                tmp[0:128, :] = total
                halves.append(tmp[pl.ds(0, 64, stride=2), :] + tmp[pl.ds(1, 64, stride=2), :])
            f1p[p, 2 + xc, 8:72] = dot_right(jnp.concatenate(halves, axis=1), r0_ref[...])
            return carry

        lax.fori_loop(0, 4, step, 0)

    def swap(buf, a, c):
        def part(x0, nx, y0, ny):
            return buf.at[pl.ds(x0, nx), pl.ds(y0, ny)]

        near = [
            copy(part(a + 1, 1, 8, c), part(1, 1, 8, c), east, gy),
            copy(part(2, 1, 8, c), part(a + 2, 1, 8, c), west, gy),
            copy(part(2, a, c, 8), part(2, a, 0, 8), gx, north),
            copy(part(2, a, 8, 8), part(2, a, c + 8, 8), gx, south),
        ]
        far = [
            copy(part(a, 1, 8, c), part(0, 1, 8, c), east, gy),
            copy(part(3, 1, 8, c), part(a + 3, 1, 8, c), west, gy),
            copy(part(a, 2, c, 8), part(0, 2, 0, 8), east, north),
            copy(part(a, 2, 8, 8), part(0, 2, c + 8, 8), east, south),
            copy(part(2, 2, c, 8), part(a + 2, 2, 0, 8), west, north),
            copy(part(2, 2, 8, 8), part(a + 2, 2, c + 8, 8), west, south),
        ]
        for one in near + far:
            one.start()
        unsent.extend(near + far)
        return near, far

    def send_margin(p):
        pair = pl.ds(2 * p, 2)
        c = copy(pot.at[pair, :, pl.ds(0, 32), :], margin.at[pair], gx, south)
        c.start()
        return c

    group = lax.broadcasted_iota(jnp.int32, (8, 128), 1) // 32

    def windows(p):
        def step(x, carry):
            columns = [
                jnp.concatenate([pot[2 * p + t, x], margin[2 * p + t, x]], axis=0) for t in range(2)
            ]
            taken = dot_left(selt[...], jnp.concatenate(columns, axis=1))
            for t in range(2):
                for k in range(10):
                    total = None
                    for j in range(4):
                        piece = taken[32 * k + 8 * j : 32 * k + 8 * j + 8, 128 * t : 128 * t + 128]
                        piece = pltpu.roll(piece, lax.rem(128 + 32 * j - usual[k][1], 128), 1)
                        total = piece if total is None else jnp.where(group == j, piece, total)
                    if k < 2:
                        wins[p][x, k, t] = total
                    else:
                        cut[p, k // 2 - 1, x, k % 2, t] = total
            return carry

        lax.fori_loop(0, 8, step, 0)

    def give_back(p):
        c, w = cut.at[p], wins[p]
        pieces = [
            (4, c.at[3], w.at[pl.ds(32, 8)]),
            (3, c.at[2], w.at[pl.ds(24, 8)]),
            (2, c.at[1, :, 0], w.at[pl.ds(16, 8), 0]),
        ]
        relays = [
            (1, c.at[0], w.at[pl.ds(8, 8)], hold3.at[p], 3),
            (2, c.at[1, :, 1], w.at[pl.ds(16, 8), 1], hold4.at[p], 2),
        ]
        return Shift(-1, pieces, relays, send, recv, slots(7))

    moves[0].arrive()
    accumulate(0)
    rims0 = send_rim(0)
    moves[1].pass_on()
    join_rim(0, rims0)
    down0(0)
    near0, far0 = swap(f1p.at[0], 4, 64)
    edge0 = send_margin(0)
    moves[1].arrive()
    accumulate(1)
    rims1 = send_rim(1)
    backs = [give_back(0), give_back(1)]
    edge0.wait_recv()
    windows(0)
    join_rim(1, rims1)
    down0(1)
    near1, far1 = swap(f1p.at[1], 4, 64)
    edge1 = send_margin(1)
    selc[...] = select_coarse(usual)

    def down1(p, xc):
        scale = DAMPING / center_of(1) / 4.0
        both = None
        for x in range(2):
            e = 2 + 2 * xc + x
            mid = f1p[p, e, 8:72]
            beside = f1p[p, e, 7:71] + f1p[p, e, 9:73] + f1p[p, e - 1, 8:72] + f1p[p, e + 1, 8:72]
            beside = beside + z_beside(mid, 64)
            res = (1.0 - DAMPING) * mid + scale * beside
            both = res if both is None else both + res
        tmp[0:64, :] = both
        pair = tmp[pl.ds(0, 32, stride=2), :] + tmp[pl.ds(1, 32, stride=2), :]
        return dot_right(pair, r1_ref[p])

    for c in near0:
        c.wait_recv()
    held = [down1(0, xc) for xc in range(2)]
    for c in near1:
        c.wait_recv()
    for xc in range(2):
        f2p[2 + xc, 8:40] = held[xc] + down1(1, xc)
    near2, far2 = swap(f2p, 2, 32)
    backs[0].start()
    for c in near2:
        c.wait_recv()

    scale = DAMPING / center_of(2) / 16.0
    total = None
    for x in range(2):
        e = 2 + x
        mid = f2p[e, 8:40]
        beside = f2p[e, 7:39] + f2p[e, 9:41] + f2p[e - 1, 8:40] + f2p[e + 1, 8:40]
        beside = beside + z_beside(mid, 32)
        res = (1.0 - DAMPING) * mid + scale * beside
        total = res if total is None else total + res
    modes = dot_high(total, fz_ref[...])
    modes = jnp.concatenate([modes, jnp.zeros((96, 128), F32)], axis=0)
    modes = dot_high(fy_ref[gy], modes)
    for q in range(m):
        qs[q] = modes[16 * q : 16 * q + 8] + pltpu.roll(modes[16 * q + 8 : 16 * q + 16], 64, 1)
    copies = []
    for d in range(1, m):
        to = lax.rem(gy + d, m)
        copies.append(copy(qs.at[to], qr.at[d - 1], gx, to))
    for c in copies:
        c.start()
    unsent.extend(copies)
    edge1.wait_recv()
    windows(1)
    backs[1].start()
    for k in range(10):
        selz[k] = select_coarse_z(usual[k][1])
    mine = qs[gy]
    for d, c in enumerate(copies):
        c.wait_recv()
        mine = mine + qr[d]
    gs[...] = mine

    def shout(d):
        return pltpu.make_async_remote_copy(
            src_ref=gs, dst_ref=gall.at[gx], send_sem=gsend.at[d], recv_sem=grecv.at[d],
            device_id=(lax.rem(gx + d, n), gy), device_id_type=MESH,
        )

    def begin(d, carry):
        shout(d).start()
        return carry

    def end(d, carry):
        shout(d).wait()
        return carry

    lax.fori_loop(1, n, begin, 0)
    gall[gx] = mine
    for b in range(2):
        for j in range(4):
            zp[b, 128 * j : 128 * j + 128], zs[b, 128 * j : 128 * j + 128] = widen_lanes(az_ref[b], j)
    lax.fori_loop(1, n, end, 0)
    spectrum = dot_high(kx_ref[...], gall[...].reshape(8 * n, 128)) * inv_ref[gy]
    for s, x in enumerate((west, gx, east)):
        us[s] = dot_high(kx_ref[pl.ds(pl.multiple_of(8 * x, 8), 8), :], spectrum)

    copies = []
    for d in range(1, m):
        to = lax.rem(gy + d, m)
        copies.append(copy(us, ur.at[gy], gx, to))
    for c in copies:
        c.start()
    unsent.extend(copies)
    ur[gy] = us[...]
    backs[0].pass_on()
    for c in copies:
        c.wait_recv()

    for c in far2:
        c.wait_recv()
    scale = DAMPING / center_of(2)
    for s in range(3):
        rows = []
        for q in range(m):
            half = ur[q, s]
            rows += [half, pltpu.roll(half, 64, 1)]
        if m < 8:
            rows.append(jnp.zeros((128 - 16 * m, 128), F32))
        ahead = dot_high(by_ref[gy], jnp.concatenate(rows, axis=0))
        ahead = dot_high(ahead, bz_ref[...])
        for x in range(2):
            v2p[2 * s + x] = scale * f2p[2 * s + x] + ahead
    for e in range(1, 5):
        mid = v2p[e]
        beside = v2p[e - 1] + v2p[e + 1] + pltpu.roll(mid, 1, 0) + pltpu.roll(mid, 47, 0)
        beside = beside + z_beside(mid, 32)
        w2[e - 1] = (1.0 - DAMPING) * mid + scale * f2p[e] + (scale / 16.0) * beside

    def rise1(p):
        scale = DAMPING / center_of(1)
        for e in range(4):
            wide = dot_right(w2[e, 4:44], p1_ref[p])
            tmp[pl.ds(0, 40, stride=2), :] = wide
            tmp[pl.ds(1, 40, stride=2), :] = wide
            for x in range(2):
                v1p[2 * e + x] = scale * f1p[p, 2 * e + x] + tmp[0:80, :]

        def step(e, carry):
            mid = v1p[e]
            beside = v1p[e - 1] + v1p[e + 1] + pltpu.roll(mid, 1, 0) + pltpu.roll(mid, 79, 0)
            beside = beside + z_beside(mid, 64)
            w1[p, e - 1] = (1.0 - DAMPING) * mid + scale * f1p[p, e] + (scale / 4.0) * beside
            return carry

        lax.fori_loop(1, 7, step, 0)

    def rise0(p):
        scale = DAMPING / center_of(0)

        def widen(i, planes):
            wide = dot_right(w1[p, i, 4:76], p0_ref[...])
            for t in range(2):
                value = wide[:, 128 * t : 128 * t + 128]
                for e in planes:
                    v0[e, t, pl.ds(0, 72, stride=2), :] = value
                    v0[e, t, pl.ds(1, 72, stride=2), :] = value

        widen(0, (0,))

        def lift(i, carry):
            widen(i, (2 * i - 1, 2 * i))
            return carry

        lax.fori_loop(1, 5, lift, 0)
        widen(5, (9,))

        def step(e, carry):
            for t in range(2):
                mid = v0[e, t, 8:136]
                beside = v0[e, t, 7:135] + v0[e, t, 9:137] + v0[e - 1, t, 8:136] + v0[e + 1, t, 8:136]
                beside = beside + z_beside(mid, 128)
                pot[2 * p + t, e - 1] = pot[2 * p + t, e - 1] + (1.0 - DAMPING) * mid + scale * beside
            return carry

        lax.fori_loop(1, 9, step, 0)
        pair = pl.ds(2 * p, 2)
        keep = pltpu.make_async_copy(pot.at[pair], out_ref.at[pair], local.at[1 + p])
        keep.start()
        return keep

    def windows1():
        for i in range(5):
            columns = [jnp.concatenate([w1[p, i, 0:72], mar1[p, i]], axis=0) for p in range(2)]
            hi, lo = split2(jnp.concatenate(columns, axis=1))
            taken[2 * i] = dot(selc[...], hi).astype(BF16)
            taken[2 * i + 1] = dot(selc[...], lo).astype(BF16)
        for k in range(10):
            rows = jnp.concatenate([taken[i, 32 * k : 32 * k + 32] for i in range(10)], axis=0)
            rows = dot(rows, selz[k])
            for i in range(5):
                part = rows[64 * i : 64 * i + 24] + rows[64 * i + 32 : 64 * i + 56]
                if k < 2:
                    cwin[i, k] = part
                elif i > 0:
                    cut1[k // 2 - 1, i - 1, k % 2] = part

    def give_back1():
        pieces = [
            (4, cut1.at[3], cwin.at[pl.ds(17, 4)]),
            (3, cut1.at[2], cwin.at[pl.ds(13, 4)]),
            (2, cut1.at[1, :, 0], cwin.at[pl.ds(9, 4), 0]),
        ]
        relays = [
            (1, cut1.at[0], cwin.at[pl.ds(5, 4)], hold5, 3),
            (2, cut1.at[1, :, 1], cwin.at[pl.ds(9, 4), 1], hold6, 2),
        ]
        return Shift(-1, pieces, relays, send, recv, slots(7))

    def expand(b):
        rows = widen_rows(ay_ref[b])
        blank = jnp.zeros((8, 128), F32)
        for g in range(11):
            planes = [x for x in (2 * g, 2 * g + 1) if x < 21]
            columns = [jnp.concatenate([cwin[x, b], blank], axis=0) for x in planes]
            wide = dot_left(rows, jnp.concatenate(columns, axis=1))
            for i, x in enumerate(planes):
                for j in range(4):
                    here = wide[:, 128 * i : 128 * i + 128]
                    lc1[8 * x : 8 * x + 8, 128 * j : 128 * j + 128] = here[8 * j : 8 * j + 8]
                    lc2[8 * x : 8 * x + 8, 128 * j : 128 * j + 128] = here[32 + 8 * j : 40 + 8 * j]
        ub[b] = dot_right(lc1[...], zp[b]).reshape(21, 8, 512)
        vb[b] = (dot_right(lc2[...], zp[b]) + dot_right(lc1[...], zs[b])).reshape(21, 8, 512)

    def project():
        scale = DAMPING / center_of(0)
        for b in range(2):

            def step(s, total, b=b):
                left, right = [], []
                for h in range(4):
                    rows = pl.ds(pl.multiple_of(s * 64 + 16 * h, 16), 16)
                    occ = occ_ref[b, :, rows, :].astype(F32)
                    vir = vir_ref[b, :, rows, :].astype(F32)
                    for g in range(2):
                        x = ax_ref[b] + s * 8 + 2 * h + g
                        mid = ub[b, halve(x + 2)]
                        late = (1.0 - DAMPING) * mid
                        late = late + scale * (ub[b, halve(x + 1)] + ub[b, halve(x + 3)] + vb[b, halve(x + 2)])
                        parts = []
                        for t in range(4):
                            cells = wins[t // 2][x, b, t % 2] + late[:, 128 * t : 128 * t + 128]
                            weighted = occ[:, 8 * g : 8 * g + 8] * cells[None]
                            parts.append(weighted.reshape(64, 128).astype(BF16))
                        left.append(jnp.concatenate(parts, axis=0))
                        right.append(vir[:, 8 * g : 8 * g + 8].reshape(64, 128).astype(BF16))
                left, right = jnp.concatenate(left, axis=1), jnp.concatenate(right, axis=1)
                return total + lax.dot_general(
                    left, right, (((1,), (1,)), ((), ())), preferred_element_type=F32
                )

            total = lax.fori_loop(0, 4, step, jnp.zeros((256, 64), F32))
            row = lax.broadcasted_iota(jnp.int32, (256, 64), 0) % 8
            col = lax.broadcasted_iota(jnp.int32, (256, 64), 1) % 8
            total = jnp.where(row == col, total, 0.0)
            total = jnp.sum(total.reshape(32, 8, 64), axis=1)
            col = lax.broadcasted_iota(jnp.int32, (64, 128), 1)
            row = lax.broadcasted_iota(jnp.int32, (64, 128), 0) // 8
            pick = jnp.where(row == col, float(BOX) ** (-1.5), 0.0)
            coup_ref[b] = dot_high(total, pick)

    for c in far0:
        c.wait_recv()
    rise1(0)
    for c in far1:
        c.wait_recv()
    rise1(1)
    margins = [copy(w1.at[p, pl.ds(0, 5), pl.ds(8, 24)], mar1.at[p], gx, south) for p in range(2)]
    for c in margins:
        c.start()
    edge0.wait_send()
    edge1.wait_send()
    backs[1].pass_on()
    for c in margins:
        c.wait_recv()
    windows1()
    late = give_back1()
    late.start()
    keeps = [rise0(0)]
    late.pass_on()
    keeps.append(rise0(1))
    backs[0].arrive()
    backs[1].arrive()
    late.arrive()
    expand(0)
    expand(1)
    project()
    for c in keeps:
        c.wait()
    for c in unsent + margins:
        c.wait_send()
    for c in moves + backs + [late]:
        c.settle()


def params(**more):
    return pltpu.CompilerParams(vmem_limit_bytes=40 * 1024 * 1024, **more)


def shaped(shape, dtype=F32):
    return jax.ShapeDtypeStruct(shape, dtype)


def per_device(slabs, tiles, occupied, virtual, trials, anchor_x, anchor_y, anchor_z):
    occ = occupied.reshape(2, 8, 256, 128)
    vir = virtual.reshape(2, 8, 256, 128)
    tab = tables(slabs, tiles)
    exact = [jnp.asarray(tab[k], BF16) for k in ("r0", "r1", "p1", "p0")]
    wide = [jnp.asarray(tab[k], F32) for k in ("fz", "bz", "fy", "by", "kx", "inv")]
    potential, coupling = pl.pallas_call(
        whole_kernel,
        out_shape=(shaped((4, 8, 128, 128)), shaped((2, 32, 128))),
        in_specs=[SMEM] * 3 + [VMEM] * 13,
        out_specs=(ANY, VMEM),
        scratch_shapes=[
            pltpu.VMEM((2, 48, 2, 8, 128), F32),
            pltpu.VMEM((2, 40, 2, 2, 8, 128), F32),
            pltpu.VMEM((2, 5, 10, 2, 2, 8, 128), F32),
            pltpu.VMEM((5, 8, 128), jnp.int32),
            pltpu.SMEM((5, 8, 128), jnp.int32),
            pltpu.VMEM((2, 160, 320), BF16),
            pltpu.VMEM((320, 160), BF16),
            pltpu.VMEM((2, 10, 2, 2, 8, 128), F32),
            pltpu.VMEM((2, 10, 2, 8, 128), F32),
            pltpu.VMEM((2, 10, 2, 160, 128), F32),
            pltpu.VMEM((2, 10, 2, 32, 128), F32),
            pltpu.VMEM((2, 2, 8, 8, 128), F32),
            pltpu.VMEM((2, 2, 8, 8, 128), F32),
            pltpu.VMEM((10, 4, 144, 128), F32),
            pltpu.VMEM((2, 8, 80, 128), F32),
            pltpu.VMEM((6, 48, 128), F32),
            pltpu.VMEM((10, 2, 144, 128), F32),
            pltpu.VMEM((8, 80, 128), F32),
            pltpu.VMEM((2, 6, 80, 128), F32),
            pltpu.VMEM((6, 48, 128), F32),
            pltpu.VMEM((4, 48, 128), F32),
            pltpu.VMEM((144, 128), F32),
            pltpu.VMEM((tiles, 8, 128), F32),
            pltpu.VMEM((tiles, 8, 128), F32),
            pltpu.VMEM((8, 128), F32),
            pltpu.VMEM((slabs, 8, 128), F32),
            pltpu.VMEM((3, 8, 128), F32),
            pltpu.VMEM((tiles, 3, 8, 128), F32),
            pltpu.VMEM((4, 8, 128, 128), F32),
            pltpu.VMEM((4, 8, 32, 128), F32),
            pltpu.VMEM((2, 4, 8, 2, 2, 8, 128), F32),
            pltpu.VMEM((40, 2, 2, 8, 128), F32),
            pltpu.VMEM((40, 2, 2, 8, 128), F32),
            pltpu.VMEM((2, 8, 2, 2, 8, 128), F32),
            pltpu.VMEM((2, 8, 2, 8, 128), F32),
            pltpu.VMEM((8, 128), jnp.int32),
            pltpu.VMEM((2, 5, 24, 128), F32),
            pltpu.VMEM((320, 96), BF16),
            pltpu.VMEM((10, 256, 128), BF16),
            pltpu.VMEM((10, 320, 256), BF16),
            pltpu.VMEM((4, 4, 2, 24, 128), F32),
            pltpu.VMEM((21, 2, 24, 128), F32),
            pltpu.VMEM((4, 2, 24, 128), F32),
            pltpu.VMEM((4, 24, 128), F32),
            pltpu.VMEM((168, 512), F32),
            pltpu.VMEM((168, 512), F32),
            pltpu.VMEM((2, 512, 512), BF16),
            pltpu.VMEM((2, 512, 512), BF16),
            pltpu.VMEM((2, 21, 8, 512), F32),
            pltpu.VMEM((2, 21, 8, 512), F32),
            pltpu.SemaphoreType.DMA((96,)),
            pltpu.SemaphoreType.DMA((96,)),
            pltpu.SemaphoreType.DMA((slabs,)),
            pltpu.SemaphoreType.DMA((slabs,)),
            pltpu.SemaphoreType.DMA((3,)),
        ],
        compiler_params=params(collective_id=0, has_side_effects=True),
        name="whole",
    )(anchor_x, anchor_y, anchor_z, occ, vir, trials.reshape(2, 32, 8), *exact, *wide)
    return potential, coupling[:, :, :8].reshape(2, 4, 8, 8)


def solution(mesh):
    placed = (
        P(("gx", "gy"), None, None),
        P(("gx", "gy"), None, None),
        P(("gx", "gy"), None, None, None),
        P(("gx", "gy")),
        P(("gx", "gy")),
        P(("gx", "gy")),
    )
    return jax.shard_map(
        functools.partial(per_device, mesh.shape["gx"], mesh.shape["gy"]),
        mesh=mesh,
        in_specs=placed,
        out_specs=(P(None, "gx", "gy", None), P(("gx", "gy"), None, None, None)),
        check_vma=False,
    )
```
